256 devices in a mesh: gx: 16 (over z_hi, y), gy: 16 (over x, z_lo, core).
Axes of the slice: x: 4, y: 4, z: 8 (z_hi: 4, z_lo: 2; z = z_hi * 2 + z_lo), core: 2. Of those that a mesh axis runs over, the one named last changes fastest.
Arguments:
- flow_state: float32 [4, 48, 256, 2048], P(None, None, 'gx', 'gy'), may hold values from -4 to 4
- inflow: float32 [4, 48, 2048], P(None, None, 'gx'), may hold values from -4 to 4
- footprint: int32 [100, 3], replicated, may hold values from 0 to 2024, as said below
- block_map: int32 [16], replicated, may hold values from 0 to 15, each once
Outputs:
- new_state: float32 [4, 48, 256, 2048], P(None, None, 'gx', 'gy')
The draws below stay inside these ranges and needn't reach their ends.
Inputs may be any that keep to these rules, and one draw needn't show every extreme that they name: `footprint`: each disk box lies inside the grid and starts at streamwise cell 1 or later. `block_map`: a permutation of the spanwise blocks.
All inputs are finite; a program needn't handle non-finite values.
Results may differ from the reference program's by a relative error of at most 0.00011.
Values sent between devices are 32-bit elements; how exact they have to be, the bound alone decides.
No kernel may reach another device: no remote copies, remote signals or barrier semaphores. Data moves between devices by JAX's collectives and lax.ppermute only.
A program may use at most 64 MiB of HBM per device.

```python
import math
import jax
import jax.numpy as jnp
from jax import lax

CY = 128
NZ = 48
NTURB = 100
DISK_X = 2
DISK_Y = 24
DISK_Z = 24
STEPS = 2
NX = 256
NY = 2048
N_GY = 16


def draw_flow_state(key, part):
    key = jax.random.fold_in(key, 1)
    first, second = jax.random.split(key, 2)
    shape_all = (4, NZ, NX, NY)
    noise = jax.random.truncated_normal(first, -4.0, 4.0, shape_all, jnp.float32)
    amplitude = 0.35
    phases = jax.random.uniform(second, (2,), jnp.float32, 0.0, 2.0 * math.pi)
    x_cells = jnp.arange(NX, dtype=jnp.float32)[:, None]
    y_cells = jnp.arange(NY, dtype=jnp.float32)[None, :]
    wave = jnp.sin(2.0 * math.pi * x_cells / 97.0 + phases[0]) * jnp.cos(2.0 * math.pi * y_cells / 211.0 + phases[1])
    scales = jnp.array([0.3, 0.3, 0.2, 1.0], jnp.float32)[:, None, None, None]
    result = noise * scales
    return result.at[0].add(1.0 + amplitude * wave[None, :, :])


def draw_inflow(key, part):
    key = jax.random.fold_in(key, 2)
    first, second = jax.random.split(key, 2)
    shape_all = (4, NZ, NY)
    noise = jax.random.truncated_normal(first, -4.0, 4.0, shape_all, jnp.float32)
    amplitude = 0.35
    phase = jax.random.uniform(second, (), jnp.float32, 0.0, 2.0 * math.pi)
    y_cells = jnp.arange(NY, dtype=jnp.float32)[None, :]
    wave = jnp.sin(2.0 * math.pi * y_cells / 173.0 + phase)
    scales = jnp.array([0.3, 0.3, 0.2, 1.0], jnp.float32)[:, None, None]
    result = noise * scales
    return result.at[0].add(1.0 + amplitude * wave)


def draw_footprint(key, part):
    key = jax.random.fold_in(key, 3)
    first, second, third = jax.random.split(key, 3)
    start_x = jax.random.randint(first, (NTURB,), 1, NX - DISK_X)
    start_y = jax.random.randint(second, (NTURB,), 0, NY - DISK_Y + 1)
    start_z = jax.random.randint(third, (NTURB,), 0, NZ - DISK_Z + 1)
    start_x = start_x.at[0].set(NX - DISK_X - 1)
    start_y = start_y.at[0].set(NY - DISK_Y)
    start_z = start_z.at[0].set(0)
    return jnp.stack([start_x, start_y, start_z], axis=1).astype(jnp.int32)


def setup_inputs(seed: int = 0) -> dict:
    seeds = jax.random.split(jax.random.key(seed), 5)
    return {
        "flow_state": draw_flow_state(jax.random.fold_in(seeds[4], 71), 0),
        "inflow": draw_inflow(jax.random.fold_in(seeds[4], 71), 0),
        "footprint": draw_footprint(jax.random.fold_in(seeds[4], 71), 0),
        "block_map": jax.random.permutation(seeds[3], N_GY).astype(jnp.int32),
    }


time_step = 0.15
viscosity = 0.3
buoyancy = 0.3
thrust_gain = 2.0


def advance(fields, west_side, east_side, south_side, north_side, below_cell, above_cell, force_field):
    up_x = jnp.maximum(fields[0], 0.0)[None]
    down_x = jnp.minimum(fields[0], 0.0)[None]
    up_y = jnp.maximum(fields[1], 0.0)[None]
    down_y = jnp.minimum(fields[1], 0.0)[None]
    up_z = jnp.maximum(fields[2], 0.0)[None]
    down_z = jnp.minimum(fields[2], 0.0)[None]
    advect = up_x * (fields - west_side) + down_x * (east_side - fields)
    advect = advect + up_y * (fields - south_side) + down_y * (north_side - fields)
    advect = advect + up_z * (fields - below_cell) + down_z * (above_cell - fields)
    spread = west_side + east_side + south_side + north_side + below_cell + above_cell - 6.0 * fields
    zeros_field = jnp.zeros_like(force_field)
    extra = jnp.stack([force_field, zeros_field, buoyancy * fields[3], zeros_field])
    return fields + time_step * (-advect + viscosity * spread + extra)


def reference(flow_state, inflow, footprint, block_map):
    inlet_plane = inflow.reshape(4, NZ, N_GY, CY)[:, :, block_map, :].reshape(4, NZ, NY)
    fields = flow_state
    disk_cells = float(DISK_X * DISK_Y * DISK_Z)
    for step_index in range(STEPS):
        velocity_u = fields[0]

        def box_sum(corner):
            return jnp.sum(lax.dynamic_slice(velocity_u, (corner[2], corner[0], corner[1]), (DISK_Z, DISK_X, DISK_Y)))

        disk_speed = jax.vmap(box_sum)(footprint) / disk_cells
        thrust = -thrust_gain * disk_speed * jnp.abs(disk_speed)

        def add_disk(turbine, field_now):
            corner = footprint[turbine]
            start = (corner[2], corner[0], corner[1])
            block = lax.dynamic_slice(field_now, start, (DISK_Z, DISK_X, DISK_Y)) + thrust[turbine]
            return lax.dynamic_update_slice(field_now, block, start)

        force_field = lax.fori_loop(0, NTURB, add_disk, jnp.zeros((NZ, NX, NY), jnp.float32))
        west_side = jnp.concatenate([inlet_plane[:, :, None, :], fields[:, :, :-1, :]], axis=2)
        east_side = jnp.concatenate([fields[:, :, 1:, :], fields[:, :, -1:, :]], axis=2)
        south_side = jnp.roll(fields, 1, axis=3)
        north_side = jnp.roll(fields, -1, axis=3)
        below_cell = jnp.concatenate([fields[:, :1], fields[:, :-1]], axis=1)
        above_cell = jnp.concatenate([fields[:, 1:], fields[:, -1:]], axis=1)
        fields = advance(fields, west_side, east_side, south_side, north_side, below_cell, above_cell, force_field)
    return fields
```

```python
import jax
import jax.numpy as jnp
from jax import lax
from jax.experimental import pallas as pl
from jax.experimental.pallas import tpu as pltpu
from jax.sharding import PartitionSpec as P

DISK_X = 2
DISK_Y = 24
DISK_Z = 24
CELLS = float(DISK_X * DISK_Y * DISK_Z)

DT = 0.15
VISC = 0.3
BUOY = 0.3
GAIN = 2.0
BASE = DT * VISC
FAR = -100000
F32 = jnp.float32


def pairs(n, odd):
    if not odd:
        return [(i, i ^ 1) for i in range(n)]
    return [(i, (i + 1) % n if i % 2 else (i - 1) % n) for i in range(n)]


def pairs_inside(nx, ny):
    out = []
    for i in range(nx):
        for j in range(ny):
            if i in (0, nx - 1):
                to = (i, j ^ 1)
            else:
                to = (i + 1 if i % 2 else i - 1, j)
            out.append((i * ny + j, to[0] * ny + to[1]))
    return out


def upwind(vel):
    scaled = DT * vel
    return jnp.maximum(scaled, 0.0) + BASE, BASE - jnp.minimum(scaled, 0.0)


def coefs(u, v, w):
    cw, ce = upwind(u)
    cs, cn = upwind(v)
    cb, ca = upwind(w)
    c0 = 1.0 - ((cw + ce) + (cs + cn) + (cb + ca))
    return c0, cw, ce, cs, cn, cb, ca


def mix(c, f, w, e, s, n, b, a):
    return c[0] * f + c[1] * w + c[2] * e + c[3] * s + c[4] * n + c[5] * b + c[6] * a


def dot_nt(a, m):
    high = a.astype(jnp.bfloat16)
    low = (a - high.astype(F32)).astype(jnp.bfloat16)
    dims = (((1,), (1,)), ((), ()))
    return lax.dot_general(high, m, dims, preferred_element_type=F32) + lax.dot_general(
        low, m, dims, preferred_element_type=F32
    )


def dot_nn(a, m):
    high = a.astype(jnp.bfloat16)
    low = (a - high.astype(F32)).astype(jnp.bfloat16)
    return jnp.dot(high, m, preferred_element_type=F32) + jnp.dot(
        low, m, preferred_element_type=F32
    )


def iota(shape, dim):
    return lax.broadcasted_iota(jnp.int32, shape, dim)


def within(cells, start, extent):
    return ((cells >= start) & (cells < start + extent)).astype(F32)


def span_mask(fp, first, count):
    return within(first + iota((count, 128), 0), fp[1:2], DISK_Y).astype(jnp.bfloat16)


def pack_x_kernel(f_ref, a_ref, b_ref):
    even = lax.axis_index("gx") % 2 == 0

    def fill(low_ref, high_ref):
        for c in range(4):
            low_ref[:, 2 * c : 2 * c + 2, :] = f_ref[c, :, 0:2, :]
            high_ref[:, 2 * c : 2 * c + 2, :] = f_ref[c, :, 14:16, :]

    @pl.when(even)
    def _():
        fill(b_ref, a_ref)

    @pl.when(jnp.logical_not(even))
    def _():
        fill(a_ref, b_ref)


def tile_kernel(f_ref, fp_ref, p_ref, sums_ref, rows_ref):
    nz = f_ref.shape[1]
    first_x = lax.axis_index("gx") * 16
    first_y = lax.axis_index("gy") * 128
    fp = fp_ref[...]
    lane = iota((16, 128), 1)
    sub = iota((16, 128), 0)
    p_ref[...] = jnp.zeros_like(p_ref)

    for half in range(2):
        lo, hi = half * 32, min(nz, half * 32 + 32)

        def one(z, packed):
            below = jnp.maximum(z - 1, 0)
            above = jnp.minimum(z + 1, nz - 1)
            cur = [f_ref[c, z] for c in range(4)]
            u = cur[0]
            c = coefs(u, cur[1], cur[2])
            west = jnp.where(sub == 0, 0.0, pltpu.roll(u, 1, 0))
            east = jnp.where(sub == 15, 0.0, pltpu.roll(u, 15, 0))
            south = jnp.where(lane == 0, 0.0, pltpu.roll(u, 1, 1))
            north = jnp.where(lane == 127, 0.0, pltpu.roll(u, 127, 1))
            rows_ref[1, z] = mix(c, u, west, east, south, north, f_ref[0, below], f_ref[0, above])
            rows_ref[0, z] = u
            here = lane // 4 == z - lo
            shift = (2 + 4 * (z - lo)) % 128
            return tuple(
                jnp.where(here, pltpu.roll(cur[i], shift, 1), packed[i]) for i in range(4)
            )

        packed = lax.fori_loop(lo, hi, one, tuple(jnp.zeros((16, 128), F32) for _ in range(4)))
        for i in range(4):
            p_ref[half, i, 0:16, :] = packed[i]

    span = span_mask(fp, first_y, 128)
    rows = rows_ref[...].reshape(2 * nz * 16, 128)
    rows_ref[...] = dot_nn(rows, span).reshape(2, nz, 16, 128)

    def add(z, acc):
        mask = within(z, fp[2:3], DISK_Z)
        return acc[0] + rows_ref[0, z] * mask, acc[1] + rows_ref[1, z] * mask

    zero = jnp.zeros((16, 128), F32)
    acc = lax.fori_loop(0, nz, add, (zero, zero))
    mask_x = within(first_x + sub, fp[0:1], DISK_X)
    sums_ref[0:1, :] = jnp.sum(acc[0] * mask_x, axis=0, keepdims=True)
    sums_ref[1:2, :] = jnp.sum(acc[1] * mask_x, axis=0, keepdims=True)
    sums_ref[2:8, :] = jnp.zeros((6, 128), F32)


def rim_kernel(
    sa_ref, sb_ref, ra_ref, rb_ref, in_ref, fp_ref, sums_ref, p_in, p_ref, hl_ref, hh_ref, rows_ref
):
    nz = hl_ref.shape[0]
    tile_x = lax.axis_index("gx")
    last_x = lax.axis_size("gx") - 1
    even = tile_x % 2 == 0
    first_x = tile_x * 16
    first_y = lax.axis_index("gy") * 128
    fp = fp_ref[...]
    lane = iota((8, 128), 1)
    sub = iota((8, 128), 0)

    @pl.when(even)
    def _():
        hl_ref[...] = rb_ref[...]
        hh_ref[...] = ra_ref[...]

    @pl.when(jnp.logical_not(even))
    def _():
        hl_ref[...] = ra_ref[...]
        hh_ref[...] = rb_ref[...]

    @pl.when(tile_x == 0)
    def _():
        for c in range(4):
            for z in range(nz):
                hl_ref[z, 2 * c + 1 : 2 * c + 2, :] = in_ref[c, z : z + 1, :]

    @pl.when(tile_x == last_x)
    def _():
        for z in range(nz):
            hh_ref[z] = pltpu.roll(sb_ref[z], 7, 0)

    def row(x, i):
        return x[i : i + 1]

    for half in range(2):
        lo, hi = half * 32, min(nz, half * 32 + 32)

        def one(z, packed):
            below = jnp.maximum(z - 1, 0)
            above = jnp.minimum(z + 1, nz - 1)
            own_a, own_b = sa_ref[z], sb_ref[z]
            own_low = jnp.where(even, own_b, own_a)
            own_high = jnp.where(even, own_a, own_b)
            low, high = hl_ref[z], hh_ref[z]
            u_low = jnp.where(sub == 0, row(low, 1), row(high, 0))
            v_low = jnp.where(sub == 0, row(low, 3), row(high, 2))
            w_low = jnp.where(sub == 0, row(low, 5), row(high, 4))
            west = jnp.where(sub == 0, row(low, 0), row(own_high, 1))
            east = jnp.where(sub == 0, row(own_low, 0), row(high, 1))
            down = jnp.where(sub == 0, row(hl_ref[below], 1), row(hh_ref[below], 0))
            up = jnp.where(sub == 0, row(hl_ref[above], 1), row(hh_ref[above], 0))
            south = jnp.where(lane == 0, 0.0, pltpu.roll(u_low, 1, 1))
            north = jnp.where(lane == 127, 0.0, pltpu.roll(u_low, 127, 1))
            ring = mix(coefs(u_low, v_low, w_low), u_low, west, east, south, north, down, up)
            into_low = upwind(row(own_low, 0))[0] * row(low, 1)
            into_high = upwind(row(own_high, 1))[1] * row(high, 0)
            both = jnp.where(sub == 2, into_low, jnp.where(sub == 3, into_high, ring))
            both = jnp.where(sub == 4, row(low, 0), both)
            both = jnp.where(sub == 5, row(low, 1), both)
            both = jnp.where(sub == 6, row(high, 0), both)
            both = jnp.where(sub == 7, row(high, 1), both)
            rows_ref[z] = both
            here = lane // 4 == z - lo
            shift = (2 + 4 * (z - lo)) % 128
            return (
                jnp.where(here, pltpu.roll(low, shift, 1), packed[0]),
                jnp.where(here, pltpu.roll(high, shift, 1), packed[1]),
            )

        zero = jnp.zeros((8, 128), F32)
        packed = lax.fori_loop(lo, hi, one, (zero, zero))
        for c in range(4):
            p_ref[half, c, 0:16, :] = p_in[half, c, 0:16, :]
            p_ref[half, c, 16:17, :] = row(packed[0], 2 * c + 1)
            p_ref[half, c, 17:18, :] = row(packed[1], 2 * c)
            p_ref[half, c, 18:24, :] = jnp.zeros((6, 128), F32)

    span = span_mask(fp, first_y, 128)
    rows_ref[...] = dot_nn(rows_ref[...].reshape(nz * 8, 128), span).reshape(nz, 8, 128)

    def add(z, acc):
        return acc + rows_ref[z] * within(z, fp[2:3], DISK_Z)

    acc = lax.fori_loop(0, nz, add, jnp.zeros((8, 128), F32))
    column = jnp.where(sub == 0, -1, 16)
    column = jnp.where(sub == 2, 0, jnp.where(sub == 3, 15, column))
    column = jnp.where(sub >= 4, jnp.where(sub < 6, sub - 6, sub + 10), column)
    acc = acc * within(first_x + column, fp[0:1], DISK_X)
    p_ref[0, 0, 18:19, :] = sums_ref[0:1, :] + jnp.sum(acc[4:8], axis=0, keepdims=True)
    p_ref[1, 0, 18:19, :] = sums_ref[1:2, :] + jnp.sum(acc[0:4], axis=0, keepdims=True)


def steps_kernel(
    f_ref,
    sa_ref,
    sb_ref,
    hl_ref,
    hh_ref,
    p_ref,
    pa_ref,
    pb_ref,
    fp_ref,
    lap_ref,
    out_ref,
    mid_ref,
    force_ref,
    rim_force_ref,
    ring_ref,
    edge_ref,
    corner_ref,
):
    nz = f_ref.shape[1]
    tile_x = lax.axis_index("gx")
    tile_y = lax.axis_index("gy")
    last_x = lax.axis_size("gx") - 1
    all_y = lax.axis_size("gy") * 128
    even_x = tile_x % 2 == 0
    even_y = tile_y % 2 == 0
    first_x = tile_x * 16
    first_y = tile_y * 128
    fp = fp_ref[...]
    fx, fy, fz = fp[0:1], fp[1:2], fp[2:3]
    lane = iota((16, 128), 1)
    sub = iota((16, 128), 0)

    def pick(half, c):
        a, b = pa_ref[half, c], pb_ref[half, c]
        return jnp.where(even_y, b, a), jnp.where(even_y, a, b)

    k24 = iota((24, 128), 1) % 4
    left_cols, right_cols = [], []
    for c in range(4):
        lefts, rights = [], []
        for half in range(2):
            left, right = pick(half, c)
            own = p_ref[half, c]
            lefts.append(jnp.where(k24 < 2, left, own))
            rights.append(jnp.where(k24 < 2, own, right))
            edge = jnp.where(k24 == 1, left, pltpu.roll(right, 126, 1))
            edge_ref[0, half, c] = edge[0:16]
            corner_ref[0, half, 2 * c + 1 : 2 * c + 2, :] = edge[16:17]
            corner_ref[1, half, 2 * c : 2 * c + 1, :] = edge[17:18]
        left_cols.append(jnp.concatenate(lefts, axis=1))
        right_cols.append(jnp.concatenate(rights, axis=1))
    for half in range(2):
        for c in range(4):
            corner_ref[0, half, 2 * c : 2 * c + 1, :] = jnp.zeros((1, 128), F32)
            corner_ref[1, half, 2 * c + 1 : 2 * c + 2, :] = jnp.zeros((1, 128), F32)

    def total(half):
        left, right = pick(half, 0)
        return p_ref[half, 0, 18:19, :] + left[18:19] + right[18:19]

    def thrust_of(sums):
        speed = sums * (1.0 / CELLS)
        return -GAIN * DT * speed * jnp.abs(speed)

    thrust1 = thrust_of(total(0))
    at = iota((256, 128), 0)
    level = at // 4
    k_at = at % 4
    mask_level = within(level, fz, DISK_Z) * (level < nz).astype(F32)
    y_left = jnp.where(k_at == 1, jnp.where(first_y == 0, all_y - 1, first_y - 1), first_y)
    y_right = jnp.where(
        k_at == 1, first_y + 127, jnp.where(first_y + 128 == all_y, 0, first_y + 128)
    )
    middle = ((k_at == 1) | (k_at == 2)).astype(F32)
    mask_left = mask_level * within(y_left, fy, DISK_Y) * middle
    mask_right = mask_level * within(y_right, fy, DISK_Y) * middle
    k256 = iota((24, 256), 1) % 4

    def facing(cols, mask):
        u, v = cols[0], cols[1]
        cs, cn = upwind(v)
        term = jnp.where(k256 == 1, cn * pltpu.roll(u, 255, 1), cs * pltpu.roll(u, 1, 1))
        term = jnp.concatenate([term, jnp.zeros((8, 256), F32)], axis=0)
        return dot_nn(term, mask.astype(jnp.bfloat16))

    faces = facing(left_cols, mask_left) + facing(right_cols, mask_right)
    sub32 = iota((32, 128), 0)
    column = jnp.where(sub32 == 16, -1, jnp.where(sub32 == 17, 16, sub32))
    mask_x32 = within(first_x + column, fx, DISK_X) * (sub32 < 18).astype(F32)
    faces = jnp.sum(faces * mask_x32, axis=0, keepdims=True)
    pushed = jnp.dot(
        jnp.broadcast_to(thrust1, (8, 128)),
        lap_ref[...],
        precision=lax.Precision.HIGHEST,
        preferred_element_type=F32,
    )
    thrust2 = thrust_of(total(1) + faces + pushed[0:1])

    span = span_mask(fp, first_y, 128)
    mask_x = within(first_x + sub, fx, DISK_X)
    by_x1 = mask_x * thrust1
    by_x2 = mask_x * thrust2
    sub8 = iota((8, 128), 0)
    rim_column = jnp.where(sub8 == 1, -1, 16)
    by_rim = within(first_x + rim_column, fx, DISK_X) * thrust1 * (sub8 < 2).astype(F32)

    def weigh(z, carry):
        mask = within(z, fz, DISK_Z)
        force_ref[0, z] = by_x1 * mask
        force_ref[1, z] = by_x2 * mask
        rim_force_ref[z] = by_rim * mask
        return carry

    lax.fori_loop(0, nz, weigh, 0)
    force_ref[...] = dot_nt(force_ref[...].reshape(2 * nz * 16, 128), span).reshape(2, nz, 16, 128)
    rim_force_ref[...] = dot_nt(rim_force_ref[...].reshape(nz * 8, 128), span).reshape(nz, 8, 128)
    y_cols = jnp.where(k_at == 1, y_left, y_right)
    mask_cols = mask_level * within(y_cols, fy, DISK_Y) * middle
    force_cols = dot_nt(by_x1, mask_cols.astype(jnp.bfloat16))

    lane256 = iota((16, 256), 1)
    sub256 = iota((16, 256), 0)

    def rim_cols(cols):
        cur = [x[0:16] for x in cols]
        c = coefs(cur[0], cur[1], cur[2])
        new = []
        for i in range(4):
            f = cur[i]
            west = jnp.where(sub256 == 0, cols[i][16:17], pltpu.roll(f, 1, 0))
            east = jnp.where(sub256 == 15, cols[i][17:18], pltpu.roll(f, 15, 0))
            south = pltpu.roll(f, 1, 1)
            north = pltpu.roll(f, 255, 1)
            down = jnp.where(lane256 < 4, f, pltpu.roll(f, 4, 1))
            up = jnp.where(lane256 >= 4 * nz - 4, f, pltpu.roll(f, 252, 1))
            new.append(mix(c, f, west, east, south, north, down, up))
        new[0] = new[0] + force_cols
        new[2] = new[2] + (DT * BUOY) * cur[3]
        return new

    left_new, right_new = rim_cols(left_cols), rim_cols(right_cols)
    for c in range(4):
        edge = jnp.where(lane256 % 4 == 1, left_new[c], pltpu.roll(right_new[c], 254, 1))
        edge_ref[1, 0, c] = edge[:, 0:128]
        edge_ref[1, 1, c] = edge[:, 128:256]

    lane8 = iota((8, 128), 1)

    def rim_rows(z, carry):
        below = jnp.maximum(z - 1, 0)
        above = jnp.minimum(z + 1, nz - 1)
        half = z // 32
        shift = (255 - 4 * (z - 32 * half)) % 128
        own_a, own_b = sa_ref[z], sb_ref[z]
        own = (jnp.where(even_x, own_b, own_a), jnp.where(even_x, own_a, own_b))
        for side, ref in ((0, hl_ref), (1, hh_ref)):
            cur = ref[z]
            at_row = 1 - side
            turn = 1 if side == 0 else 7
            outer = pltpu.roll(cur, turn, 0)
            inner = pltpu.roll(own[side], turn, 0)
            west, east = (outer, inner) if side == 0 else (inner, outer)
            corner = pltpu.roll(corner_ref[side, half], shift, 1)
            south = jnp.where(lane8 == 0, corner, pltpu.roll(cur, 1, 1))
            north = jnp.where(lane8 == 127, corner, pltpu.roll(cur, 127, 1))
            c = coefs(
                cur[at_row : at_row + 1],
                cur[at_row + 2 : at_row + 3],
                cur[at_row + 4 : at_row + 5],
            )
            new = mix(c, cur, west, east, south, north, ref[below], ref[above])
            warm = cur[at_row + 6 : at_row + 7]
            new = new + jnp.where(sub8 == at_row + 4, (DT * BUOY) * warm, 0.0)
            new = new + jnp.where(
                sub8 == at_row, rim_force_ref[z, at_row : at_row + 1, :], 0.0
            )
            if side == 0:
                new = jnp.where(tile_x == 0, cur, new)
            ring_ref[side, z] = new
        return carry

    lax.fori_loop(0, nz, rim_rows, 0)

    def tile_step(step, src, dst, low_ref, high_ref):
        def one(z, carry):
            below = jnp.maximum(z - 1, 0)
            above = jnp.minimum(z + 1, nz - 1)
            half = z // 32
            shift = (255 - 4 * (z - 32 * half)) % 128
            cur = [src[c, z] for c in range(4)]
            low, high = low_ref(z), high_ref(z)
            c = coefs(cur[0], cur[1], cur[2])
            for i in range(4):
                f = cur[i]
                west = jnp.where(sub == 0, low[2 * i + 1 : 2 * i + 2], pltpu.roll(f, 1, 0))
                outside = high[2 * i : 2 * i + 1]
                if step == 1:
                    outside = jnp.where(tile_x == last_x, f[15:16], outside)
                east = jnp.where(sub == 15, outside, pltpu.roll(f, 15, 0))
                edge = pltpu.roll(edge_ref[step, half, i], shift, 1)
                south = jnp.where(lane == 0, edge, pltpu.roll(f, 1, 1))
                north = jnp.where(lane == 127, edge, pltpu.roll(f, 127, 1))
                new = mix(c, f, west, east, south, north, src[i, below], src[i, above])
                if i == 0:
                    new = new + force_ref[step, z]
                if i == 2:
                    new = new + (DT * BUOY) * cur[3]
                dst[i, z] = new
            return carry

        lax.fori_loop(0, nz, one, 0)

    tile_step(0, f_ref, mid_ref, lambda z: hl_ref[z], lambda z: hh_ref[z])
    tile_step(1, mid_ref, out_ref, lambda z: ring_ref[0, z], lambda z: ring_ref[1, z])


def call(kernel, out, scratch=(), aliases=None, flops=1 << 20, size=1 << 20):
    return pl.pallas_call(
        kernel,
        out_shape=out,
        scratch_shapes=scratch,
        input_output_aliases=aliases or {},
        compiler_params=pltpu.CompilerParams(vmem_limit_bytes=24 << 20),
        cost_estimate=pl.CostEstimate(flops=flops, bytes_accessed=size, transcendentals=0),
    )


def fetch_inlet(inflow, target, tile_x, count):
    stride = count
    block = inflow
    while stride > 1:
        radix = 4 if stride % 4 == 0 else 2
        stride //= radix
        digit = (target // stride) % radix
        parts = [
            lax.ppermute(block, "gx", [(x + k * stride, x) for x in range(stride)])
            for k in range(1, radix)
        ]
        for k in range(1, radix):
            block = jnp.where(digit == k, parts[k - 1], block)
    return block


def body(flow_state, inflow, footprint, block_map):
    levels = flow_state.shape[1]
    tile_x = lax.axis_index("gx")
    tile_y = lax.axis_index("gy")
    count_x = lax.axis_size("gx")
    count_y = lax.axis_size("gy")
    turbines = footprint.shape[0]
    shape = lambda *s: jax.ShapeDtypeStruct(s, F32)

    fp = jnp.pad(
        footprint.T, ((0, 5), (0, 128 - turbines)), constant_values=FAR
    )
    lap = jnp.ones((128, 128), F32)
    for i, extent in enumerate((DISK_X, DISK_Y, DISK_Z)):
        lap = lap * jnp.maximum(extent - jnp.abs(fp[i][:, None] - fp[i][None, :]), 0).astype(F32)
    live = jnp.arange(128) < turbines
    lap = jnp.where(live[:, None] & live[None, :], lap, 0.0)

    inlet = fetch_inlet(inflow, block_map[tile_y], tile_x, count_x)

    x_pack = shape(levels, 8, 128)
    send_a, send_b = call(pack_x_kernel, (x_pack, x_pack))(flow_state)
    recv_a = lax.ppermute(send_a, "gx", pairs(count_x, False))
    recv_b = lax.ppermute(send_b, ("gx", "gy"), pairs_inside(count_x, count_y))

    y_pack = shape(2, 4, 24, 128)
    own, sums = call(
        tile_kernel, (y_pack, shape(8, 128)), [pltpu.VMEM((2, levels, 16, 128), F32)]
    )(flow_state, fp)
    own, low, high = call(
        rim_kernel, (y_pack, x_pack, x_pack), [pltpu.VMEM((levels, 8, 128), F32)]
    )(send_a, send_b, recv_a, recv_b, inlet, fp, sums, own)
    side_a = lax.ppermute(own, "gy", pairs(count_y, False))
    side_b = lax.ppermute(own, "gy", pairs(count_y, True))
    return call(
        steps_kernel,
        shape(*flow_state.shape),
        [
            pltpu.VMEM(flow_state.shape, F32),
            pltpu.VMEM((2, levels, 16, 128), F32),
            pltpu.VMEM((levels, 8, 128), F32),
            pltpu.VMEM((2, levels, 8, 128), F32),
            pltpu.VMEM((2, 2, 4, 16, 128), F32),
            pltpu.VMEM((2, 2, 8, 128), F32),
        ],
    )(flow_state, send_a, send_b, low, high, own, side_a, side_b, fp, lap)


def solution(mesh):
    placed = (P(None, None, "gx", "gy"), P(None, None, "gx"), P(), P())
    return jax.shard_map(
        body, mesh=mesh, in_specs=placed, out_specs=P(None, None, "gx", "gy"), check_vma=False
    )
```

```python
import jax
import jax.numpy as jnp
from jax import lax
from jax.experimental import pallas as pl
from jax.experimental.pallas import tpu as pltpu
from jax.sharding import PartitionSpec as P

DISK_X = 2
DISK_Y = 24
DISK_Z = 24
CELLS = float(DISK_X * DISK_Y * DISK_Z)

DT = 0.15
VISC = 0.3
BUOY = 0.3
GAIN = 2.0
BASE = DT * VISC
FAR = -100000
F32 = jnp.float32


def pairs(n, odd):
    if not odd:
        return [(i, i ^ 1) for i in range(n)]
    return [(i, (i + 1) % n if i % 2 else (i - 1) % n) for i in range(n)]


def pairs_inside(nx, ny):
    out = []
    for i in range(nx):
        for j in range(ny):
            if i in (0, nx - 1):
                to = (i, j ^ 1)
            else:
                to = (i + 1 if i % 2 else i - 1, j)
            out.append((i * ny + j, to[0] * ny + to[1]))
    return out


def upwind(vel):
    scaled = DT * vel
    return jnp.maximum(scaled, 0.0) + BASE, BASE - jnp.minimum(scaled, 0.0)


def coefs(u, v, w):
    cw, ce = upwind(u)
    cs, cn = upwind(v)
    cb, ca = upwind(w)
    c0 = 1.0 - ((cw + ce) + (cs + cn) + (cb + ca))
    return c0, cw, ce, cs, cn, cb, ca


def mix(c, f, w, e, s, n, b, a):
    return c[0] * f + c[1] * w + c[2] * e + c[3] * s + c[4] * n + c[5] * b + c[6] * a


def dot_nt(a, m):
    high = a.astype(jnp.bfloat16)
    low = (a - high.astype(F32)).astype(jnp.bfloat16)
    dims = (((1,), (1,)), ((), ()))
    return lax.dot_general(high, m, dims, preferred_element_type=F32) + lax.dot_general(
        low, m, dims, preferred_element_type=F32
    )


def dot_nn(a, m):
    high = a.astype(jnp.bfloat16)
    low = (a - high.astype(F32)).astype(jnp.bfloat16)
    return jnp.dot(high, m, preferred_element_type=F32) + jnp.dot(
        low, m, preferred_element_type=F32
    )


def iota(shape, dim):
    return lax.broadcasted_iota(jnp.int32, shape, dim)


def within(cells, start, extent):
    return ((cells >= start) & (cells < start + extent)).astype(F32)


def span_mask(fp, first, count):
    return within(first + iota((count, 128), 0), fp[1:2], DISK_Y).astype(jnp.bfloat16)


def pack_x_kernel(f_ref, a_ref, b_ref):
    even = lax.axis_index("gx") % 2 == 0

    def fill(low_ref, high_ref):
        for c in range(4):
            low_ref[:, 2 * c : 2 * c + 2, :] = f_ref[c, :, 0:2, :]
            high_ref[:, 2 * c : 2 * c + 2, :] = f_ref[c, :, 14:16, :]

    @pl.when(even)
    def _():
        fill(b_ref, a_ref)

    @pl.when(jnp.logical_not(even))
    def _():
        fill(a_ref, b_ref)


def tile_kernel(f_ref, fp_ref, p_ref, sums_ref, rows_ref):
    nz = f_ref.shape[1]
    first_x = lax.axis_index("gx") * 16
    first_y = lax.axis_index("gy") * 128
    fp = fp_ref[...]
    lane = iota((16, 128), 1)
    sub = iota((16, 128), 0)
    p_ref[...] = jnp.zeros_like(p_ref)

    for half in range(2):
        lo, hi = half * 32, min(nz, half * 32 + 32)

        def one(z, packed):
            below = jnp.maximum(z - 1, 0)
            above = jnp.minimum(z + 1, nz - 1)
            cur = [f_ref[c, z] for c in range(4)]
            u = cur[0]
            c = coefs(u, cur[1], cur[2])
            west = jnp.where(sub == 0, 0.0, pltpu.roll(u, 1, 0))
            east = jnp.where(sub == 15, 0.0, pltpu.roll(u, 15, 0))
            south = jnp.where(lane == 0, 0.0, pltpu.roll(u, 1, 1))
            north = jnp.where(lane == 127, 0.0, pltpu.roll(u, 127, 1))
            rows_ref[1, z] = mix(c, u, west, east, south, north, f_ref[0, below], f_ref[0, above])
            rows_ref[0, z] = u
            here = lane // 4 == z - lo
            shift = (2 + 4 * (z - lo)) % 128
            return tuple(
                jnp.where(here, pltpu.roll(cur[i], shift, 1), packed[i]) for i in range(4)
            )

        packed = lax.fori_loop(lo, hi, one, tuple(jnp.zeros((16, 128), F32) for _ in range(4)), unroll=8)
        for i in range(4):
            p_ref[half, i, 0:16, :] = packed[i]

    span = span_mask(fp, first_y, 128)
    rows = rows_ref[...].reshape(2 * nz * 16, 128)
    rows_ref[...] = dot_nn(rows, span).reshape(2, nz, 16, 128)

    def add(z, acc):
        mask = within(z, fp[2:3], DISK_Z)
        return acc[0] + rows_ref[0, z] * mask, acc[1] + rows_ref[1, z] * mask

    zero = jnp.zeros((16, 128), F32)
    acc = lax.fori_loop(0, nz, add, (zero, zero), unroll=8)
    mask_x = within(first_x + sub, fp[0:1], DISK_X)
    sums_ref[0:1, :] = jnp.sum(acc[0] * mask_x, axis=0, keepdims=True)
    sums_ref[1:2, :] = jnp.sum(acc[1] * mask_x, axis=0, keepdims=True)
    sums_ref[2:8, :] = jnp.zeros((6, 128), F32)


def rim_kernel(
    sa_ref, sb_ref, ra_ref, rb_ref, in_ref, fp_ref, sums_ref, p_in, p_ref, hl_ref, hh_ref, rows_ref
):
    nz = hl_ref.shape[0]
    tile_x = lax.axis_index("gx")
    last_x = lax.axis_size("gx") - 1
    even = tile_x % 2 == 0
    first_x = tile_x * 16
    first_y = lax.axis_index("gy") * 128
    fp = fp_ref[...]
    lane = iota((8, 128), 1)
    sub = iota((8, 128), 0)

    @pl.when(even)
    def _():
        hl_ref[...] = rb_ref[...]
        hh_ref[...] = ra_ref[...]

    @pl.when(jnp.logical_not(even))
    def _():
        hl_ref[...] = ra_ref[...]
        hh_ref[...] = rb_ref[...]

    @pl.when(tile_x == 0)
    def _():
        for c in range(4):
            for z in range(nz):
                hl_ref[z, 2 * c + 1 : 2 * c + 2, :] = in_ref[c, z : z + 1, :]

    @pl.when(tile_x == last_x)
    def _():
        for z in range(nz):
            hh_ref[z] = pltpu.roll(sb_ref[z], 7, 0)

    def row(x, i):
        return x[i : i + 1]

    for half in range(2):
        lo, hi = half * 32, min(nz, half * 32 + 32)

        def one(z, packed):
            below = jnp.maximum(z - 1, 0)
            above = jnp.minimum(z + 1, nz - 1)
            own_a, own_b = sa_ref[z], sb_ref[z]
            own_low = jnp.where(even, own_b, own_a)
            own_high = jnp.where(even, own_a, own_b)
            low, high = hl_ref[z], hh_ref[z]
            u_low = jnp.where(sub == 0, row(low, 1), row(high, 0))
            v_low = jnp.where(sub == 0, row(low, 3), row(high, 2))
            w_low = jnp.where(sub == 0, row(low, 5), row(high, 4))
            west = jnp.where(sub == 0, row(low, 0), row(own_high, 1))
            east = jnp.where(sub == 0, row(own_low, 0), row(high, 1))
            down = jnp.where(sub == 0, row(hl_ref[below], 1), row(hh_ref[below], 0))
            up = jnp.where(sub == 0, row(hl_ref[above], 1), row(hh_ref[above], 0))
            south = jnp.where(lane == 0, 0.0, pltpu.roll(u_low, 1, 1))
            north = jnp.where(lane == 127, 0.0, pltpu.roll(u_low, 127, 1))
            ring = mix(coefs(u_low, v_low, w_low), u_low, west, east, south, north, down, up)
            into_low = upwind(row(own_low, 0))[0] * row(low, 1)
            into_high = upwind(row(own_high, 1))[1] * row(high, 0)
            both = jnp.where(sub == 2, into_low, jnp.where(sub == 3, into_high, ring))
            both = jnp.where(sub == 4, row(low, 0), both)
            both = jnp.where(sub == 5, row(low, 1), both)
            both = jnp.where(sub == 6, row(high, 0), both)
            both = jnp.where(sub == 7, row(high, 1), both)
            rows_ref[z] = both
            here = lane // 4 == z - lo
            shift = (2 + 4 * (z - lo)) % 128
            return (
                jnp.where(here, pltpu.roll(low, shift, 1), packed[0]),
                jnp.where(here, pltpu.roll(high, shift, 1), packed[1]),
            )

        zero = jnp.zeros((8, 128), F32)
        packed = lax.fori_loop(lo, hi, one, (zero, zero), unroll=8)
        for c in range(4):
            p_ref[half, c, 0:16, :] = p_in[half, c, 0:16, :]
            p_ref[half, c, 16:17, :] = row(packed[0], 2 * c + 1)
            p_ref[half, c, 17:18, :] = row(packed[1], 2 * c)
            p_ref[half, c, 18:24, :] = jnp.zeros((6, 128), F32)

    span = span_mask(fp, first_y, 128)
    rows_ref[...] = dot_nn(rows_ref[...].reshape(nz * 8, 128), span).reshape(nz, 8, 128)

    def add(z, acc):
        return acc + rows_ref[z] * within(z, fp[2:3], DISK_Z)

    acc = lax.fori_loop(0, nz, add, jnp.zeros((8, 128), F32), unroll=8)
    column = jnp.where(sub == 0, -1, 16)
    column = jnp.where(sub == 2, 0, jnp.where(sub == 3, 15, column))
    column = jnp.where(sub >= 4, jnp.where(sub < 6, sub - 6, sub + 10), column)
    acc = acc * within(first_x + column, fp[0:1], DISK_X)
    p_ref[0, 0, 18:19, :] = sums_ref[0:1, :] + jnp.sum(acc[4:8], axis=0, keepdims=True)
    p_ref[1, 0, 18:19, :] = sums_ref[1:2, :] + jnp.sum(acc[0:4], axis=0, keepdims=True)


def steps_kernel(
    f_ref,
    sa_ref,
    sb_ref,
    hl_ref,
    hh_ref,
    p_ref,
    pa_ref,
    pb_ref,
    fp_ref,
    lap_ref,
    out_ref,
    mid_ref,
    force_ref,
    rim_force_ref,
    ring_ref,
    edge_ref,
    corner_ref,
):
    nz = f_ref.shape[1]
    tile_x = lax.axis_index("gx")
    tile_y = lax.axis_index("gy")
    last_x = lax.axis_size("gx") - 1
    all_y = lax.axis_size("gy") * 128
    even_x = tile_x % 2 == 0
    even_y = tile_y % 2 == 0
    first_x = tile_x * 16
    first_y = tile_y * 128
    fp = fp_ref[...]
    fx, fy, fz = fp[0:1], fp[1:2], fp[2:3]
    lane = iota((16, 128), 1)
    sub = iota((16, 128), 0)

    def pick(half, c):
        a, b = pa_ref[half, c], pb_ref[half, c]
        return jnp.where(even_y, b, a), jnp.where(even_y, a, b)

    k24 = iota((24, 128), 1) % 4
    left_cols, right_cols = [], []
    for c in range(4):
        lefts, rights = [], []
        for half in range(2):
            left, right = pick(half, c)
            own = p_ref[half, c]
            lefts.append(jnp.where(k24 < 2, left, own))
            rights.append(jnp.where(k24 < 2, own, right))
            edge = jnp.where(k24 == 1, left, pltpu.roll(right, 126, 1))
            edge_ref[0, half, c] = edge[0:16]
            corner_ref[0, half, 2 * c + 1 : 2 * c + 2, :] = edge[16:17]
            corner_ref[1, half, 2 * c : 2 * c + 1, :] = edge[17:18]
        left_cols.append(jnp.concatenate(lefts, axis=1))
        right_cols.append(jnp.concatenate(rights, axis=1))
    for half in range(2):
        for c in range(4):
            corner_ref[0, half, 2 * c : 2 * c + 1, :] = jnp.zeros((1, 128), F32)
            corner_ref[1, half, 2 * c + 1 : 2 * c + 2, :] = jnp.zeros((1, 128), F32)

    def total(half):
        left, right = pick(half, 0)
        return p_ref[half, 0, 18:19, :] + left[18:19] + right[18:19]

    def thrust_of(sums):
        speed = sums * (1.0 / CELLS)
        return -GAIN * DT * speed * jnp.abs(speed)

    thrust1 = thrust_of(total(0))
    at = iota((256, 128), 0)
    level = at // 4
    k_at = at % 4
    mask_level = within(level, fz, DISK_Z) * (level < nz).astype(F32)
    y_left = jnp.where(k_at == 1, jnp.where(first_y == 0, all_y - 1, first_y - 1), first_y)
    y_right = jnp.where(
        k_at == 1, first_y + 127, jnp.where(first_y + 128 == all_y, 0, first_y + 128)
    )
    middle = ((k_at == 1) | (k_at == 2)).astype(F32)
    mask_left = mask_level * within(y_left, fy, DISK_Y) * middle
    mask_right = mask_level * within(y_right, fy, DISK_Y) * middle
    k256 = iota((24, 256), 1) % 4

    def facing(cols, mask):
        u, v = cols[0], cols[1]
        cs, cn = upwind(v)
        term = jnp.where(k256 == 1, cn * pltpu.roll(u, 255, 1), cs * pltpu.roll(u, 1, 1))
        term = jnp.concatenate([term, jnp.zeros((8, 256), F32)], axis=0)
        return dot_nn(term, mask.astype(jnp.bfloat16))

    faces = facing(left_cols, mask_left) + facing(right_cols, mask_right)
    sub32 = iota((32, 128), 0)
    column = jnp.where(sub32 == 16, -1, jnp.where(sub32 == 17, 16, sub32))
    mask_x32 = within(first_x + column, fx, DISK_X) * (sub32 < 18).astype(F32)
    faces = jnp.sum(faces * mask_x32, axis=0, keepdims=True)
    pushed = jnp.dot(
        jnp.broadcast_to(thrust1, (8, 128)),
        lap_ref[...],
        precision=lax.Precision.HIGHEST,
        preferred_element_type=F32,
    )
    thrust2 = thrust_of(total(1) + faces + pushed[0:1])

    span = span_mask(fp, first_y, 128)
    mask_x = within(first_x + sub, fx, DISK_X)
    by_x1 = mask_x * thrust1
    by_x2 = mask_x * thrust2
    sub8 = iota((8, 128), 0)
    rim_column = jnp.where(sub8 == 1, -1, 16)
    by_rim = within(first_x + rim_column, fx, DISK_X) * thrust1 * (sub8 < 2).astype(F32)

    def weigh(z, carry):
        mask = within(z, fz, DISK_Z)
        force_ref[0, z] = by_x1 * mask
        force_ref[1, z] = by_x2 * mask
        rim_force_ref[z] = by_rim * mask
        return carry

    lax.fori_loop(0, nz, weigh, 0, unroll=8)
    force_ref[...] = dot_nt(force_ref[...].reshape(2 * nz * 16, 128), span).reshape(2, nz, 16, 128)
    rim_force_ref[...] = dot_nt(rim_force_ref[...].reshape(nz * 8, 128), span).reshape(nz, 8, 128)
    y_cols = jnp.where(k_at == 1, y_left, y_right)
    mask_cols = mask_level * within(y_cols, fy, DISK_Y) * middle
    force_cols = dot_nt(by_x1, mask_cols.astype(jnp.bfloat16))

    lane256 = iota((16, 256), 1)
    sub256 = iota((16, 256), 0)

    def rim_cols(cols):
        cur = [x[0:16] for x in cols]
        c = coefs(cur[0], cur[1], cur[2])
        new = []
        for i in range(4):
            f = cur[i]
            west = jnp.where(sub256 == 0, cols[i][16:17], pltpu.roll(f, 1, 0))
            east = jnp.where(sub256 == 15, cols[i][17:18], pltpu.roll(f, 15, 0))
            south = pltpu.roll(f, 1, 1)
            north = pltpu.roll(f, 255, 1)
            down = jnp.where(lane256 < 4, f, pltpu.roll(f, 4, 1))
            up = jnp.where(lane256 >= 4 * nz - 4, f, pltpu.roll(f, 252, 1))
            new.append(mix(c, f, west, east, south, north, down, up))
        new[0] = new[0] + force_cols
        new[2] = new[2] + (DT * BUOY) * cur[3]
        return new

    left_new, right_new = rim_cols(left_cols), rim_cols(right_cols)
    for c in range(4):
        edge = jnp.where(lane256 % 4 == 1, left_new[c], pltpu.roll(right_new[c], 254, 1))
        edge_ref[1, 0, c] = edge[:, 0:128]
        edge_ref[1, 1, c] = edge[:, 128:256]

    lane8 = iota((8, 128), 1)

    def rim_rows(z, carry):
        below = jnp.maximum(z - 1, 0)
        above = jnp.minimum(z + 1, nz - 1)
        half = z // 32
        shift = (255 - 4 * (z - 32 * half)) % 128
        own_a, own_b = sa_ref[z], sb_ref[z]
        own = (jnp.where(even_x, own_b, own_a), jnp.where(even_x, own_a, own_b))
        for side, ref in ((0, hl_ref), (1, hh_ref)):
            cur = ref[z]
            at_row = 1 - side
            turn = 1 if side == 0 else 7
            outer = pltpu.roll(cur, turn, 0)
            inner = pltpu.roll(own[side], turn, 0)
            west, east = (outer, inner) if side == 0 else (inner, outer)
            corner = pltpu.roll(corner_ref[side, half], shift, 1)
            south = jnp.where(lane8 == 0, corner, pltpu.roll(cur, 1, 1))
            north = jnp.where(lane8 == 127, corner, pltpu.roll(cur, 127, 1))
            c = coefs(
                cur[at_row : at_row + 1],
                cur[at_row + 2 : at_row + 3],
                cur[at_row + 4 : at_row + 5],
            )
            new = mix(c, cur, west, east, south, north, ref[below], ref[above])
            warm = cur[at_row + 6 : at_row + 7]
            new = new + jnp.where(sub8 == at_row + 4, (DT * BUOY) * warm, 0.0)
            new = new + jnp.where(
                sub8 == at_row, rim_force_ref[z, at_row : at_row + 1, :], 0.0
            )
            if side == 0:
                new = jnp.where(tile_x == 0, cur, new)
            ring_ref[side, z] = new
        return carry

    lax.fori_loop(0, nz, rim_rows, 0, unroll=8)

    def tile_step(step, src, dst, low_ref, high_ref):
        def one(z, carry):
            below = jnp.maximum(z - 1, 0)
            above = jnp.minimum(z + 1, nz - 1)
            half = z // 32
            shift = (255 - 4 * (z - 32 * half)) % 128
            cur = [src[c, z] for c in range(4)]
            low, high = low_ref(z), high_ref(z)
            c = coefs(cur[0], cur[1], cur[2])
            for i in range(4):
                f = cur[i]
                west = jnp.where(sub == 0, low[2 * i + 1 : 2 * i + 2], pltpu.roll(f, 1, 0))
                outside = high[2 * i : 2 * i + 1]
                if step == 1:
                    outside = jnp.where(tile_x == last_x, f[15:16], outside)
                east = jnp.where(sub == 15, outside, pltpu.roll(f, 15, 0))
                edge = pltpu.roll(edge_ref[step, half, i], shift, 1)
                south = jnp.where(lane == 0, edge, pltpu.roll(f, 1, 1))
                north = jnp.where(lane == 127, edge, pltpu.roll(f, 127, 1))
                new = mix(c, f, west, east, south, north, src[i, below], src[i, above])
                if i == 0:
                    new = new + force_ref[step, z]
                if i == 2:
                    new = new + (DT * BUOY) * cur[3]
                dst[i, z] = new
            return carry

        lax.fori_loop(0, nz, one, 0, unroll=8)

    tile_step(0, f_ref, mid_ref, lambda z: hl_ref[z], lambda z: hh_ref[z])
    tile_step(1, mid_ref, out_ref, lambda z: ring_ref[0, z], lambda z: ring_ref[1, z])


def call(kernel, out, scratch=(), aliases=None, flops=1 << 20, size=1 << 20):
    return pl.pallas_call(
        kernel,
        out_shape=out,
        scratch_shapes=scratch,
        input_output_aliases=aliases or {},
        compiler_params=pltpu.CompilerParams(vmem_limit_bytes=24 << 20),
        cost_estimate=pl.CostEstimate(flops=flops, bytes_accessed=size, transcendentals=0),
    )


def fetch_inlet(inflow, target, tile_x, count):
    stride = count
    block = inflow
    while stride > 1:
        radix = 4 if stride % 4 == 0 else 2
        stride //= radix
        digit = (target // stride) % radix
        parts = [
            lax.ppermute(block, "gx", [(x + k * stride, x) for x in range(stride)])
            for k in range(1, radix)
        ]
        for k in range(1, radix):
            block = jnp.where(digit == k, parts[k - 1], block)
    return block


def body(flow_state, inflow, footprint, block_map):
    levels = flow_state.shape[1]
    tile_x = lax.axis_index("gx")
    tile_y = lax.axis_index("gy")
    count_x = lax.axis_size("gx")
    count_y = lax.axis_size("gy")
    turbines = footprint.shape[0]
    shape = lambda *s: jax.ShapeDtypeStruct(s, F32)

    fp = jnp.pad(
        footprint.T, ((0, 5), (0, 128 - turbines)), constant_values=FAR
    )
    lap = jnp.ones((128, 128), F32)
    for i, extent in enumerate((DISK_X, DISK_Y, DISK_Z)):
        lap = lap * jnp.maximum(extent - jnp.abs(fp[i][:, None] - fp[i][None, :]), 0).astype(F32)
    live = jnp.arange(128) < turbines
    lap = jnp.where(live[:, None] & live[None, :], lap, 0.0)

    inlet = fetch_inlet(inflow, block_map[tile_y], tile_x, count_x)

    x_pack = shape(levels, 8, 128)
    send_a, send_b = call(pack_x_kernel, (x_pack, x_pack))(flow_state)
    recv_a = lax.ppermute(send_a, "gx", pairs(count_x, False))
    recv_b = lax.ppermute(send_b, ("gx", "gy"), pairs_inside(count_x, count_y))

    y_pack = shape(2, 4, 24, 128)
    own, sums = call(
        tile_kernel, (y_pack, shape(8, 128)), [pltpu.VMEM((2, levels, 16, 128), F32)]
    )(flow_state, fp)
    own, low, high = call(
        rim_kernel, (y_pack, x_pack, x_pack), [pltpu.VMEM((levels, 8, 128), F32)]
    )(send_a, send_b, recv_a, recv_b, inlet, fp, sums, own)
    side_a = lax.ppermute(own, "gy", pairs(count_y, False))
    side_b = lax.ppermute(own, "gy", pairs(count_y, True))
    return call(
        steps_kernel,
        shape(*flow_state.shape),
        [
            pltpu.VMEM(flow_state.shape, F32),
            pltpu.VMEM((2, levels, 16, 128), F32),
            pltpu.VMEM((levels, 8, 128), F32),
            pltpu.VMEM((2, levels, 8, 128), F32),
            pltpu.VMEM((2, 2, 4, 16, 128), F32),
            pltpu.VMEM((2, 2, 8, 128), F32),
        ],
    )(flow_state, send_a, send_b, low, high, own, side_a, side_b, fp, lap)


def solution(mesh):
    placed = (P(None, None, "gx", "gy"), P(None, None, "gx"), P(), P())
    return jax.shard_map(
        body, mesh=mesh, in_specs=placed, out_specs=P(None, None, "gx", "gy"), check_vma=False
    )
```

```python
import jax
import jax.numpy as jnp
from jax import lax
from jax.experimental import pallas as pl
from jax.experimental.pallas import tpu as pltpu
from jax.sharding import PartitionSpec as P

DISK_X = 2
DISK_Y = 24
DISK_Z = 24
CELLS = float(DISK_X * DISK_Y * DISK_Z)

DT = 0.15
VISC = 0.3
BUOY = 0.3
GAIN = 2.0
BASE = DT * VISC
FAR = -100000
F32 = jnp.float32
UNROLL = 8
GROUP = 4
TILE_COST = 1 << 20
PACK_COST = 1 << 33
STEPS_COST = 1 << 32


def pairs(n, odd):
    if not odd:
        return [(i, i ^ 1) for i in range(n)]
    return [(i, (i + 1) % n if i % 2 else (i - 1) % n) for i in range(n)]


def pairs_inside(nx, ny):
    out = []
    for i in range(nx):
        for j in range(ny):
            if i in (0, nx - 1):
                to = (i, j ^ 1)
            else:
                to = (i + 1 if i % 2 else i - 1, j)
            out.append((i * ny + j, to[0] * ny + to[1]))
    return out


def upwind(vel):
    scaled = DT * vel
    return jnp.maximum(scaled, 0.0) + BASE, BASE - jnp.minimum(scaled, 0.0)


def coefs(u, v, w):
    cw, ce = upwind(u)
    cs, cn = upwind(v)
    cb, ca = upwind(w)
    c0 = 1.0 - ((cw + ce) + (cs + cn) + (cb + ca))
    return c0, cw, ce, cs, cn, cb, ca


def mix(c, f, w, e, s, n, b, a):
    return c[0] * f + c[1] * w + c[2] * e + c[3] * s + c[4] * n + c[5] * b + c[6] * a


def dot_nt(a, m):
    high = a.astype(jnp.bfloat16)
    low = (a - high.astype(F32)).astype(jnp.bfloat16)
    dims = (((1,), (1,)), ((), ()))
    return lax.dot_general(high, m, dims, preferred_element_type=F32) + lax.dot_general(
        low, m, dims, preferred_element_type=F32
    )


def dot_nn(a, m):
    high = a.astype(jnp.bfloat16)
    low = (a - high.astype(F32)).astype(jnp.bfloat16)
    return jnp.dot(high, m, preferred_element_type=F32) + jnp.dot(
        low, m, preferred_element_type=F32
    )


def iota(shape, dim):
    return lax.broadcasted_iota(jnp.int32, shape, dim)


def within(cells, start, extent):
    return ((cells >= start) & (cells < start + extent)).astype(F32)


def span_mask(fp, first, count):
    return within(first + iota((count, 128), 0), fp[1:2], DISK_Y).astype(jnp.bfloat16)


def pack_x_kernel(f_ref, a_ref, b_ref, sems):
    even = lax.axis_index("gx") % 2 == 0
    first_a = jnp.where(even, 14, 0)
    first_b = jnp.where(even, 0, 14)
    copies = []
    for c in range(4):
        for i, (first, ref) in enumerate(((first_a, a_ref), (first_b, b_ref))):
            copies.append(
                pltpu.make_async_copy(
                    f_ref.at[c, :, pl.ds(first, 2), :],
                    ref.at[:, pl.ds(2 * c, 2), :],
                    sems.at[c, i],
                )
            )
    for copy in copies:
        copy.start()
    for copy in copies:
        copy.wait()


def pack_inlet_kernel(map_ref, in_ref, after_ref, msg_ref, code_ref):
    nz = in_ref.shape[1]
    lane = iota((1, 128), 1)
    for c in range(4):
        msg_ref[c, 0:nz, :] = in_ref[c]
        msg_ref[c, nz : nz + 8, :] = jnp.zeros((8, 128), F32)
        for half in range(2):
            packed = jnp.zeros((1, 128), F32)
            for z in range(half * 32, min(nz, half * 32 + 32)):
                at = z - half * 32
                moved = pltpu.roll(in_ref[c, z : z + 1, :], (4 * at + 1) % 128, 1)
                packed = jnp.where(lane // 4 == at, moved, packed)
            msg_ref[c, nz + half : nz + half + 1, :] = packed

    tile_y = lax.axis_index("gy")
    count = lax.axis_size("gy")
    place = tile_y % GROUP
    level = iota((nz + 8, 128), 0)
    first = iota((nz + 8, 128), 1) % 4 == 0
    for k in range(GROUP):
        column = tile_y // GROUP * GROUP + (place ^ k)
        own = map_ref[column]
        left = map_ref[(column + count - 1) % count]
        right = map_ref[(column + 1) % count]
        source = jnp.where(level < nz, own, jnp.where(first, left, right))
        source = jnp.where(source == 3, 6, jnp.where(source == 6, 3, source))
        code = source // GROUP
        code = code + jnp.where(source % GROUP == place, 8, 0)
        code_ref[k] = code + jnp.where(source % GROUP // 2 == place // 2, 16, 0)


def pack_y_kernel(f_ref, after_ref, p_ref):
    nz = f_ref.shape[1]
    lane = iota((16, 128), 1)
    p_ref[...] = jnp.zeros_like(p_ref)
    for half in range(2):
        lo, hi = half * 32, min(nz, half * 32 + 32)

        def one(z, packed):
            here = lane // 4 == z - lo
            shift = (2 + 4 * (z - lo)) % 128
            return tuple(
                jnp.where(here, pltpu.roll(f_ref[i, z], shift, 1), packed[i]) for i in range(4)
            )

        zero = jnp.zeros((16, 128), F32)
        packed = lax.fori_loop(lo, hi, one, (zero,) * 4, unroll=UNROLL)
        for i in range(4):
            p_ref[half, i, 0:16, :] = packed[i]


def base_kernel(f_ref, fp_ref, base_ref, disks_ref, sums_ref, rows_ref):
    nz = f_ref.shape[1]
    first_x = lax.axis_index("gx") * 16
    first_y = lax.axis_index("gy") * 128
    fp = fp_ref[...]
    lane = iota((16, 128), 1)
    sub = iota((16, 128), 0)
    mask_x = within(first_x + sub, fp[0:1], DISK_X)

    def one(z, carry):
        below = jnp.maximum(z - 1, 0)
        above = jnp.minimum(z + 1, nz - 1)
        cur = [f_ref[c, z] for c in range(4)]
        c = coefs(cur[0], cur[1], cur[2])
        cw = jnp.where(sub == 0, 0.0, c[1])
        ce = jnp.where(sub == 15, 0.0, c[2])
        cs = jnp.where(lane == 0, 0.0, c[3])
        cn = jnp.where(lane == 127, 0.0, c[4])
        c = (c[0], cw, ce, cs, cn, c[5], c[6])
        for i in range(4):
            f = cur[i]
            new = mix(
                c,
                f,
                pltpu.roll(f, 1, 0),
                pltpu.roll(f, 15, 0),
                pltpu.roll(f, 1, 1),
                pltpu.roll(f, 127, 1),
                f_ref[i, below],
                f_ref[i, above],
            )
            if i == 2:
                new = new + (DT * BUOY) * cur[3]
            base_ref[i, z] = new
        disks_ref[z] = (mask_x * within(z, fp[2:3], DISK_Z)).astype(jnp.bfloat16)
        return carry

    lax.fori_loop(0, nz, one, 0, unroll=UNROLL)
    span = span_mask(fp, first_y, 128)
    rows_ref[0] = dot_nn(f_ref[0].reshape(nz * 16, 128), span).reshape(nz, 16, 128)
    rows_ref[1] = dot_nn(base_ref[0].reshape(nz * 16, 128), span).reshape(nz, 16, 128)

    def add(z, acc):
        mask = within(z, fp[2:3], DISK_Z)
        return acc[0] + rows_ref[0, z] * mask, acc[1] + rows_ref[1, z] * mask

    zero = jnp.zeros((16, 128), F32)
    acc = lax.fori_loop(0, nz, add, (zero, zero), unroll=UNROLL)
    sums_ref[0:1, :] = jnp.sum(acc[0] * mask_x, axis=0, keepdims=True)
    sums_ref[1:2, :] = jnp.sum(acc[1] * mask_x, axis=0, keepdims=True)
    sums_ref[2:8, :] = jnp.zeros((6, 128), F32)


def rim_kernel(
    sa_ref,
    sb_ref,
    ra_ref,
    rb_ref,
    fp_ref,
    sums_ref,
    p_in,
    p_ref,
    cur_ref,
    west_ref,
    east_ref,
    hl_ref,
    hh_ref,
    rows_ref,
):
    nz = hl_ref.shape[0]
    tile_x = lax.axis_index("gx")
    last_x = lax.axis_size("gx") - 1
    even = tile_x % 2 == 0
    first_x = tile_x * 16
    first_y = lax.axis_index("gy") * 128
    fp = fp_ref[...]
    lane = iota((8, 128), 1)
    sub = iota((8, 128), 0)

    @pl.when(even)
    def _():
        hl_ref[...] = rb_ref[...]
        hh_ref[...] = ra_ref[...]

    @pl.when(jnp.logical_not(even))
    def _():
        hl_ref[...] = ra_ref[...]
        hh_ref[...] = rb_ref[...]

    @pl.when(tile_x == 0)
    def _():
        hl_ref[...] = jnp.zeros_like(hl_ref)

    @pl.when(tile_x == last_x)
    def _():
        for z in range(nz):
            hh_ref[z] = pltpu.roll(sb_ref[z], 7, 0)

    def row(x, i):
        return x[i : i + 1]

    for half in range(2):
        lo, hi = half * 32, min(nz, half * 32 + 32)

        def one(z, packed):
            below = jnp.maximum(z - 1, 0)
            above = jnp.minimum(z + 1, nz - 1)
            own_a, own_b = sa_ref[z], sb_ref[z]
            own_low = jnp.where(even, own_b, own_a)
            own_high = jnp.where(even, own_a, own_b)
            low, high = hl_ref[z], hh_ref[z]
            u_low = jnp.where(sub == 0, row(low, 1), row(high, 0))
            v_low = jnp.where(sub == 0, row(low, 3), row(high, 2))
            w_low = jnp.where(sub == 0, row(low, 5), row(high, 4))
            west = jnp.where(sub == 0, row(low, 0), row(own_high, 1))
            east = jnp.where(sub == 0, row(own_low, 0), row(high, 1))
            down = jnp.where(sub == 0, row(hl_ref[below], 1), row(hh_ref[below], 0))
            up = jnp.where(sub == 0, row(hl_ref[above], 1), row(hh_ref[above], 0))
            south = jnp.where(lane == 0, 0.0, pltpu.roll(u_low, 1, 1))
            north = jnp.where(lane == 127, 0.0, pltpu.roll(u_low, 127, 1))
            ring = mix(coefs(u_low, v_low, w_low), u_low, west, east, south, north, down, up)
            into_low = upwind(row(own_low, 0))[0] * row(low, 1)
            into_high = upwind(row(own_high, 1))[1] * row(high, 0)
            both = jnp.where(sub == 2, into_low, jnp.where(sub == 3, into_high, ring))
            both = jnp.where(sub == 4, row(low, 0), both)
            both = jnp.where(sub == 5, row(low, 1), both)
            both = jnp.where(sub == 6, row(high, 0), both)
            both = jnp.where(sub == 7, row(high, 1), both)
            rows_ref[z] = both
            odd = sub % 2 == 1
            cur_ref[z] = jnp.where(odd, low, high)
            west_ref[z] = jnp.where(odd, pltpu.roll(low, 1, 0), pltpu.roll(own_high, 7, 0))
            east_ref[z] = jnp.where(odd, pltpu.roll(own_low, 1, 0), pltpu.roll(high, 7, 0))
            here = lane // 4 == z - lo
            shift = (2 + 4 * (z - lo)) % 128
            return (
                jnp.where(here, pltpu.roll(low, shift, 1), packed[0]),
                jnp.where(here, pltpu.roll(high, shift, 1), packed[1]),
            )

        zero = jnp.zeros((8, 128), F32)
        packed = lax.fori_loop(lo, hi, one, (zero, zero), unroll=UNROLL)
        for c in range(4):
            p_ref[half, c, 0:16, :] = p_in[half, c, 0:16, :]
            p_ref[half, c, 16:17, :] = row(packed[0], 2 * c + 1)
            p_ref[half, c, 17:18, :] = row(packed[1], 2 * c)
            p_ref[half, c, 18:24, :] = jnp.zeros((6, 128), F32)

    span = span_mask(fp, first_y, 128)
    rows_ref[...] = dot_nn(rows_ref[...].reshape(nz * 8, 128), span).reshape(nz, 8, 128)

    def add(z, acc):
        return acc + rows_ref[z] * within(z, fp[2:3], DISK_Z)

    acc = lax.fori_loop(0, nz, add, jnp.zeros((8, 128), F32), unroll=UNROLL)
    column = jnp.where(sub == 0, -1, 16)
    column = jnp.where(sub == 2, 0, jnp.where(sub == 3, 15, column))
    column = jnp.where(sub >= 4, jnp.where(sub < 6, sub - 6, sub + 10), column)
    acc = acc * within(first_x + column, fp[0:1], DISK_X)
    p_ref[0, 0, 18:19, :] = sums_ref[0:1, :] + jnp.sum(acc[4:8], axis=0, keepdims=True)
    p_ref[1, 0, 18:19, :] = sums_ref[1:2, :] + jnp.sum(acc[0:4], axis=0, keepdims=True)


def steps_kernel(
    f_ref,
    base_ref,
    disks_ref,
    cur_ref,
    west_ref,
    east_ref,
    p_ref,
    pa_ref,
    pb_ref,
    fp_ref,
    lap_ref,
    out_ref,
    first_ref,
    first_corner_ref,
    last_ref,
    mid_ref,
    new_ref,
    force_ref,
    rim_force_ref,
    ring_ref,
    edge_ref,
    corner_ref,
    sems,
):
    nz = f_ref.shape[1]
    tile_x = lax.axis_index("gx")
    tile_y = lax.axis_index("gy")
    last_x = lax.axis_size("gx") - 1
    all_y = lax.axis_size("gy") * 128
    even_y = tile_y % 2 == 0
    first_x = tile_x * 16
    first_y = tile_y * 128
    fp = fp_ref[...]
    fx, fy, fz = fp[0:1], fp[1:2], fp[2:3]
    lane = iota((16, 128), 1)
    sub = iota((16, 128), 0)

    def pick(half, c):
        a, b = pa_ref[half, c], pb_ref[half, c]
        return jnp.where(even_y, b, a), jnp.where(even_y, a, b)

    k24 = iota((24, 128), 1) % 4
    left_cols, right_cols = [], []
    for c in range(4):
        lefts, rights = [], []
        for half in range(2):
            left, right = pick(half, c)
            own = p_ref[half, c]
            lefts.append(jnp.where(k24 < 2, left, own))
            rights.append(jnp.where(k24 < 2, own, right))
            edge = jnp.where(k24 == 1, left, pltpu.roll(right, 126, 1))
            edge_ref[0, half, c] = edge[0:16]
            corner_ref[half, 2 * c + 1 : 2 * c + 2, :] = edge[16:17]
            corner_ref[half, 2 * c : 2 * c + 1, :] = edge[17:18]
        left_cols.append(jnp.concatenate(lefts, axis=1))
        right_cols.append(jnp.concatenate(rights, axis=1))
    def total(half):
        left, right = pick(half, 0)
        return p_ref[half, 0, 18:19, :] + left[18:19] + right[18:19]

    def thrust_of(sums):
        speed = sums * (1.0 / CELLS)
        return -GAIN * DT * speed * jnp.abs(speed)

    thrust1 = thrust_of(total(0))
    at = iota((256, 128), 0)
    level = at // 4
    k_at = at % 4
    mask_level = within(level, fz, DISK_Z) * (level < nz).astype(F32)
    y_left = jnp.where(k_at == 1, jnp.where(first_y == 0, all_y - 1, first_y - 1), first_y)
    y_right = jnp.where(
        k_at == 1, first_y + 127, jnp.where(first_y + 128 == all_y, 0, first_y + 128)
    )
    middle = ((k_at == 1) | (k_at == 2)).astype(F32)
    mask_left = mask_level * within(y_left, fy, DISK_Y) * middle
    mask_right = mask_level * within(y_right, fy, DISK_Y) * middle
    k256 = iota((24, 256), 1) % 4

    def facing(cols, mask):
        u, v = cols[0], cols[1]
        cs, cn = upwind(v)
        term = jnp.where(k256 == 1, cn * pltpu.roll(u, 255, 1), cs * pltpu.roll(u, 1, 1))
        term = jnp.concatenate([term, jnp.zeros((8, 256), F32)], axis=0)
        return dot_nn(term, mask.astype(jnp.bfloat16))

    faces = facing(left_cols, mask_left) + facing(right_cols, mask_right)
    sub32 = iota((32, 128), 0)
    column = jnp.where(sub32 == 16, -1, jnp.where(sub32 == 17, 16, sub32))
    mask_x32 = within(first_x + column, fx, DISK_X) * (sub32 < 18).astype(F32)
    faces = jnp.sum(faces * mask_x32, axis=0, keepdims=True)
    pushed = jnp.dot(
        jnp.broadcast_to(thrust1, (8, 128)),
        lap_ref[...],
        precision=lax.Precision.HIGHEST,
        preferred_element_type=F32,
    )
    thrust2 = thrust_of(total(1) + faces + pushed[0:1])

    span = within(first_y + iota((128, 128), 0), fy, DISK_Y)
    disks = disks_ref[...].reshape(nz * 16, 128)

    def dot_disks(mask, weights):
        high = weights.astype(jnp.bfloat16)
        low = (weights - high.astype(F32)).astype(jnp.bfloat16)
        dims = (((1,), (1,)), ((), ()))
        return lax.dot_general(
            mask, high, dims, preferred_element_type=F32
        ) + lax.dot_general(mask, low, dims, preferred_element_type=F32)

    force_ref[0] = dot_disks(disks, span * thrust1).reshape(nz, 16, 128)
    force_ref[1] = dot_disks(disks, span * thrust2).reshape(nz, 16, 128)
    levels = within(iota((nz, 128), 0), fz, DISK_Z).astype(jnp.bfloat16)
    for side, x in ((0, 16), (1, -1)):
        weights = span * (thrust1 * within(first_x + x, fx, DISK_X))
        rim_force_ref[side] = dot_disks(levels, weights)
    by_x1 = within(first_x + sub, fx, DISK_X) * thrust1
    y_cols = jnp.where(k_at == 1, y_left, y_right)
    mask_cols = mask_level * within(y_cols, fy, DISK_Y) * middle
    force_cols = dot_nt(by_x1, mask_cols.astype(jnp.bfloat16))

    lane256 = iota((16, 256), 1)
    sub256 = iota((16, 256), 0)

    def rim_cols(cols):
        cur = [x[0:16] for x in cols]
        c = coefs(cur[0], cur[1], cur[2])
        new = []
        for i in range(4):
            f = cur[i]
            west = jnp.where(sub256 == 0, cols[i][16:17], pltpu.roll(f, 1, 0))
            east = jnp.where(sub256 == 15, cols[i][17:18], pltpu.roll(f, 15, 0))
            south = pltpu.roll(f, 1, 1)
            north = pltpu.roll(f, 255, 1)
            down = jnp.where(lane256 < 4, f, pltpu.roll(f, 4, 1))
            up = jnp.where(lane256 >= 4 * nz - 4, f, pltpu.roll(f, 252, 1))
            new.append(mix(c, f, west, east, south, north, down, up))
        new[0] = new[0] + force_cols
        new[2] = new[2] + (DT * BUOY) * cur[3]
        return new

    left_new, right_new = rim_cols(left_cols), rim_cols(right_cols)
    for c in range(4):
        edge = jnp.where(lane256 % 4 == 1, left_new[c], pltpu.roll(right_new[c], 254, 1))
        edge_ref[1, 0, c] = edge[:, 0:128]
        edge_ref[1, 1, c] = edge[:, 128:256]

    lane8 = iota((8, 128), 1)
    sub8 = iota((8, 128), 0)
    odd = sub8 % 2 == 1

    def rim_rows(z, carry):
        below = jnp.maximum(z - 1, 0)
        above = jnp.minimum(z + 1, nz - 1)
        half = z // 32
        shift = (255 - 4 * (z - 32 * half)) % 128
        cur = cur_ref[z]
        corner = pltpu.roll(corner_ref[half], shift, 1)
        south = jnp.where(lane8 == 0, corner, pltpu.roll(cur, 1, 1))
        north = jnp.where(lane8 == 127, corner, pltpu.roll(cur, 127, 1))
        vel = [jnp.where(odd, cur[2 * i + 1 : 2 * i + 2], cur[2 * i : 2 * i + 1]) for i in range(4)]
        c = coefs(vel[0], vel[1], vel[2])
        new = mix(c, cur, west_ref[z], east_ref[z], south, north, cur_ref[below], cur_ref[above])
        new = new + jnp.where(sub8 // 2 == 2, (DT * BUOY) * vel[3], 0.0)
        new = new + jnp.where(sub8 == 0, rim_force_ref[0, pl.ds(z, 1), :], 0.0)
        new = new + jnp.where(sub8 == 1, rim_force_ref[1, pl.ds(z, 1), :], 0.0)
        ring_ref[z] = jnp.where(odd & (tile_x == 0), cur, new)
        return carry

    lax.fori_loop(0, nz, rim_rows, 0, unroll=UNROLL)

    def first_step(group, carry):
        for j in range(UNROLL):
            z = group * UNROLL + j
            half = z // 32
            shift = (255 - 4 * (z - 32 * half)) % 128
            near = cur_ref[z]
            cw, ce = upwind(f_ref[0, z])
            cs, cn = upwind(f_ref[1, z])
            along_x = jnp.where(sub == 0, cw, jnp.where(sub == 15, ce, 0.0))
            along_y = jnp.where(lane == 0, cs, jnp.where(lane == 127, cn, 0.0))
            for i in range(4):
                beside = jnp.where(sub < 8, near[2 * i + 1 : 2 * i + 2], near[2 * i : 2 * i + 1])
                edge = pltpu.roll(edge_ref[0, half, i], shift, 1)
                new = base_ref[i, z] + along_x * beside + along_y * edge
                if i == 0:
                    new = new + force_ref[0, z]
                mid_ref[i, z] = new
        return carry

    def level(z):
        below = jnp.maximum(z - 1, 0)
        above = jnp.minimum(z + 1, nz - 1)
        half = z // 32
        shift = (255 - 4 * (z - 32 * half)) % 128
        cur = [mid_ref[c, z] for c in range(4)]
        ring = ring_ref[z]
        c = coefs(cur[0], cur[1], cur[2])
        for i in range(4):
            f = cur[i]
            west = jnp.where(sub == 0, ring[2 * i + 1 : 2 * i + 2], pltpu.roll(f, 1, 0))
            outside = jnp.where(tile_x == last_x, f[15:16], ring[2 * i : 2 * i + 1])
            east = jnp.where(sub == 15, outside, pltpu.roll(f, 15, 0))
            edge = pltpu.roll(edge_ref[1, half, i], shift, 1)
            south = jnp.where(lane == 0, edge, pltpu.roll(f, 1, 1))
            north = jnp.where(lane == 127, edge, pltpu.roll(f, 127, 1))
            new = mix(c, f, west, east, south, north, mid_ref[i, below], mid_ref[i, above])
            if i == 0:
                new = new + force_ref[1, z]
            if i == 2:
                new = new + (DT * BUOY) * cur[3]
            new_ref[i, z] = new

    def send(group):
        part = pl.ds(group * UNROLL, UNROLL)
        return pltpu.make_async_copy(new_ref.at[:, part], out_ref.at[:, part], sems.at[group])

    def second_step(group, carry):
        for i in range(UNROLL):
            z = group * UNROLL + i
            level(z)
        send(group).start()
        return carry

    lax.fori_loop(0, nz // UNROLL, first_step, 0)
    lax.fori_loop(0, nz // UNROLL, second_step, 0)

    @pl.when(tile_x == 0)
    def _():
        for c in range(4):
            first_ref[:, 2 * c : 2 * c + 2, :] = mid_ref[c, :, 0:2, :]
            last_ref[:, 2 * c : 2 * c + 2, :] = new_ref[c, :, 0:2, :]
            for half in range(2):
                first_corner_ref[half, 2 * c : 2 * c + 1, :] = edge_ref[1, half, c, 0:1, :]
                first_corner_ref[half, 2 * c + 1 : 2 * c + 2, :] = edge_ref[0, half, c, 0:1, :]

    for group in range(nz // UNROLL):
        send(group).wait()


def fix_kernel(
    out_in, in_ref, sb_ref, first_ref, corner_ref, last_ref, out_ref, inlet, new, wide, done, sems
):
    nz = first_ref.shape[0]
    lane = iota((8, 128), 1)
    sub = iota((8, 128), 0)
    is_even = sub % 2 == 0

    copies = [
        pltpu.make_async_copy(
            done.at[:, pl.ds(2 * c, 2), :], out_ref.at[c, :, pl.ds(0, 2), :], sems.at[c]
        )
        for c in range(4)
    ]

    @pl.when(lax.axis_index("gx") == 0)
    def _():
        inlet[...] = jnp.zeros_like(inlet)
        for c in range(4):
            for z in range(nz):
                inlet[z, 2 * c : 2 * c + 1, :] = in_ref[c, z : z + 1, :]
        for half in range(2):
            old = corner_ref[half]
            push = upwind(old[1:2])[0]
            for c in range(4):
                msg = in_ref[c, nz + half : nz + half + 1, :]
                side = jnp.where(
                    lane[0:1] % 4 == 1, pltpu.roll(msg, 1, 1), pltpu.roll(msg, 127, 1)
                )
                wide[half, 2 * c : 2 * c + 1, :] = old[2 * c : 2 * c + 1] + push * side
                wide[half, 2 * c + 1 : 2 * c + 2, :] = jnp.zeros((1, 128), F32)

        def first(group, carry):
            for i in range(UNROLL):
                z = group * UNROLL + i
                push = upwind(sb_ref[z, 0:1, :])[0]
                new[z] = first_ref[z] + jnp.where(is_even, push * inlet[z], 0.0)
            return carry

        lax.fori_loop(0, nz // UNROLL, first, 0)

        def second(group, carry):
            for i in range(UNROLL):
                z = group * UNROLL + i
                below = jnp.maximum(z - 1, 0)
                above = jnp.minimum(z + 1, nz - 1)
                half = z // 32
                shift = (255 - 4 * (z - 32 * half)) % 128
                cur = new[z]
                east = pltpu.roll(cur, 7, 0)
                corner = pltpu.roll(wide[half], shift, 1)
                south = jnp.where(lane == 0, corner, pltpu.roll(cur, 1, 1))
                north = jnp.where(lane == 127, corner, pltpu.roll(cur, 127, 1))
                c = coefs(cur[0:1], cur[2:3], cur[4:5])
                zero = mix(c, cur, inlet[z], east, south, north, new[below], new[above])
                zero = zero + jnp.where(sub == 4, (DT * BUOY) * cur[6:7], 0.0)
                delta = pltpu.roll(cur - first_ref[z], 1, 0)
                one = last_ref[z] + upwind(cur[1:2])[0] * delta
                done[z] = jnp.where(is_even, zero, one)
            return carry

        lax.fori_loop(0, nz // UNROLL, second, 0)
        for copy in copies:
            copy.start()
        for copy in copies:
            copy.wait()


VMEM = pl.BlockSpec(memory_space=pltpu.VMEM)
ANY = pl.BlockSpec(memory_space=pl.ANY)
SMEM = pl.BlockSpec(memory_space=pltpu.SMEM)
HBM = pl.BlockSpec(memory_space=pltpu.HBM)


def call(kernel, out, scratch=(), aliases=None, ins=None, outs=None, flops=1 << 20):
    specs = {}
    if ins is not None:
        specs["in_specs"] = ins
    if outs is not None:
        specs["out_specs"] = outs
    return pl.pallas_call(
        kernel,
        out_shape=out,
        scratch_shapes=scratch,
        input_output_aliases=aliases or {},
        compiler_params=pltpu.CompilerParams(vmem_limit_bytes=24 << 20),
        cost_estimate=pl.CostEstimate(flops=flops, bytes_accessed=1 << 20, transcendentals=0),
        **specs,
    )


def row_of(place):
    return {3: 6, 6: 3}.get(place, place)


def send_inlet(msg, after, count_x, count_y):
    heard = {}
    for m in (2, 3, 1, 0):
        moves = [
            (row_of(GROUP * m + j % GROUP) * count_y + j, j)
            for j in range(count_y)
            if GROUP * m + j % GROUP
        ]
        if m == 0:
            sent, *_ = lax.optimization_barrier((msg, *after))
        else:
            sent = msg
        heard[m] = lax.ppermute(sent, ("gx", "gy"), moves)
    return [heard[m] for m in range(4)]


def share_inlet(msg, heard, code, count_y):
    heard[0] = jnp.where(lax.axis_index("gy") % GROUP == 0, msg, heard[0])

    def pick(k):
        out = heard[0]
        for m in range(1, len(heard)):
            out = jnp.where(code[k] & 7 == m, heard[m], out)
        return out

    core = lax.ppermute(
        jnp.concatenate([pick(1), pick(3)]), "gy", [(j, j ^ 1) for j in range(count_y)]
    )
    mine = jnp.where(code[0] & 8 != 0, pick(0), core[0:4])
    theirs = jnp.where(code[2] & 8 != 0, pick(2), core[4:8])
    other = lax.ppermute(theirs, "gy", [(j, j ^ 2) for j in range(count_y)])
    return jnp.where(code[0] & 16 != 0, mine, other)


def body(flow_state, inflow, footprint, block_map):
    levels = flow_state.shape[1]
    count_x = lax.axis_size("gx")
    count_y = lax.axis_size("gy")
    turbines = footprint.shape[0]
    shape = lambda *s: jax.ShapeDtypeStruct(s, F32)
    x_pack = shape(levels, 8, 128)
    y_pack = shape(2, 4, 24, 128)

    send_a, send_b = call(
        pack_x_kernel, (x_pack, x_pack), [pltpu.SemaphoreType.DMA((4, 2))], ins=[HBM], outs=[VMEM] * 2
    )(flow_state)
    recv_a = lax.ppermute(send_a, "gx", pairs(count_x, False))
    recv_b = lax.ppermute(send_b, ("gx", "gy"), pairs_inside(count_x, count_y))

    late, _ = lax.optimization_barrier((footprint, send_a))
    fp = jnp.pad(late.T, ((0, 5), (0, 128 - turbines)), constant_values=FAR)
    lap = jnp.ones((128, 128), F32)
    for i, extent in enumerate((DISK_X, DISK_Y, DISK_Z)):
        lap = lap * jnp.maximum(extent - jnp.abs(fp[i][:, None] - fp[i][None, :]), 0).astype(F32)
    live = jnp.arange(128) < turbines
    lap = jnp.where(live[:, None] & live[None, :], lap, 0.0)

    own = call(pack_y_kernel, y_pack, flops=PACK_COST)(flow_state, send_a)
    msg, code = call(
        pack_inlet_kernel,
        (shape(4, levels + 8, 128), jax.ShapeDtypeStruct((GROUP, levels + 8, 128), jnp.int32)),
        ins=[SMEM, VMEM, VMEM],
    )(block_map, inflow, own)
    base, disks, sums = call(
        base_kernel,
        (
            shape(*flow_state.shape),
            jax.ShapeDtypeStruct((levels, 16, 128), jnp.bfloat16),
            shape(8, 128),
        ),
        [pltpu.VMEM((2, levels, 16, 128), F32)],
        flops=TILE_COST,
    )(flow_state, fp)
    heard = send_inlet(msg, (recv_b, sums), count_x, count_y)

    own, near, west, east = call(
        rim_kernel, (y_pack, x_pack, x_pack, x_pack), [pltpu.VMEM((levels, 8, 128), F32)] * 3
    )(send_a, send_b, recv_a, recv_b, fp, sums, own)
    side_a = lax.ppermute(own, "gy", pairs(count_y, False))
    side_b = lax.ppermute(own, "gy", pairs(count_y, True))
    *heard, _ = lax.optimization_barrier((*heard, side_b))
    inlet = share_inlet(msg, list(heard), code, count_y)
    out, first, corner, last = call(
        steps_kernel,
        (shape(*flow_state.shape), x_pack, shape(2, 8, 128), x_pack),
        [
            pltpu.VMEM(flow_state.shape, F32),
            pltpu.VMEM(flow_state.shape, F32),
            pltpu.VMEM((2, levels, 16, 128), F32),
            pltpu.VMEM((2, levels, 128), F32),
            pltpu.VMEM((levels, 8, 128), F32),
            pltpu.VMEM((2, 2, 4, 16, 128), F32),
            pltpu.VMEM((2, 8, 128), F32),
            pltpu.SemaphoreType.DMA((levels // UNROLL,)),
        ],
        outs=[ANY, VMEM, VMEM, VMEM],
        flops=STEPS_COST,
    )(flow_state, base, disks, near, west, east, own, side_a, side_b, fp, lap)
    return call(
        fix_kernel,
        shape(*flow_state.shape),
        [
            pltpu.VMEM((levels, 8, 128), F32),
            pltpu.VMEM((levels, 8, 128), F32),
            pltpu.VMEM((2, 8, 128), F32),
            pltpu.VMEM((levels, 8, 128), F32),
            pltpu.SemaphoreType.DMA((4,)),
        ],
        aliases={0: 0},
        ins=[ANY, VMEM, VMEM, VMEM, VMEM, VMEM],
        outs=ANY,
    )(out, inlet, send_b, first, corner, last)


def solution(mesh):
    placed = (P(None, None, "gx", "gy"), P(None, None, "gx"), P(), P())
    return jax.shard_map(
        body, mesh=mesh, in_specs=placed, out_specs=P(None, None, "gx", "gy"), check_vma=False
    )
```

```python
import jax
import jax.numpy as jnp
from jax import lax
from jax.experimental import pallas as pl
from jax.experimental.pallas import tpu as pltpu
from jax.sharding import PartitionSpec as P

DISK_X = 2
DISK_Y = 24
DISK_Z = 24
CELLS = float(DISK_X * DISK_Y * DISK_Z)

DT = 0.15
VISC = 0.3
BUOY = 0.3
GAIN = 2.0
BASE = DT * VISC
FAR = -100000
F32 = jnp.float32
UNROLL = 16
CHUNK = 8
GROUP = 4
TILE_COST = 1 << 20
PACK_COST = 1 << 33
STEPS_COST = 1 << 32


def pairs(n, odd):
    if not odd:
        return [(i, i ^ 1) for i in range(n)]
    return [(i, (i + 1) % n if i % 2 else (i - 1) % n) for i in range(n)]


def pairs_inside(nx, ny):
    out = []
    for i in range(nx):
        for j in range(ny):
            if i in (0, nx - 1):
                to = (i, j ^ 1)
            else:
                to = (i + 1 if i % 2 else i - 1, j)
            out.append((i * ny + j, to[0] * ny + to[1]))
    return out


def upwind(vel):
    scaled = DT * vel
    return jnp.maximum(scaled, 0.0) + BASE, BASE - jnp.minimum(scaled, 0.0)


def coefs(u, v, w):
    cw, ce = upwind(u)
    cs, cn = upwind(v)
    cb, ca = upwind(w)
    c0 = 1.0 - ((cw + ce) + (cs + cn) + (cb + ca))
    return c0, cw, ce, cs, cn, cb, ca


def mix(c, f, w, e, s, n, b, a):
    return c[0] * f + c[1] * w + c[2] * e + c[3] * s + c[4] * n + c[5] * b + c[6] * a


def dot_nt(a, m):
    high = a.astype(jnp.bfloat16)
    low = (a - high.astype(F32)).astype(jnp.bfloat16)
    dims = (((1,), (1,)), ((), ()))
    return lax.dot_general(high, m, dims, preferred_element_type=F32) + lax.dot_general(
        low, m, dims, preferred_element_type=F32
    )


def dot_nn(a, m):
    high = a.astype(jnp.bfloat16)
    low = (a - high.astype(F32)).astype(jnp.bfloat16)
    return jnp.dot(high, m, preferred_element_type=F32) + jnp.dot(
        low, m, preferred_element_type=F32
    )


def iota(shape, dim):
    return lax.broadcasted_iota(jnp.int32, shape, dim)


def within(cells, start, extent):
    return ((cells >= start) & (cells < start + extent)).astype(F32)


def span_mask(fp, first, count):
    return within(first + iota((count, 128), 0), fp[1:2], DISK_Y).astype(jnp.bfloat16)


def pack_x_kernel(f_ref, a_ref, b_ref, sems):
    even = lax.axis_index("gx") % 2 == 0
    first_a = jnp.where(even, 14, 0)
    first_b = jnp.where(even, 0, 14)
    copies = []
    for c in range(4):
        for i, (first, ref) in enumerate(((first_a, a_ref), (first_b, b_ref))):
            copies.append(
                pltpu.make_async_copy(
                    f_ref.at[c, :, pl.ds(first, 2), :],
                    ref.at[:, pl.ds(2 * c, 2), :],
                    sems.at[c, i],
                )
            )
    for copy in copies:
        copy.start()
    for copy in copies:
        copy.wait()


def pack_inlet_kernel(map_ref, in_ref, after_ref, msg_ref, code_ref):
    nz = in_ref.shape[1]
    lane = iota((1, 128), 1)
    for c in range(4):
        msg_ref[c, 0:nz, :] = in_ref[c]
        msg_ref[c, nz : nz + 8, :] = jnp.zeros((8, 128), F32)
        for half in range(2):
            packed = jnp.zeros((1, 128), F32)
            for z in range(half * 32, min(nz, half * 32 + 32)):
                at = z - half * 32
                moved = pltpu.roll(in_ref[c, z : z + 1, :], (4 * at + 1) % 128, 1)
                packed = jnp.where(lane // 4 == at, moved, packed)
            msg_ref[c, nz + half : nz + half + 1, :] = packed

    tile_y = lax.axis_index("gy")
    count = lax.axis_size("gy")
    place = tile_y % GROUP
    level = iota((nz + 8, 128), 0)
    first = iota((nz + 8, 128), 1) % 4 == 0
    for k in range(GROUP):
        column = tile_y // GROUP * GROUP + (place ^ k)
        own = map_ref[column]
        left = map_ref[(column + count - 1) % count]
        right = map_ref[(column + 1) % count]
        source = jnp.where(level < nz, own, jnp.where(first, left, right))
        source = jnp.where(source == 3, 6, jnp.where(source == 6, 3, source))
        code = source // GROUP
        code = code + jnp.where(source % GROUP == place, 8, 0)
        code_ref[k] = code + jnp.where(source % GROUP // 2 == place // 2, 16, 0)


def pack_y_kernel(f_ref, after_ref, p_ref):
    nz = f_ref.shape[1]
    lane = iota((16, 128), 1)
    p_ref[...] = jnp.zeros_like(p_ref)
    for half in range(2):
        lo, hi = half * 32, min(nz, half * 32 + 32)

        def one(z, packed):
            here = lane // 4 == z - lo
            shift = (2 + 4 * (z - lo)) % 128
            return tuple(
                jnp.where(here, pltpu.roll(f_ref[i, z], shift, 1), packed[i]) for i in range(4)
            )

        zero = jnp.zeros((16, 128), F32)
        packed = lax.fori_loop(lo, hi, one, (zero,) * 4, unroll=UNROLL)
        for i in range(4):
            p_ref[half, i, 0:16, :] = packed[i]


def base_kernel(f_ref, fp_ref, base_ref, disks_ref, sums_ref, rows_ref):
    nz = f_ref.shape[1]
    first_x = lax.axis_index("gx") * 16
    first_y = lax.axis_index("gy") * 128
    fp = fp_ref[...]
    lane = iota((16, 128), 1)
    sub = iota((16, 128), 0)
    mask_x = within(first_x + sub, fp[0:1], DISK_X)

    def one(z, carry):
        below = jnp.maximum(z - 1, 0)
        above = jnp.minimum(z + 1, nz - 1)
        cur = [f_ref[c, z] for c in range(4)]
        c = coefs(cur[0], cur[1], cur[2])
        cw = jnp.where(sub == 0, 0.0, c[1])
        ce = jnp.where(sub == 15, 0.0, c[2])
        cs = jnp.where(lane == 0, 0.0, c[3])
        cn = jnp.where(lane == 127, 0.0, c[4])
        c = (c[0], cw, ce, cs, cn, c[5], c[6])
        for i in range(4):
            f = cur[i]
            new = mix(
                c,
                f,
                pltpu.roll(f, 1, 0),
                pltpu.roll(f, 15, 0),
                pltpu.roll(f, 1, 1),
                pltpu.roll(f, 127, 1),
                f_ref[i, below],
                f_ref[i, above],
            )
            if i == 2:
                new = new + (DT * BUOY) * cur[3]
            base_ref[i, z] = new
        disks_ref[z] = (mask_x * within(z, fp[2:3], DISK_Z)).astype(jnp.bfloat16)
        return carry

    lax.fori_loop(0, nz, one, 0, unroll=UNROLL)
    span = span_mask(fp, first_y, 128)
    rows_ref[0] = dot_nn(f_ref[0].reshape(nz * 16, 128), span).reshape(nz, 16, 128)
    rows_ref[1] = dot_nn(base_ref[0].reshape(nz * 16, 128), span).reshape(nz, 16, 128)

    def add(z, acc):
        mask = within(z, fp[2:3], DISK_Z)
        return acc[0] + rows_ref[0, z] * mask, acc[1] + rows_ref[1, z] * mask

    zero = jnp.zeros((16, 128), F32)
    acc = lax.fori_loop(0, nz, add, (zero, zero), unroll=UNROLL)
    sums_ref[0:1, :] = jnp.sum(acc[0] * mask_x, axis=0, keepdims=True)
    sums_ref[1:2, :] = jnp.sum(acc[1] * mask_x, axis=0, keepdims=True)
    sums_ref[2:8, :] = jnp.zeros((6, 128), F32)


def rim_kernel(
    sa_ref,
    sb_ref,
    ra_ref,
    rb_ref,
    fp_ref,
    sums_ref,
    p_in,
    p_ref,
    cur_ref,
    west_ref,
    east_ref,
    hl_ref,
    hh_ref,
    rows_ref,
):
    nz = hl_ref.shape[0]
    tile_x = lax.axis_index("gx")
    last_x = lax.axis_size("gx") - 1
    even = tile_x % 2 == 0
    first_x = tile_x * 16
    first_y = lax.axis_index("gy") * 128
    fp = fp_ref[...]
    lane = iota((8, 128), 1)
    sub = iota((8, 128), 0)

    @pl.when(even)
    def _():
        hl_ref[...] = rb_ref[...]
        hh_ref[...] = ra_ref[...]

    @pl.when(jnp.logical_not(even))
    def _():
        hl_ref[...] = ra_ref[...]
        hh_ref[...] = rb_ref[...]

    @pl.when(tile_x == 0)
    def _():
        hl_ref[...] = jnp.zeros_like(hl_ref)

    @pl.when(tile_x == last_x)
    def _():
        for z in range(nz):
            hh_ref[z] = pltpu.roll(sb_ref[z], 7, 0)

    def row(x, i):
        return x[i : i + 1]

    for half in range(2):
        lo, hi = half * 32, min(nz, half * 32 + 32)

        def one(z, packed):
            below = jnp.maximum(z - 1, 0)
            above = jnp.minimum(z + 1, nz - 1)
            own_a, own_b = sa_ref[z], sb_ref[z]
            own_low = jnp.where(even, own_b, own_a)
            own_high = jnp.where(even, own_a, own_b)
            low, high = hl_ref[z], hh_ref[z]
            u_low = jnp.where(sub == 0, row(low, 1), row(high, 0))
            v_low = jnp.where(sub == 0, row(low, 3), row(high, 2))
            w_low = jnp.where(sub == 0, row(low, 5), row(high, 4))
            west = jnp.where(sub == 0, row(low, 0), row(own_high, 1))
            east = jnp.where(sub == 0, row(own_low, 0), row(high, 1))
            down = jnp.where(sub == 0, row(hl_ref[below], 1), row(hh_ref[below], 0))
            up = jnp.where(sub == 0, row(hl_ref[above], 1), row(hh_ref[above], 0))
            south = jnp.where(lane == 0, 0.0, pltpu.roll(u_low, 1, 1))
            north = jnp.where(lane == 127, 0.0, pltpu.roll(u_low, 127, 1))
            ring = mix(coefs(u_low, v_low, w_low), u_low, west, east, south, north, down, up)
            into_low = upwind(row(own_low, 0))[0] * row(low, 1)
            into_high = upwind(row(own_high, 1))[1] * row(high, 0)
            both = jnp.where(sub == 2, into_low, jnp.where(sub == 3, into_high, ring))
            both = jnp.where(sub == 4, row(low, 0), both)
            both = jnp.where(sub == 5, row(low, 1), both)
            both = jnp.where(sub == 6, row(high, 0), both)
            both = jnp.where(sub == 7, row(high, 1), both)
            rows_ref[z] = both
            odd = sub % 2 == 1
            cur_ref[z] = jnp.where(odd, low, high)
            west_ref[z] = jnp.where(odd, pltpu.roll(low, 1, 0), pltpu.roll(own_high, 7, 0))
            east_ref[z] = jnp.where(odd, pltpu.roll(own_low, 1, 0), pltpu.roll(high, 7, 0))
            here = lane // 4 == z - lo
            shift = (2 + 4 * (z - lo)) % 128
            return (
                jnp.where(here, pltpu.roll(low, shift, 1), packed[0]),
                jnp.where(here, pltpu.roll(high, shift, 1), packed[1]),
            )

        zero = jnp.zeros((8, 128), F32)
        packed = lax.fori_loop(lo, hi, one, (zero, zero), unroll=UNROLL)
        for c in range(4):
            p_ref[half, c, 0:16, :] = p_in[half, c, 0:16, :]
            p_ref[half, c, 16:17, :] = row(packed[0], 2 * c + 1)
            p_ref[half, c, 17:18, :] = row(packed[1], 2 * c)
            p_ref[half, c, 18:24, :] = jnp.zeros((6, 128), F32)

    span = span_mask(fp, first_y, 128)
    rows_ref[...] = dot_nn(rows_ref[...].reshape(nz * 8, 128), span).reshape(nz, 8, 128)

    def add(z, acc):
        return acc + rows_ref[z] * within(z, fp[2:3], DISK_Z)

    acc = lax.fori_loop(0, nz, add, jnp.zeros((8, 128), F32), unroll=UNROLL)
    column = jnp.where(sub == 0, -1, 16)
    column = jnp.where(sub == 2, 0, jnp.where(sub == 3, 15, column))
    column = jnp.where(sub >= 4, jnp.where(sub < 6, sub - 6, sub + 10), column)
    acc = acc * within(first_x + column, fp[0:1], DISK_X)
    p_ref[0, 0, 18:19, :] = sums_ref[0:1, :] + jnp.sum(acc[4:8], axis=0, keepdims=True)
    p_ref[1, 0, 18:19, :] = sums_ref[1:2, :] + jnp.sum(acc[0:4], axis=0, keepdims=True)


def steps_kernel(
    f_ref,
    base_ref,
    disks_ref,
    cur_ref,
    west_ref,
    east_ref,
    p_ref,
    pa_ref,
    pb_ref,
    fp_ref,
    lap_ref,
    out_ref,
    first_ref,
    first_corner_ref,
    last_ref,
    mid_ref,
    new_ref,
    force_ref,
    rim_force_ref,
    ring_ref,
    edge_ref,
    corner_ref,
    sems,
):
    nz = f_ref.shape[1]
    tile_x = lax.axis_index("gx")
    tile_y = lax.axis_index("gy")
    last_x = lax.axis_size("gx") - 1
    all_y = lax.axis_size("gy") * 128
    even_y = tile_y % 2 == 0
    first_x = tile_x * 16
    first_y = tile_y * 128
    fp = fp_ref[...]
    fx, fy, fz = fp[0:1], fp[1:2], fp[2:3]
    lane = iota((16, 128), 1)
    sub = iota((16, 128), 0)

    def pick(half, c):
        a, b = pa_ref[half, c], pb_ref[half, c]
        return jnp.where(even_y, b, a), jnp.where(even_y, a, b)

    k24 = iota((24, 128), 1) % 4
    left_cols, right_cols = [], []
    for c in range(4):
        lefts, rights = [], []
        for half in range(2):
            left, right = pick(half, c)
            own = p_ref[half, c]
            lefts.append(jnp.where(k24 < 2, left, own))
            rights.append(jnp.where(k24 < 2, own, right))
            edge = jnp.where(k24 == 1, left, pltpu.roll(right, 126, 1))
            edge_ref[0, half, c] = edge[0:16]
            corner_ref[half, 2 * c + 1 : 2 * c + 2, :] = edge[16:17]
            corner_ref[half, 2 * c : 2 * c + 1, :] = edge[17:18]
        left_cols.append(jnp.concatenate(lefts, axis=1))
        right_cols.append(jnp.concatenate(rights, axis=1))
    def total(half):
        left, right = pick(half, 0)
        return p_ref[half, 0, 18:19, :] + left[18:19] + right[18:19]

    def thrust_of(sums):
        speed = sums * (1.0 / CELLS)
        return -GAIN * DT * speed * jnp.abs(speed)

    thrust1 = thrust_of(total(0))
    at = iota((256, 128), 0)
    level = at // 4
    k_at = at % 4
    mask_level = within(level, fz, DISK_Z) * (level < nz).astype(F32)
    y_left = jnp.where(k_at == 1, jnp.where(first_y == 0, all_y - 1, first_y - 1), first_y)
    y_right = jnp.where(
        k_at == 1, first_y + 127, jnp.where(first_y + 128 == all_y, 0, first_y + 128)
    )
    middle = ((k_at == 1) | (k_at == 2)).astype(F32)
    mask_left = mask_level * within(y_left, fy, DISK_Y) * middle
    mask_right = mask_level * within(y_right, fy, DISK_Y) * middle
    k256 = iota((24, 256), 1) % 4

    def facing(cols, mask):
        u, v = cols[0], cols[1]
        cs, cn = upwind(v)
        term = jnp.where(k256 == 1, cn * pltpu.roll(u, 255, 1), cs * pltpu.roll(u, 1, 1))
        term = jnp.concatenate([term, jnp.zeros((8, 256), F32)], axis=0)
        return dot_nn(term, mask.astype(jnp.bfloat16))

    faces = facing(left_cols, mask_left) + facing(right_cols, mask_right)
    sub32 = iota((32, 128), 0)
    column = jnp.where(sub32 == 16, -1, jnp.where(sub32 == 17, 16, sub32))
    mask_x32 = within(first_x + column, fx, DISK_X) * (sub32 < 18).astype(F32)
    faces = jnp.sum(faces * mask_x32, axis=0, keepdims=True)
    pushed = jnp.dot(
        jnp.broadcast_to(thrust1, (8, 128)),
        lap_ref[...],
        precision=lax.Precision.HIGHEST,
        preferred_element_type=F32,
    )
    thrust2 = thrust_of(total(1) + faces + pushed[0:1])

    span = within(first_y + iota((128, 128), 0), fy, DISK_Y)
    disks = disks_ref[...].reshape(nz * 16, 128)

    def dot_disks(mask, weights):
        high = weights.astype(jnp.bfloat16)
        low = (weights - high.astype(F32)).astype(jnp.bfloat16)
        dims = (((1,), (1,)), ((), ()))
        return lax.dot_general(
            mask, high, dims, preferred_element_type=F32
        ) + lax.dot_general(mask, low, dims, preferred_element_type=F32)

    force_ref[0] = dot_disks(disks, span * thrust1).reshape(nz, 16, 128)
    force_ref[1] = dot_disks(disks, span * thrust2).reshape(nz, 16, 128)
    levels = within(iota((nz, 128), 0), fz, DISK_Z).astype(jnp.bfloat16)
    for side, x in ((0, 16), (1, -1)):
        weights = span * (thrust1 * within(first_x + x, fx, DISK_X))
        rim_force_ref[side] = dot_disks(levels, weights)
    by_x1 = within(first_x + sub, fx, DISK_X) * thrust1
    y_cols = jnp.where(k_at == 1, y_left, y_right)
    mask_cols = mask_level * within(y_cols, fy, DISK_Y) * middle
    force_cols = dot_nt(by_x1, mask_cols.astype(jnp.bfloat16))

    lane256 = iota((16, 256), 1)
    sub256 = iota((16, 256), 0)

    def rim_cols(cols):
        cur = [x[0:16] for x in cols]
        c = coefs(cur[0], cur[1], cur[2])
        new = []
        for i in range(4):
            f = cur[i]
            west = jnp.where(sub256 == 0, cols[i][16:17], pltpu.roll(f, 1, 0))
            east = jnp.where(sub256 == 15, cols[i][17:18], pltpu.roll(f, 15, 0))
            south = pltpu.roll(f, 1, 1)
            north = pltpu.roll(f, 255, 1)
            down = jnp.where(lane256 < 4, f, pltpu.roll(f, 4, 1))
            up = jnp.where(lane256 >= 4 * nz - 4, f, pltpu.roll(f, 252, 1))
            new.append(mix(c, f, west, east, south, north, down, up))
        new[0] = new[0] + force_cols
        new[2] = new[2] + (DT * BUOY) * cur[3]
        return new

    left_new, right_new = rim_cols(left_cols), rim_cols(right_cols)
    for c in range(4):
        edge = jnp.where(lane256 % 4 == 1, left_new[c], pltpu.roll(right_new[c], 254, 1))
        edge_ref[1, 0, c] = edge[:, 0:128]
        edge_ref[1, 1, c] = edge[:, 128:256]

    lane8 = iota((8, 128), 1)
    sub8 = iota((8, 128), 0)
    odd = sub8 % 2 == 1

    def rim_rows(z, carry):
        below = jnp.maximum(z - 1, 0)
        above = jnp.minimum(z + 1, nz - 1)
        half = z // 32
        shift = (255 - 4 * (z - 32 * half)) % 128
        cur = cur_ref[z]
        corner = pltpu.roll(corner_ref[half], shift, 1)
        south = jnp.where(lane8 == 0, corner, pltpu.roll(cur, 1, 1))
        north = jnp.where(lane8 == 127, corner, pltpu.roll(cur, 127, 1))
        vel = [jnp.where(odd, cur[2 * i + 1 : 2 * i + 2], cur[2 * i : 2 * i + 1]) for i in range(4)]
        c = coefs(vel[0], vel[1], vel[2])
        new = mix(c, cur, west_ref[z], east_ref[z], south, north, cur_ref[below], cur_ref[above])
        new = new + jnp.where(sub8 // 2 == 2, (DT * BUOY) * vel[3], 0.0)
        new = new + jnp.where(sub8 == 0, rim_force_ref[0, pl.ds(z, 1), :], 0.0)
        new = new + jnp.where(sub8 == 1, rim_force_ref[1, pl.ds(z, 1), :], 0.0)
        ring_ref[z] = jnp.where(odd & (tile_x == 0), cur, new)
        return carry

    lax.fori_loop(0, nz, rim_rows, 0, unroll=UNROLL)

    def first_step(group, carry):
        for j in range(UNROLL):
            z = group * UNROLL + j
            half = z // 32
            shift = (255 - 4 * (z - 32 * half)) % 128
            near = cur_ref[z]
            cw, ce = upwind(f_ref[0, z])
            cs, cn = upwind(f_ref[1, z])
            along_x = jnp.where(sub == 0, cw, jnp.where(sub == 15, ce, 0.0))
            along_y = jnp.where(lane == 0, cs, jnp.where(lane == 127, cn, 0.0))
            for i in range(4):
                beside = jnp.where(sub < 8, near[2 * i + 1 : 2 * i + 2], near[2 * i : 2 * i + 1])
                edge = pltpu.roll(edge_ref[0, half, i], shift, 1)
                new = base_ref[i, z] + along_x * beside + along_y * edge
                if i == 0:
                    new = new + force_ref[0, z]
                mid_ref[i, z] = new
        return carry

    def level(z):
        below = jnp.maximum(z - 1, 0)
        above = jnp.minimum(z + 1, nz - 1)
        half = z // 32
        shift = (255 - 4 * (z - 32 * half)) % 128
        cur = [mid_ref[c, z] for c in range(4)]
        ring = ring_ref[z]
        c = coefs(cur[0], cur[1], cur[2])
        for i in range(4):
            f = cur[i]
            west = jnp.where(sub == 0, ring[2 * i + 1 : 2 * i + 2], pltpu.roll(f, 1, 0))
            outside = jnp.where(tile_x == last_x, f[15:16], ring[2 * i : 2 * i + 1])
            east = jnp.where(sub == 15, outside, pltpu.roll(f, 15, 0))
            edge = pltpu.roll(edge_ref[1, half, i], shift, 1)
            south = jnp.where(lane == 0, edge, pltpu.roll(f, 1, 1))
            north = jnp.where(lane == 127, edge, pltpu.roll(f, 127, 1))
            new = mix(c, f, west, east, south, north, mid_ref[i, below], mid_ref[i, above])
            if i == 0:
                new = new + force_ref[1, z]
            if i == 2:
                new = new + (DT * BUOY) * cur[3]
            new_ref[i, z] = new

    def send(chunk):
        part = pl.ds(chunk * CHUNK, CHUNK)
        return pltpu.make_async_copy(new_ref.at[:, part], out_ref.at[:, part], sems.at[chunk])

    def second_step(group, carry):
        for i in range(UNROLL):
            z = group * UNROLL + i
            level(z)
            if i % CHUNK == CHUNK - 1:
                send(group * (UNROLL // CHUNK) + i // CHUNK).start()
        return carry

    lax.fori_loop(0, nz // UNROLL, first_step, 0)
    lax.fori_loop(0, nz // UNROLL, second_step, 0)

    @pl.when(tile_x == 0)
    def _():
        for c in range(4):
            first_ref[:, 2 * c : 2 * c + 2, :] = mid_ref[c, :, 0:2, :]
            last_ref[:, 2 * c : 2 * c + 2, :] = new_ref[c, :, 0:2, :]
            for half in range(2):
                first_corner_ref[half, 2 * c : 2 * c + 1, :] = edge_ref[1, half, c, 0:1, :]
                first_corner_ref[half, 2 * c + 1 : 2 * c + 2, :] = edge_ref[0, half, c, 0:1, :]

    for chunk in range(nz // CHUNK):
        send(chunk).wait()


def fix_kernel(
    out_in, in_ref, sb_ref, first_ref, corner_ref, last_ref, out_ref, inlet, new, wide, done, sems
):
    nz = first_ref.shape[0]
    lane = iota((8, 128), 1)
    sub = iota((8, 128), 0)
    is_even = sub % 2 == 0


    def send(group):
        part = pl.ds(group * UNROLL, UNROLL)
        return [
            pltpu.make_async_copy(
                done.at[part, pl.ds(2 * c, 2), :], out_ref.at[c, part, pl.ds(0, 2), :], sems.at[group, c]
            )
            for c in range(4)
        ]

    @pl.when(lax.axis_index("gx") == 0)
    def _():
        inlet[...] = jnp.zeros_like(inlet)
        for c in range(4):
            for z in range(nz):
                inlet[z, 2 * c : 2 * c + 1, :] = in_ref[c, z : z + 1, :]
        for half in range(2):
            old = corner_ref[half]
            push = upwind(old[1:2])[0]
            for c in range(4):
                msg = in_ref[c, nz + half : nz + half + 1, :]
                side = jnp.where(
                    lane[0:1] % 4 == 1, pltpu.roll(msg, 1, 1), pltpu.roll(msg, 127, 1)
                )
                wide[half, 2 * c : 2 * c + 1, :] = old[2 * c : 2 * c + 1] + push * side
                wide[half, 2 * c + 1 : 2 * c + 2, :] = jnp.zeros((1, 128), F32)

        def first(group, carry):
            for i in range(UNROLL):
                z = group * UNROLL + i
                push = upwind(sb_ref[z, 0:1, :])[0]
                new[z] = first_ref[z] + jnp.where(is_even, push * inlet[z], 0.0)
            return carry

        lax.fori_loop(0, nz // UNROLL, first, 0)

        def second(group, carry):
            for i in range(UNROLL):
                z = group * UNROLL + i
                below = jnp.maximum(z - 1, 0)
                above = jnp.minimum(z + 1, nz - 1)
                half = z // 32
                shift = (255 - 4 * (z - 32 * half)) % 128
                cur = new[z]
                east = pltpu.roll(cur, 7, 0)
                corner = pltpu.roll(wide[half], shift, 1)
                south = jnp.where(lane == 0, corner, pltpu.roll(cur, 1, 1))
                north = jnp.where(lane == 127, corner, pltpu.roll(cur, 127, 1))
                c = coefs(cur[0:1], cur[2:3], cur[4:5])
                zero = mix(c, cur, inlet[z], east, south, north, new[below], new[above])
                zero = zero + jnp.where(sub == 4, (DT * BUOY) * cur[6:7], 0.0)
                delta = pltpu.roll(cur - first_ref[z], 1, 0)
                one = last_ref[z] + upwind(cur[1:2])[0] * delta
                done[z] = jnp.where(is_even, zero, one)
            for copy in send(group):
                copy.start()
            return carry

        lax.fori_loop(0, nz // UNROLL, second, 0)
        for group in range(nz // UNROLL):
            for copy in send(group):
                copy.wait()


VMEM = pl.BlockSpec(memory_space=pltpu.VMEM)
ANY = pl.BlockSpec(memory_space=pl.ANY)
SMEM = pl.BlockSpec(memory_space=pltpu.SMEM)
HBM = pl.BlockSpec(memory_space=pltpu.HBM)


def call(kernel, out, scratch=(), aliases=None, ins=None, outs=None, flops=1 << 20):
    specs = {}
    if ins is not None:
        specs["in_specs"] = ins
    if outs is not None:
        specs["out_specs"] = outs
    return pl.pallas_call(
        kernel,
        out_shape=out,
        scratch_shapes=scratch,
        input_output_aliases=aliases or {},
        compiler_params=pltpu.CompilerParams(vmem_limit_bytes=24 << 20),
        cost_estimate=pl.CostEstimate(flops=flops, bytes_accessed=1 << 20, transcendentals=0),
        **specs,
    )


def row_of(place):
    return {3: 6, 6: 3}.get(place, place)


def send_inlet(msg, after, count_x, count_y):
    heard = {}
    for m in (2, 3, 1, 0):
        moves = [
            (row_of(GROUP * m + j % GROUP) * count_y + j, j)
            for j in range(count_y)
            if GROUP * m + j % GROUP
        ]
        if m == 0:
            sent, *_ = lax.optimization_barrier((msg, *after))
        else:
            sent = msg
        heard[m] = lax.ppermute(sent, ("gx", "gy"), moves)
    return [heard[m] for m in range(4)]


def share_inlet(msg, heard, code, count_y):
    heard[0] = jnp.where(lax.axis_index("gy") % GROUP == 0, msg, heard[0])

    def pick(k):
        out = heard[0]
        for m in range(1, len(heard)):
            out = jnp.where(code[k] & 7 == m, heard[m], out)
        return out

    core = lax.ppermute(
        jnp.concatenate([pick(1), pick(3)]), "gy", [(j, j ^ 1) for j in range(count_y)]
    )
    mine = jnp.where(code[0] & 8 != 0, pick(0), core[0:4])
    theirs = jnp.where(code[2] & 8 != 0, pick(2), core[4:8])
    other = lax.ppermute(theirs, "gy", [(j, j ^ 2) for j in range(count_y)])
    return jnp.where(code[0] & 16 != 0, mine, other)


def body(flow_state, inflow, footprint, block_map):
    levels = flow_state.shape[1]
    count_x = lax.axis_size("gx")
    count_y = lax.axis_size("gy")
    turbines = footprint.shape[0]
    shape = lambda *s: jax.ShapeDtypeStruct(s, F32)
    x_pack = shape(levels, 8, 128)
    y_pack = shape(2, 4, 24, 128)

    send_a, send_b = call(
        pack_x_kernel, (x_pack, x_pack), [pltpu.SemaphoreType.DMA((4, 2))], ins=[HBM], outs=[VMEM] * 2
    )(flow_state)
    recv_a = lax.ppermute(send_a, "gx", pairs(count_x, False))
    recv_b = lax.ppermute(send_b, ("gx", "gy"), pairs_inside(count_x, count_y))

    late, _ = lax.optimization_barrier((footprint, send_a))
    fp = jnp.pad(late.T, ((0, 5), (0, 128 - turbines)), constant_values=FAR)
    lap = jnp.ones((128, 128), F32)
    for i, extent in enumerate((DISK_X, DISK_Y, DISK_Z)):
        lap = lap * jnp.maximum(extent - jnp.abs(fp[i][:, None] - fp[i][None, :]), 0).astype(F32)
    live = jnp.arange(128) < turbines
    lap = jnp.where(live[:, None] & live[None, :], lap, 0.0)

    own = call(pack_y_kernel, y_pack, flops=PACK_COST)(flow_state, send_a)
    msg, code = call(
        pack_inlet_kernel,
        (shape(4, levels + 8, 128), jax.ShapeDtypeStruct((GROUP, levels + 8, 128), jnp.int32)),
        ins=[SMEM, VMEM, VMEM],
    )(block_map, inflow, own)
    base, disks, sums = call(
        base_kernel,
        (
            shape(*flow_state.shape),
            jax.ShapeDtypeStruct((levels, 16, 128), jnp.bfloat16),
            shape(8, 128),
        ),
        [pltpu.VMEM((2, levels, 16, 128), F32)],
        flops=TILE_COST,
    )(flow_state, fp)
    heard = send_inlet(msg, (recv_b, sums), count_x, count_y)

    own, near, west, east = call(
        rim_kernel, (y_pack, x_pack, x_pack, x_pack), [pltpu.VMEM((levels, 8, 128), F32)] * 3
    )(send_a, send_b, recv_a, recv_b, fp, sums, own)
    side_a = lax.ppermute(own, "gy", pairs(count_y, False))
    side_b = lax.ppermute(own, "gy", pairs(count_y, True))
    *heard, _ = lax.optimization_barrier((*heard, side_b))
    inlet = share_inlet(msg, list(heard), code, count_y)
    out, first, corner, last = call(
        steps_kernel,
        (shape(*flow_state.shape), x_pack, shape(2, 8, 128), x_pack),
        [
            pltpu.VMEM(flow_state.shape, F32),
            pltpu.VMEM(flow_state.shape, F32),
            pltpu.VMEM((2, levels, 16, 128), F32),
            pltpu.VMEM((2, levels, 128), F32),
            pltpu.VMEM((levels, 8, 128), F32),
            pltpu.VMEM((2, 2, 4, 16, 128), F32),
            pltpu.VMEM((2, 8, 128), F32),
            pltpu.SemaphoreType.DMA((levels // CHUNK,)),
        ],
        outs=[ANY, VMEM, VMEM, VMEM],
        flops=STEPS_COST,
    )(flow_state, base, disks, near, west, east, own, side_a, side_b, fp, lap)
    return call(
        fix_kernel,
        shape(*flow_state.shape),
        [
            pltpu.VMEM((levels, 8, 128), F32),
            pltpu.VMEM((levels, 8, 128), F32),
            pltpu.VMEM((2, 8, 128), F32),
            pltpu.VMEM((levels, 8, 128), F32),
            pltpu.SemaphoreType.DMA((levels // UNROLL, 4)),
        ],
        aliases={0: 0},
        ins=[ANY, VMEM, VMEM, VMEM, VMEM, VMEM],
        outs=ANY,
    )(out, inlet, send_b, first, corner, last)


def solution(mesh):
    placed = (P(None, None, "gx", "gy"), P(None, None, "gx"), P(), P())
    return jax.shard_map(
        body, mesh=mesh, in_specs=placed, out_specs=P(None, None, "gx", "gy"), check_vma=False
    )
```

```python
import jax
import jax.numpy as jnp
from jax import lax
from jax.experimental import pallas as pl
from jax.experimental.pallas import tpu as pltpu
from jax.sharding import PartitionSpec as P

DISK_X = 2
DISK_Y = 24
DISK_Z = 24
CELLS = float(DISK_X * DISK_Y * DISK_Z)

DT = 0.15
VISC = 0.3
BUOY = 0.3
GAIN = 2.0
BASE = DT * VISC
FAR = -100000
F32 = jnp.float32
UNROLL = 16
WIDE = 24
TRADES = ((2, 5), (3, 13))
CHUNK = 8
GROUP = 4
TILE_COST = 1 << 20
PACK_COST = 1 << 33
STEPS_COST = 1 << 32


def pairs(n, odd):
    if not odd:
        return [(i, i ^ 1) for i in range(n)]
    return [(i, (i + 1) % n if i % 2 else (i - 1) % n) for i in range(n)]


def pairs_inside(nx, ny):
    out = []
    for i in range(nx):
        for j in range(ny):
            if i in (0, nx - 1):
                to = (i, j ^ 1)
            else:
                to = (i + 1 if i % 2 else i - 1, j)
            out.append((i * ny + j, to[0] * ny + to[1]))
    return out


def upwind(vel):
    scaled = DT * vel
    return jnp.maximum(scaled, 0.0) + BASE, BASE - jnp.minimum(scaled, 0.0)


def coefs(u, v, w):
    cw, ce = upwind(u)
    cs, cn = upwind(v)
    cb, ca = upwind(w)
    c0 = 1.0 - ((cw + ce) + (cs + cn) + (cb + ca))
    return c0, cw, ce, cs, cn, cb, ca


def mix(c, f, w, e, s, n, b, a):
    return c[0] * f + c[1] * w + c[2] * e + c[3] * s + c[4] * n + c[5] * b + c[6] * a


def dot_nt(a, m):
    high = a.astype(jnp.bfloat16)
    low = (a - high.astype(F32)).astype(jnp.bfloat16)
    dims = (((1,), (1,)), ((), ()))
    return lax.dot_general(high, m, dims, preferred_element_type=F32) + lax.dot_general(
        low, m, dims, preferred_element_type=F32
    )


def dot_nn(a, m):
    high = a.astype(jnp.bfloat16)
    low = (a - high.astype(F32)).astype(jnp.bfloat16)
    return jnp.dot(high, m, preferred_element_type=F32) + jnp.dot(
        low, m, preferred_element_type=F32
    )


def iota(shape, dim):
    return lax.broadcasted_iota(jnp.int32, shape, dim)


def within(cells, start, extent):
    return ((cells >= start) & (cells < start + extent)).astype(F32)


def span_mask(fp, first, count):
    return within(first + iota((count, 128), 0), fp[1:2], DISK_Y).astype(jnp.bfloat16)


def pack_x_kernel(f_ref, a_ref, b_ref, sems):
    even = lax.axis_index("gx") % 2 == 0
    first_a = jnp.where(even, 14, 0)
    first_b = jnp.where(even, 0, 14)
    copies = []
    for c in range(4):
        for i, (first, ref) in enumerate(((first_a, a_ref), (first_b, b_ref))):
            copies.append(
                pltpu.make_async_copy(
                    f_ref.at[c, :, pl.ds(first, 2), :],
                    ref.at[:, pl.ds(2 * c, 2), :],
                    sems.at[c, i],
                )
            )
    for copy in copies:
        copy.start()
    for copy in copies:
        copy.wait()


def pack_inlet_kernel(map_ref, in_ref, after_ref, msg_ref, code_ref):
    nz = in_ref.shape[1]
    lane = iota((1, 128), 1)
    for c in range(4):
        msg_ref[c, 0:nz, :] = in_ref[c]
        msg_ref[c, nz : nz + 8, :] = jnp.zeros((8, 128), F32)
        for half in range(2):
            packed = jnp.zeros((1, 128), F32)
            for z in range(half * 32, min(nz, half * 32 + 32)):
                at = z - half * 32
                moved = pltpu.roll(in_ref[c, z : z + 1, :], (4 * at + 1) % 128, 1)
                packed = jnp.where(lane // 4 == at, moved, packed)
            msg_ref[c, nz + half : nz + half + 1, :] = packed

    tile_y = lax.axis_index("gy")
    count = lax.axis_size("gy")
    place = tile_y % GROUP
    level = iota((nz + 8, 128), 0)
    first = iota((nz + 8, 128), 1) % 4 == 0
    for k in range(GROUP):
        column = tile_y // GROUP * GROUP + (place ^ k)
        own = map_ref[column]
        left = map_ref[(column + count - 1) % count]
        right = map_ref[(column + 1) % count]
        source = jnp.where(level < nz, own, jnp.where(first, left, right))
        moved = source
        for one, two in TRADES:
            moved = jnp.where(source == one, two, jnp.where(source == two, one, moved))
        source = moved
        code = source // GROUP
        code = code + jnp.where(source % GROUP == place, 8, 0)
        code_ref[k] = code + jnp.where(source % GROUP // 2 == place // 2, 16, 0)


def pack_y_kernel(f_ref, after_ref, p_ref):
    nz = f_ref.shape[1]
    lane = iota((16, 128), 1)
    p_ref[...] = jnp.zeros_like(p_ref)
    for half in range(2):
        lo, hi = half * 32, min(nz, half * 32 + 32)

        def one(z, packed):
            here = lane // 4 == z - lo
            shift = (2 + 4 * (z - lo)) % 128
            return tuple(
                jnp.where(here, pltpu.roll(f_ref[i, z], shift, 1), packed[i]) for i in range(4)
            )

        zero = jnp.zeros((16, 128), F32)
        packed = lax.fori_loop(lo, hi, one, (zero,) * 4, unroll=UNROLL)
        for i in range(4):
            p_ref[half, i, 0:16, :] = packed[i]


def base_kernel(f_ref, fp_ref, base_ref, disks_ref, sums_ref, rows_ref):
    nz = f_ref.shape[1]
    first_x = lax.axis_index("gx") * 16
    first_y = lax.axis_index("gy") * 128
    fp = fp_ref[...]
    lane = iota((16, 128), 1)
    sub = iota((16, 128), 0)
    mask_x = within(first_x + sub, fp[0:1], DISK_X)

    def one(z, carry):
        below = jnp.maximum(z - 1, 0)
        above = jnp.minimum(z + 1, nz - 1)
        cur = [f_ref[c, z] for c in range(4)]
        c = coefs(cur[0], cur[1], cur[2])
        cw = jnp.where(sub == 0, 0.0, c[1])
        ce = jnp.where(sub == 15, 0.0, c[2])
        cs = jnp.where(lane == 0, 0.0, c[3])
        cn = jnp.where(lane == 127, 0.0, c[4])
        c = (c[0], cw, ce, cs, cn, c[5], c[6])
        for i in range(4):
            f = cur[i]
            new = mix(
                c,
                f,
                pltpu.roll(f, 1, 0),
                pltpu.roll(f, 15, 0),
                pltpu.roll(f, 1, 1),
                pltpu.roll(f, 127, 1),
                f_ref[i, below],
                f_ref[i, above],
            )
            if i == 2:
                new = new + (DT * BUOY) * cur[3]
            base_ref[i, z] = new
        disks_ref[z] = (mask_x * within(z, fp[2:3], DISK_Z)).astype(jnp.bfloat16)
        return carry

    lax.fori_loop(0, nz, one, 0, unroll=WIDE)
    span = span_mask(fp, first_y, 128)
    rows_ref[0] = dot_nn(f_ref[0].reshape(nz * 16, 128), span).reshape(nz, 16, 128)
    rows_ref[1] = dot_nn(base_ref[0].reshape(nz * 16, 128), span).reshape(nz, 16, 128)

    def add(z, acc):
        mask = within(z, fp[2:3], DISK_Z)
        return acc[0] + rows_ref[0, z] * mask, acc[1] + rows_ref[1, z] * mask

    zero = jnp.zeros((16, 128), F32)
    acc = lax.fori_loop(0, nz, add, (zero, zero), unroll=WIDE)
    sums_ref[0:1, :] = jnp.sum(acc[0] * mask_x, axis=0, keepdims=True)
    sums_ref[1:2, :] = jnp.sum(acc[1] * mask_x, axis=0, keepdims=True)
    sums_ref[2:8, :] = jnp.zeros((6, 128), F32)


def rim_kernel(
    sa_ref,
    sb_ref,
    ra_ref,
    rb_ref,
    fp_ref,
    sums_ref,
    p_in,
    p_ref,
    cur_ref,
    west_ref,
    east_ref,
    hl_ref,
    hh_ref,
    rows_ref,
):
    nz = hl_ref.shape[0]
    tile_x = lax.axis_index("gx")
    last_x = lax.axis_size("gx") - 1
    even = tile_x % 2 == 0
    first_x = tile_x * 16
    first_y = lax.axis_index("gy") * 128
    fp = fp_ref[...]
    lane = iota((8, 128), 1)
    sub = iota((8, 128), 0)

    @pl.when(even)
    def _():
        hl_ref[...] = rb_ref[...]
        hh_ref[...] = ra_ref[...]

    @pl.when(jnp.logical_not(even))
    def _():
        hl_ref[...] = ra_ref[...]
        hh_ref[...] = rb_ref[...]

    @pl.when(tile_x == 0)
    def _():
        hl_ref[...] = jnp.zeros_like(hl_ref)

    @pl.when(tile_x == last_x)
    def _():
        for z in range(nz):
            hh_ref[z] = pltpu.roll(sb_ref[z], 7, 0)

    def row(x, i):
        return x[i : i + 1]

    for half in range(2):
        lo, hi = half * 32, min(nz, half * 32 + 32)

        def one(z, packed):
            below = jnp.maximum(z - 1, 0)
            above = jnp.minimum(z + 1, nz - 1)
            own_a, own_b = sa_ref[z], sb_ref[z]
            own_low = jnp.where(even, own_b, own_a)
            own_high = jnp.where(even, own_a, own_b)
            low, high = hl_ref[z], hh_ref[z]
            u_low = jnp.where(sub == 0, row(low, 1), row(high, 0))
            v_low = jnp.where(sub == 0, row(low, 3), row(high, 2))
            w_low = jnp.where(sub == 0, row(low, 5), row(high, 4))
            west = jnp.where(sub == 0, row(low, 0), row(own_high, 1))
            east = jnp.where(sub == 0, row(own_low, 0), row(high, 1))
            down = jnp.where(sub == 0, row(hl_ref[below], 1), row(hh_ref[below], 0))
            up = jnp.where(sub == 0, row(hl_ref[above], 1), row(hh_ref[above], 0))
            south = jnp.where(lane == 0, 0.0, pltpu.roll(u_low, 1, 1))
            north = jnp.where(lane == 127, 0.0, pltpu.roll(u_low, 127, 1))
            ring = mix(coefs(u_low, v_low, w_low), u_low, west, east, south, north, down, up)
            into_low = upwind(row(own_low, 0))[0] * row(low, 1)
            into_high = upwind(row(own_high, 1))[1] * row(high, 0)
            both = jnp.where(sub == 2, into_low, jnp.where(sub == 3, into_high, ring))
            both = jnp.where(sub == 4, row(low, 0), both)
            both = jnp.where(sub == 5, row(low, 1), both)
            both = jnp.where(sub == 6, row(high, 0), both)
            both = jnp.where(sub == 7, row(high, 1), both)
            rows_ref[z] = both
            odd = sub % 2 == 1
            cur_ref[z] = jnp.where(odd, low, high)
            west_ref[z] = jnp.where(odd, pltpu.roll(low, 1, 0), pltpu.roll(own_high, 7, 0))
            east_ref[z] = jnp.where(odd, pltpu.roll(own_low, 1, 0), pltpu.roll(high, 7, 0))
            here = lane // 4 == z - lo
            shift = (2 + 4 * (z - lo)) % 128
            return (
                jnp.where(here, pltpu.roll(low, shift, 1), packed[0]),
                jnp.where(here, pltpu.roll(high, shift, 1), packed[1]),
            )

        zero = jnp.zeros((8, 128), F32)
        packed = lax.fori_loop(lo, hi, one, (zero, zero), unroll=UNROLL)
        for c in range(4):
            p_ref[half, c, 0:16, :] = p_in[half, c, 0:16, :]
            p_ref[half, c, 16:17, :] = row(packed[0], 2 * c + 1)
            p_ref[half, c, 17:18, :] = row(packed[1], 2 * c)
            p_ref[half, c, 18:24, :] = jnp.zeros((6, 128), F32)

    span = span_mask(fp, first_y, 128)
    rows_ref[...] = dot_nn(rows_ref[...].reshape(nz * 8, 128), span).reshape(nz, 8, 128)

    def add(z, acc):
        return acc + rows_ref[z] * within(z, fp[2:3], DISK_Z)

    acc = lax.fori_loop(0, nz, add, jnp.zeros((8, 128), F32), unroll=WIDE)
    column = jnp.where(sub == 0, -1, 16)
    column = jnp.where(sub == 2, 0, jnp.where(sub == 3, 15, column))
    column = jnp.where(sub >= 4, jnp.where(sub < 6, sub - 6, sub + 10), column)
    acc = acc * within(first_x + column, fp[0:1], DISK_X)
    p_ref[0, 0, 18:19, :] = sums_ref[0:1, :] + jnp.sum(acc[4:8], axis=0, keepdims=True)
    p_ref[1, 0, 18:19, :] = sums_ref[1:2, :] + jnp.sum(acc[0:4], axis=0, keepdims=True)


def steps_kernel(
    f_ref,
    base_ref,
    disks_ref,
    cur_ref,
    west_ref,
    east_ref,
    p_ref,
    pa_ref,
    pb_ref,
    fp_ref,
    lap_ref,
    out_ref,
    first_ref,
    first_corner_ref,
    last_ref,
    mid_ref,
    new_ref,
    force_ref,
    rim_force_ref,
    ring_ref,
    edge_ref,
    corner_ref,
    sems,
):
    nz = f_ref.shape[1]
    tile_x = lax.axis_index("gx")
    tile_y = lax.axis_index("gy")
    last_x = lax.axis_size("gx") - 1
    all_y = lax.axis_size("gy") * 128
    even_y = tile_y % 2 == 0
    first_x = tile_x * 16
    first_y = tile_y * 128
    fp = fp_ref[...]
    fx, fy, fz = fp[0:1], fp[1:2], fp[2:3]
    lane = iota((16, 128), 1)
    sub = iota((16, 128), 0)

    def pick(half, c):
        a, b = pa_ref[half, c], pb_ref[half, c]
        return jnp.where(even_y, b, a), jnp.where(even_y, a, b)

    k24 = iota((24, 128), 1) % 4
    left_cols, right_cols = [], []
    for c in range(4):
        lefts, rights = [], []
        for half in range(2):
            left, right = pick(half, c)
            own = p_ref[half, c]
            lefts.append(jnp.where(k24 < 2, left, own))
            rights.append(jnp.where(k24 < 2, own, right))
            edge = jnp.where(k24 == 1, left, pltpu.roll(right, 126, 1))
            edge_ref[0, half, c] = edge[0:16]
            corner_ref[half, 2 * c + 1 : 2 * c + 2, :] = edge[16:17]
            corner_ref[half, 2 * c : 2 * c + 1, :] = edge[17:18]
        left_cols.append(jnp.concatenate(lefts, axis=1))
        right_cols.append(jnp.concatenate(rights, axis=1))
    def total(half):
        left, right = pick(half, 0)
        return p_ref[half, 0, 18:19, :] + left[18:19] + right[18:19]

    def thrust_of(sums):
        speed = sums * (1.0 / CELLS)
        return -GAIN * DT * speed * jnp.abs(speed)

    thrust1 = thrust_of(total(0))
    at = iota((256, 128), 0)
    level = at // 4
    k_at = at % 4
    mask_level = within(level, fz, DISK_Z) * (level < nz).astype(F32)
    y_left = jnp.where(k_at == 1, jnp.where(first_y == 0, all_y - 1, first_y - 1), first_y)
    y_right = jnp.where(
        k_at == 1, first_y + 127, jnp.where(first_y + 128 == all_y, 0, first_y + 128)
    )
    middle = ((k_at == 1) | (k_at == 2)).astype(F32)
    mask_left = mask_level * within(y_left, fy, DISK_Y) * middle
    mask_right = mask_level * within(y_right, fy, DISK_Y) * middle
    k256 = iota((24, 256), 1) % 4

    def facing(cols, mask):
        u, v = cols[0], cols[1]
        cs, cn = upwind(v)
        term = jnp.where(k256 == 1, cn * pltpu.roll(u, 255, 1), cs * pltpu.roll(u, 1, 1))
        term = jnp.concatenate([term, jnp.zeros((8, 256), F32)], axis=0)
        return dot_nn(term, mask.astype(jnp.bfloat16))

    faces = facing(left_cols, mask_left) + facing(right_cols, mask_right)
    sub32 = iota((32, 128), 0)
    column = jnp.where(sub32 == 16, -1, jnp.where(sub32 == 17, 16, sub32))
    mask_x32 = within(first_x + column, fx, DISK_X) * (sub32 < 18).astype(F32)
    faces = jnp.sum(faces * mask_x32, axis=0, keepdims=True)
    pushed = jnp.dot(
        jnp.broadcast_to(thrust1, (8, 128)),
        lap_ref[...],
        precision=lax.Precision.HIGHEST,
        preferred_element_type=F32,
    )
    thrust2 = thrust_of(total(1) + faces + pushed[0:1])

    span = within(first_y + iota((128, 128), 0), fy, DISK_Y)
    disks = disks_ref[...].reshape(nz * 16, 128)

    def dot_disks(mask, weights):
        high = weights.astype(jnp.bfloat16)
        low = (weights - high.astype(F32)).astype(jnp.bfloat16)
        dims = (((1,), (1,)), ((), ()))
        return lax.dot_general(
            mask, high, dims, preferred_element_type=F32
        ) + lax.dot_general(mask, low, dims, preferred_element_type=F32)

    force_ref[0] = dot_disks(disks, span * thrust1).reshape(nz, 16, 128)
    force_ref[1] = dot_disks(disks, span * thrust2).reshape(nz, 16, 128)
    levels = within(iota((nz, 128), 0), fz, DISK_Z).astype(jnp.bfloat16)
    for side, x in ((0, 16), (1, -1)):
        weights = span * (thrust1 * within(first_x + x, fx, DISK_X))
        rim_force_ref[side] = dot_disks(levels, weights)
    by_x1 = within(first_x + sub, fx, DISK_X) * thrust1
    y_cols = jnp.where(k_at == 1, y_left, y_right)
    mask_cols = mask_level * within(y_cols, fy, DISK_Y) * middle
    force_cols = dot_nt(by_x1, mask_cols.astype(jnp.bfloat16))

    lane256 = iota((16, 256), 1)
    sub256 = iota((16, 256), 0)

    def rim_cols(cols):
        cur = [x[0:16] for x in cols]
        c = coefs(cur[0], cur[1], cur[2])
        new = []
        for i in range(4):
            f = cur[i]
            west = jnp.where(sub256 == 0, cols[i][16:17], pltpu.roll(f, 1, 0))
            east = jnp.where(sub256 == 15, cols[i][17:18], pltpu.roll(f, 15, 0))
            south = pltpu.roll(f, 1, 1)
            north = pltpu.roll(f, 255, 1)
            down = jnp.where(lane256 < 4, f, pltpu.roll(f, 4, 1))
            up = jnp.where(lane256 >= 4 * nz - 4, f, pltpu.roll(f, 252, 1))
            new.append(mix(c, f, west, east, south, north, down, up))
        new[0] = new[0] + force_cols
        new[2] = new[2] + (DT * BUOY) * cur[3]
        return new

    left_new, right_new = rim_cols(left_cols), rim_cols(right_cols)
    for c in range(4):
        edge = jnp.where(lane256 % 4 == 1, left_new[c], pltpu.roll(right_new[c], 254, 1))
        edge_ref[1, 0, c] = edge[:, 0:128]
        edge_ref[1, 1, c] = edge[:, 128:256]

    lane8 = iota((8, 128), 1)
    sub8 = iota((8, 128), 0)
    odd = sub8 % 2 == 1

    def rim_rows(z, carry):
        below = jnp.maximum(z - 1, 0)
        above = jnp.minimum(z + 1, nz - 1)
        half = z // 32
        shift = (255 - 4 * (z - 32 * half)) % 128
        cur = cur_ref[z]
        corner = pltpu.roll(corner_ref[half], shift, 1)
        south = jnp.where(lane8 == 0, corner, pltpu.roll(cur, 1, 1))
        north = jnp.where(lane8 == 127, corner, pltpu.roll(cur, 127, 1))
        vel = [jnp.where(odd, cur[2 * i + 1 : 2 * i + 2], cur[2 * i : 2 * i + 1]) for i in range(4)]
        c = coefs(vel[0], vel[1], vel[2])
        new = mix(c, cur, west_ref[z], east_ref[z], south, north, cur_ref[below], cur_ref[above])
        new = new + jnp.where(sub8 // 2 == 2, (DT * BUOY) * vel[3], 0.0)
        new = new + jnp.where(sub8 == 0, rim_force_ref[0, pl.ds(z, 1), :], 0.0)
        new = new + jnp.where(sub8 == 1, rim_force_ref[1, pl.ds(z, 1), :], 0.0)
        ring_ref[z] = jnp.where(odd & (tile_x == 0), cur, new)
        return carry

    lax.fori_loop(0, nz, rim_rows, 0, unroll=WIDE)

    def first_step(group, carry):
        for j in range(WIDE):
            z = group * WIDE + j
            half = z // 32
            shift = (255 - 4 * (z - 32 * half)) % 128
            near = cur_ref[z]
            cw, ce = upwind(f_ref[0, z])
            cs, cn = upwind(f_ref[1, z])
            along_x = jnp.where(sub == 0, cw, jnp.where(sub == 15, ce, 0.0))
            along_y = jnp.where(lane == 0, cs, jnp.where(lane == 127, cn, 0.0))
            for i in range(4):
                beside = jnp.where(sub < 8, near[2 * i + 1 : 2 * i + 2], near[2 * i : 2 * i + 1])
                edge = pltpu.roll(edge_ref[0, half, i], shift, 1)
                new = base_ref[i, z] + along_x * beside + along_y * edge
                if i == 0:
                    new = new + force_ref[0, z]
                mid_ref[i, z] = new
        return carry

    def level(z):
        below = jnp.maximum(z - 1, 0)
        above = jnp.minimum(z + 1, nz - 1)
        half = z // 32
        shift = (255 - 4 * (z - 32 * half)) % 128
        cur = [mid_ref[c, z] for c in range(4)]
        ring = ring_ref[z]
        c = coefs(cur[0], cur[1], cur[2])
        for i in range(4):
            f = cur[i]
            west = jnp.where(sub == 0, ring[2 * i + 1 : 2 * i + 2], pltpu.roll(f, 1, 0))
            outside = jnp.where(tile_x == last_x, f[15:16], ring[2 * i : 2 * i + 1])
            east = jnp.where(sub == 15, outside, pltpu.roll(f, 15, 0))
            edge = pltpu.roll(edge_ref[1, half, i], shift, 1)
            south = jnp.where(lane == 0, edge, pltpu.roll(f, 1, 1))
            north = jnp.where(lane == 127, edge, pltpu.roll(f, 127, 1))
            new = mix(c, f, west, east, south, north, mid_ref[i, below], mid_ref[i, above])
            if i == 0:
                new = new + force_ref[1, z]
            if i == 2:
                new = new + (DT * BUOY) * cur[3]
            new_ref[i, z] = new

    def send(chunk):
        part = pl.ds(chunk * CHUNK, CHUNK)
        return pltpu.make_async_copy(new_ref.at[:, part], out_ref.at[:, part], sems.at[chunk])

    def second_step(group, carry):
        for i in range(WIDE):
            z = group * WIDE + i
            level(z)
            if i % CHUNK == CHUNK - 1:
                send(group * (WIDE // CHUNK) + i // CHUNK).start()
        return carry

    lax.fori_loop(0, nz // WIDE, first_step, 0)
    lax.fori_loop(0, nz // WIDE, second_step, 0)

    @pl.when(tile_x == 0)
    def _():
        for c in range(4):
            first_ref[:, 2 * c : 2 * c + 2, :] = mid_ref[c, :, 0:2, :]
            last_ref[:, 2 * c : 2 * c + 2, :] = new_ref[c, :, 0:2, :]
            for half in range(2):
                first_corner_ref[half, 2 * c : 2 * c + 1, :] = edge_ref[1, half, c, 0:1, :]
                first_corner_ref[half, 2 * c + 1 : 2 * c + 2, :] = edge_ref[0, half, c, 0:1, :]

    for chunk in range(nz // CHUNK):
        send(chunk).wait()


def fix_kernel(
    out_in, in_ref, sb_ref, first_ref, corner_ref, last_ref, out_ref, inlet, new, wide, done, sems
):
    nz = first_ref.shape[0]
    lane = iota((8, 128), 1)
    sub = iota((8, 128), 0)
    is_even = sub % 2 == 0


    def send(group):
        part = pl.ds(group * WIDE, WIDE)
        return [
            pltpu.make_async_copy(
                done.at[part, pl.ds(2 * c, 2), :], out_ref.at[c, part, pl.ds(0, 2), :], sems.at[group, c]
            )
            for c in range(4)
        ]

    @pl.when(lax.axis_index("gx") == 0)
    def _():
        inlet[...] = jnp.zeros_like(inlet)
        for c in range(4):
            for z in range(nz):
                inlet[z, 2 * c : 2 * c + 1, :] = in_ref[c, z : z + 1, :]
        for half in range(2):
            old = corner_ref[half]
            push = upwind(old[1:2])[0]
            for c in range(4):
                msg = in_ref[c, nz + half : nz + half + 1, :]
                side = jnp.where(
                    lane[0:1] % 4 == 1, pltpu.roll(msg, 1, 1), pltpu.roll(msg, 127, 1)
                )
                wide[half, 2 * c : 2 * c + 1, :] = old[2 * c : 2 * c + 1] + push * side
                wide[half, 2 * c + 1 : 2 * c + 2, :] = jnp.zeros((1, 128), F32)

        def first(group, carry):
            for i in range(WIDE):
                z = group * WIDE + i
                push = upwind(sb_ref[z, 0:1, :])[0]
                new[z] = first_ref[z] + jnp.where(is_even, push * inlet[z], 0.0)
            return carry

        lax.fori_loop(0, nz // WIDE, first, 0)

        def second(group, carry):
            for i in range(WIDE):
                z = group * WIDE + i
                below = jnp.maximum(z - 1, 0)
                above = jnp.minimum(z + 1, nz - 1)
                half = z // 32
                shift = (255 - 4 * (z - 32 * half)) % 128
                cur = new[z]
                east = pltpu.roll(cur, 7, 0)
                corner = pltpu.roll(wide[half], shift, 1)
                south = jnp.where(lane == 0, corner, pltpu.roll(cur, 1, 1))
                north = jnp.where(lane == 127, corner, pltpu.roll(cur, 127, 1))
                c = coefs(cur[0:1], cur[2:3], cur[4:5])
                zero = mix(c, cur, inlet[z], east, south, north, new[below], new[above])
                zero = zero + jnp.where(sub == 4, (DT * BUOY) * cur[6:7], 0.0)
                delta = pltpu.roll(cur - first_ref[z], 1, 0)
                one = last_ref[z] + upwind(cur[1:2])[0] * delta
                done[z] = jnp.where(is_even, zero, one)
            for copy in send(group):
                copy.start()
            return carry

        lax.fori_loop(0, nz // WIDE, second, 0)
        for group in range(nz // WIDE):
            for copy in send(group):
                copy.wait()


VMEM = pl.BlockSpec(memory_space=pltpu.VMEM)
ANY = pl.BlockSpec(memory_space=pl.ANY)
SMEM = pl.BlockSpec(memory_space=pltpu.SMEM)
HBM = pl.BlockSpec(memory_space=pltpu.HBM)


def call(kernel, out, scratch=(), aliases=None, ins=None, outs=None, flops=1 << 20):
    specs = {}
    if ins is not None:
        specs["in_specs"] = ins
    if outs is not None:
        specs["out_specs"] = outs
    return pl.pallas_call(
        kernel,
        out_shape=out,
        scratch_shapes=scratch,
        input_output_aliases=aliases or {},
        compiler_params=pltpu.CompilerParams(vmem_limit_bytes=24 << 20),
        cost_estimate=pl.CostEstimate(flops=flops, bytes_accessed=1 << 20, transcendentals=0),
        **specs,
    )


def row_of(place):
    for one, two in TRADES:
        if place in (one, two):
            return one + two - place
    return place


def send_inlet(msg, after, count_x, count_y):
    heard = {}
    for m in (2, 3, 1, 0):
        moves = [
            (row_of(GROUP * m + j % GROUP) * count_y + j, j)
            for j in range(count_y)
            if GROUP * m + j % GROUP
        ]
        if m == 0:
            sent, *_ = lax.optimization_barrier((msg, *after))
        else:
            sent = msg
        heard[m] = lax.ppermute(sent, ("gx", "gy"), moves)
    return [heard[m] for m in range(4)]


def share_inlet(msg, heard, code, count_y):
    heard[0] = jnp.where(lax.axis_index("gy") % GROUP == 0, msg, heard[0])

    def pick(k):
        out = heard[0]
        for m in range(1, len(heard)):
            out = jnp.where(code[k] & 7 == m, heard[m], out)
        return out

    core = lax.ppermute(
        jnp.concatenate([pick(1), pick(3)]), "gy", [(j, j ^ 1) for j in range(count_y)]
    )
    mine = jnp.where(code[0] & 8 != 0, pick(0), core[0:4])
    theirs = jnp.where(code[2] & 8 != 0, pick(2), core[4:8])
    other = lax.ppermute(theirs, "gy", [(j, j ^ 2) for j in range(count_y)])
    return jnp.where(code[0] & 16 != 0, mine, other)


def body(flow_state, inflow, footprint, block_map):
    levels = flow_state.shape[1]
    count_x = lax.axis_size("gx")
    count_y = lax.axis_size("gy")
    turbines = footprint.shape[0]
    shape = lambda *s: jax.ShapeDtypeStruct(s, F32)
    x_pack = shape(levels, 8, 128)
    y_pack = shape(2, 4, 24, 128)

    send_a, send_b = call(
        pack_x_kernel, (x_pack, x_pack), [pltpu.SemaphoreType.DMA((4, 2))], ins=[HBM], outs=[VMEM] * 2
    )(flow_state)
    recv_a = lax.ppermute(send_a, "gx", pairs(count_x, False))
    recv_b = lax.ppermute(send_b, ("gx", "gy"), pairs_inside(count_x, count_y))

    late, _ = lax.optimization_barrier((footprint, send_a))
    fp = jnp.pad(late.T, ((0, 5), (0, 128 - turbines)), constant_values=FAR)
    lap = jnp.ones((128, 128), F32)
    for i, extent in enumerate((DISK_X, DISK_Y, DISK_Z)):
        lap = lap * jnp.maximum(extent - jnp.abs(fp[i][:, None] - fp[i][None, :]), 0).astype(F32)
    live = jnp.arange(128) < turbines
    lap = jnp.where(live[:, None] & live[None, :], lap, 0.0)

    own = call(pack_y_kernel, y_pack, flops=PACK_COST)(flow_state, send_a)
    msg, code = call(
        pack_inlet_kernel,
        (shape(4, levels + 8, 128), jax.ShapeDtypeStruct((GROUP, levels + 8, 128), jnp.int32)),
        ins=[SMEM, VMEM, VMEM],
    )(block_map, inflow, own)
    base, disks, sums = call(
        base_kernel,
        (
            shape(*flow_state.shape),
            jax.ShapeDtypeStruct((levels, 16, 128), jnp.bfloat16),
            shape(8, 128),
        ),
        [pltpu.VMEM((2, levels, 16, 128), F32)],
        flops=TILE_COST,
    )(flow_state, fp)
    heard = send_inlet(msg, (recv_b, sums), count_x, count_y)

    own, near, west, east = call(
        rim_kernel, (y_pack, x_pack, x_pack, x_pack), [pltpu.VMEM((levels, 8, 128), F32)] * 3
    )(send_a, send_b, recv_a, recv_b, fp, sums, own)
    side_a = lax.ppermute(own, "gy", pairs(count_y, False))
    side_b = lax.ppermute(own, "gy", pairs(count_y, True))
    *heard, _ = lax.optimization_barrier((*heard, side_b))
    inlet = share_inlet(msg, list(heard), code, count_y)
    out, first, corner, last = call(
        steps_kernel,
        (shape(*flow_state.shape), x_pack, shape(2, 8, 128), x_pack),
        [
            pltpu.VMEM(flow_state.shape, F32),
            pltpu.VMEM(flow_state.shape, F32),
            pltpu.VMEM((2, levels, 16, 128), F32),
            pltpu.VMEM((2, levels, 128), F32),
            pltpu.VMEM((levels, 8, 128), F32),
            pltpu.VMEM((2, 2, 4, 16, 128), F32),
            pltpu.VMEM((2, 8, 128), F32),
            pltpu.SemaphoreType.DMA((levels // CHUNK,)),
        ],
        outs=[ANY, VMEM, VMEM, VMEM],
        flops=STEPS_COST,
    )(flow_state, base, disks, near, west, east, own, side_a, side_b, fp, lap)
    return call(
        fix_kernel,
        shape(*flow_state.shape),
        [
            pltpu.VMEM((levels, 8, 128), F32),
            pltpu.VMEM((levels, 8, 128), F32),
            pltpu.VMEM((2, 8, 128), F32),
            pltpu.VMEM((levels, 8, 128), F32),
            pltpu.SemaphoreType.DMA((levels // WIDE, 4)),
        ],
        aliases={0: 0},
        ins=[ANY, VMEM, VMEM, VMEM, VMEM, VMEM],
        outs=ANY,
    )(out, inlet, send_b, first, corner, last)


def solution(mesh):
    placed = (P(None, None, "gx", "gy"), P(None, None, "gx"), P(), P())
    return jax.shard_map(
        body, mesh=mesh, in_specs=placed, out_specs=P(None, None, "gx", "gy"), check_vma=False
    )
```

```python
import jax
import jax.numpy as jnp
from jax import lax
from jax.experimental import pallas as pl
from jax.experimental.pallas import tpu as pltpu
from jax.sharding import PartitionSpec as P

DISK_X = 2
DISK_Y = 24
DISK_Z = 24
CELLS = float(DISK_X * DISK_Y * DISK_Z)

DT = 0.15
VISC = 0.3
BUOY = 0.3
GAIN = 2.0
BASE = DT * VISC
FAR = -100000
F32 = jnp.float32
UNROLL = 16
WIDE = 48
TRADES = ((2, 5), (3, 13))
CHUNK = 8
GROUP = 4
TILE_COST = 1 << 20
PACK_COST = 1 << 33
STEPS_COST = 1 << 32


def pairs(n, odd):
    if not odd:
        return [(i, i ^ 1) for i in range(n)]
    return [(i, (i + 1) % n if i % 2 else (i - 1) % n) for i in range(n)]


def pairs_inside(nx, ny):
    out = []
    for i in range(nx):
        for j in range(ny):
            if i in (0, nx - 1):
                to = (i, j ^ 1)
            else:
                to = (i + 1 if i % 2 else i - 1, j)
            out.append((i * ny + j, to[0] * ny + to[1]))
    return out


def upwind(vel):
    scaled = DT * vel
    return jnp.maximum(scaled, 0.0) + BASE, BASE - jnp.minimum(scaled, 0.0)


def coefs(u, v, w):
    cw, ce = upwind(u)
    cs, cn = upwind(v)
    cb, ca = upwind(w)
    c0 = 1.0 - ((cw + ce) + (cs + cn) + (cb + ca))
    return c0, cw, ce, cs, cn, cb, ca


def mix(c, f, w, e, s, n, b, a):
    return c[0] * f + c[1] * w + c[2] * e + c[3] * s + c[4] * n + c[5] * b + c[6] * a


def dot_nt(a, m):
    high = a.astype(jnp.bfloat16)
    low = (a - high.astype(F32)).astype(jnp.bfloat16)
    dims = (((1,), (1,)), ((), ()))
    return lax.dot_general(high, m, dims, preferred_element_type=F32) + lax.dot_general(
        low, m, dims, preferred_element_type=F32
    )


def dot_nn(a, m):
    high = a.astype(jnp.bfloat16)
    low = (a - high.astype(F32)).astype(jnp.bfloat16)
    return jnp.dot(high, m, preferred_element_type=F32) + jnp.dot(
        low, m, preferred_element_type=F32
    )


def iota(shape, dim):
    return lax.broadcasted_iota(jnp.int32, shape, dim)


def within(cells, start, extent):
    return ((cells >= start) & (cells < start + extent)).astype(F32)


def span_mask(fp, first, count):
    return within(first + iota((count, 128), 0), fp[1:2], DISK_Y).astype(jnp.bfloat16)


def pack_x_kernel(f_ref, a_ref, b_ref, sems):
    even = lax.axis_index("gx") % 2 == 0
    first_a = jnp.where(even, 14, 0)
    first_b = jnp.where(even, 0, 14)
    copies = []
    for c in range(4):
        for i, (first, ref) in enumerate(((first_a, a_ref), (first_b, b_ref))):
            copies.append(
                pltpu.make_async_copy(
                    f_ref.at[c, :, pl.ds(first, 2), :],
                    ref.at[:, pl.ds(2 * c, 2), :],
                    sems.at[c, i],
                )
            )
    for copy in copies:
        copy.start()
    for copy in copies:
        copy.wait()


def pack_inlet_kernel(map_ref, in_ref, after_ref, msg_ref, code_ref):
    nz = in_ref.shape[1]
    lane = iota((1, 128), 1)
    for c in range(4):
        msg_ref[c, 0:nz, :] = in_ref[c]
        msg_ref[c, nz : nz + 8, :] = jnp.zeros((8, 128), F32)
        for half in range(2):
            packed = jnp.zeros((1, 128), F32)
            for z in range(half * 32, min(nz, half * 32 + 32)):
                at = z - half * 32
                moved = pltpu.roll(in_ref[c, z : z + 1, :], (4 * at + 1) % 128, 1)
                packed = jnp.where(lane // 4 == at, moved, packed)
            msg_ref[c, nz + half : nz + half + 1, :] = packed

    tile_y = lax.axis_index("gy")
    count = lax.axis_size("gy")
    place = tile_y % GROUP
    level = iota((nz + 8, 128), 0)
    first = iota((nz + 8, 128), 1) % 4 == 0
    for k in range(GROUP):
        column = tile_y // GROUP * GROUP + (place ^ k)
        own = map_ref[column]
        left = map_ref[(column + count - 1) % count]
        right = map_ref[(column + 1) % count]
        source = jnp.where(level < nz, own, jnp.where(first, left, right))
        moved = source
        for one, two in TRADES:
            moved = jnp.where(source == one, two, jnp.where(source == two, one, moved))
        source = moved
        code = source // GROUP
        code = code + jnp.where(source % GROUP == place, 8, 0)
        code_ref[k] = code + jnp.where(source % GROUP // 2 == place // 2, 16, 0)


def pack_y_kernel(f_ref, after_ref, p_ref):
    nz = f_ref.shape[1]
    lane = iota((16, 128), 1)
    p_ref[...] = jnp.zeros_like(p_ref)
    for half in range(2):
        lo, hi = half * 32, min(nz, half * 32 + 32)

        def one(z, packed):
            here = lane // 4 == z - lo
            shift = (2 + 4 * (z - lo)) % 128
            return tuple(
                jnp.where(here, pltpu.roll(f_ref[i, z], shift, 1), packed[i]) for i in range(4)
            )

        zero = jnp.zeros((16, 128), F32)
        packed = lax.fori_loop(lo, hi, one, (zero,) * 4, unroll=UNROLL)
        for i in range(4):
            p_ref[half, i, 0:16, :] = packed[i]


def base_kernel(f_ref, fp_ref, base_ref, disks_ref, masks_ref, sums_ref, rows_ref):
    nz = f_ref.shape[1]
    first_x = lax.axis_index("gx") * 16
    first_y = lax.axis_index("gy") * 128
    fp = fp_ref[...]
    lane = iota((16, 128), 1)
    sub = iota((16, 128), 0)
    mask_x = within(first_x + sub, fp[0:1], DISK_X)

    def one(z, carry):
        below = jnp.maximum(z - 1, 0)
        above = jnp.minimum(z + 1, nz - 1)
        cur = [f_ref[c, z] for c in range(4)]
        c = coefs(cur[0], cur[1], cur[2])
        cw = jnp.where(sub == 0, 0.0, c[1])
        ce = jnp.where(sub == 15, 0.0, c[2])
        cs = jnp.where(lane == 0, 0.0, c[3])
        cn = jnp.where(lane == 127, 0.0, c[4])
        c = (c[0], cw, ce, cs, cn, c[5], c[6])
        for i in range(4):
            f = cur[i]
            new = mix(
                c,
                f,
                pltpu.roll(f, 1, 0),
                pltpu.roll(f, 15, 0),
                pltpu.roll(f, 1, 1),
                pltpu.roll(f, 127, 1),
                f_ref[i, below],
                f_ref[i, above],
            )
            if i == 2:
                new = new + (DT * BUOY) * cur[3]
            base_ref[i, z] = new
        disks_ref[z] = (mask_x * within(z, fp[2:3], DISK_Z)).astype(jnp.bfloat16)
        return carry

    lax.fori_loop(0, nz, one, 0, unroll=WIDE)
    span = span_mask(fp, first_y, 128)
    rows_ref[0] = dot_nn(f_ref[0].reshape(nz * 16, 128), span).reshape(nz, 16, 128)
    rows_ref[1] = dot_nn(base_ref[0].reshape(nz * 16, 128), span).reshape(nz, 16, 128)

    def add(z, acc):
        mask = within(z, fp[2:3], DISK_Z)
        return acc[0] + rows_ref[0, z] * mask, acc[1] + rows_ref[1, z] * mask

    zero = jnp.zeros((16, 128), F32)
    acc = lax.fori_loop(0, nz, add, (zero, zero), unroll=WIDE)
    sums_ref[0:1, :] = jnp.sum(acc[0] * mask_x, axis=0, keepdims=True)
    sums_ref[1:2, :] = jnp.sum(acc[1] * mask_x, axis=0, keepdims=True)
    sums_ref[2:8, :] = jnp.zeros((6, 128), F32)

    fy, fz = fp[1:2], fp[2:3]
    all_y = lax.axis_size("gy") * 128
    at = iota((256, 128), 0)
    level = at // 4
    k_at = at % 4
    mask_level = within(level, fz, DISK_Z) * (level < nz).astype(F32)
    y_left = jnp.where(k_at == 1, jnp.where(first_y == 0, all_y - 1, first_y - 1), first_y)
    y_right = jnp.where(
        k_at == 1, first_y + 127, jnp.where(first_y + 128 == all_y, 0, first_y + 128)
    )
    middle = ((k_at == 1) | (k_at == 2)).astype(F32)
    mask_left = mask_level * within(y_left, fy, DISK_Y) * middle
    mask_right = mask_level * within(y_right, fy, DISK_Y) * middle
    y_cols = jnp.where(k_at == 1, y_left, y_right)
    mask_cols = mask_level * within(y_cols, fy, DISK_Y) * middle
    for i, mask in enumerate((mask_left, mask_right, mask_cols)):
        masks_ref[i] = mask.astype(jnp.bfloat16)


def rim_kernel(
    sa_ref,
    sb_ref,
    ra_ref,
    rb_ref,
    fp_ref,
    sums_ref,
    p_in,
    p_ref,
    cur_ref,
    west_ref,
    east_ref,
    hl_ref,
    hh_ref,
    rows_ref,
):
    nz = hl_ref.shape[0]
    tile_x = lax.axis_index("gx")
    last_x = lax.axis_size("gx") - 1
    even = tile_x % 2 == 0
    first_x = tile_x * 16
    first_y = lax.axis_index("gy") * 128
    fp = fp_ref[...]
    lane = iota((8, 128), 1)
    sub = iota((8, 128), 0)

    @pl.when(even)
    def _():
        hl_ref[...] = rb_ref[...]
        hh_ref[...] = ra_ref[...]

    @pl.when(jnp.logical_not(even))
    def _():
        hl_ref[...] = ra_ref[...]
        hh_ref[...] = rb_ref[...]

    @pl.when(tile_x == 0)
    def _():
        hl_ref[...] = jnp.zeros_like(hl_ref)

    @pl.when(tile_x == last_x)
    def _():
        for z in range(nz):
            hh_ref[z] = pltpu.roll(sb_ref[z], 7, 0)

    def row(x, i):
        return x[i : i + 1]

    for half in range(2):
        lo, hi = half * 32, min(nz, half * 32 + 32)

        def one(z, packed):
            below = jnp.maximum(z - 1, 0)
            above = jnp.minimum(z + 1, nz - 1)
            own_a, own_b = sa_ref[z], sb_ref[z]
            own_low = jnp.where(even, own_b, own_a)
            own_high = jnp.where(even, own_a, own_b)
            low, high = hl_ref[z], hh_ref[z]
            u_low = jnp.where(sub == 0, row(low, 1), row(high, 0))
            v_low = jnp.where(sub == 0, row(low, 3), row(high, 2))
            w_low = jnp.where(sub == 0, row(low, 5), row(high, 4))
            west = jnp.where(sub == 0, row(low, 0), row(own_high, 1))
            east = jnp.where(sub == 0, row(own_low, 0), row(high, 1))
            down = jnp.where(sub == 0, row(hl_ref[below], 1), row(hh_ref[below], 0))
            up = jnp.where(sub == 0, row(hl_ref[above], 1), row(hh_ref[above], 0))
            south = jnp.where(lane == 0, 0.0, pltpu.roll(u_low, 1, 1))
            north = jnp.where(lane == 127, 0.0, pltpu.roll(u_low, 127, 1))
            ring = mix(coefs(u_low, v_low, w_low), u_low, west, east, south, north, down, up)
            into_low = upwind(row(own_low, 0))[0] * row(low, 1)
            into_high = upwind(row(own_high, 1))[1] * row(high, 0)
            both = jnp.where(sub == 2, into_low, jnp.where(sub == 3, into_high, ring))
            both = jnp.where(sub == 4, row(low, 0), both)
            both = jnp.where(sub == 5, row(low, 1), both)
            both = jnp.where(sub == 6, row(high, 0), both)
            both = jnp.where(sub == 7, row(high, 1), both)
            rows_ref[z] = both
            odd = sub % 2 == 1
            cur_ref[z] = jnp.where(odd, low, high)
            west_ref[z] = jnp.where(odd, pltpu.roll(low, 1, 0), pltpu.roll(own_high, 7, 0))
            east_ref[z] = jnp.where(odd, pltpu.roll(own_low, 1, 0), pltpu.roll(high, 7, 0))
            here = lane // 4 == z - lo
            shift = (2 + 4 * (z - lo)) % 128
            return (
                jnp.where(here, pltpu.roll(low, shift, 1), packed[0]),
                jnp.where(here, pltpu.roll(high, shift, 1), packed[1]),
            )

        zero = jnp.zeros((8, 128), F32)
        packed = lax.fori_loop(lo, hi, one, (zero, zero), unroll=UNROLL)
        for c in range(4):
            p_ref[half, c, 0:16, :] = p_in[half, c, 0:16, :]
            p_ref[half, c, 16:17, :] = row(packed[0], 2 * c + 1)
            p_ref[half, c, 17:18, :] = row(packed[1], 2 * c)
            p_ref[half, c, 18:24, :] = jnp.zeros((6, 128), F32)

    span = span_mask(fp, first_y, 128)
    rows_ref[...] = dot_nn(rows_ref[...].reshape(nz * 8, 128), span).reshape(nz, 8, 128)

    def add(z, acc):
        return acc + rows_ref[z] * within(z, fp[2:3], DISK_Z)

    acc = lax.fori_loop(0, nz, add, jnp.zeros((8, 128), F32), unroll=WIDE)
    column = jnp.where(sub == 0, -1, 16)
    column = jnp.where(sub == 2, 0, jnp.where(sub == 3, 15, column))
    column = jnp.where(sub >= 4, jnp.where(sub < 6, sub - 6, sub + 10), column)
    acc = acc * within(first_x + column, fp[0:1], DISK_X)
    p_ref[0, 0, 18:19, :] = sums_ref[0:1, :] + jnp.sum(acc[4:8], axis=0, keepdims=True)
    p_ref[1, 0, 18:19, :] = sums_ref[1:2, :] + jnp.sum(acc[0:4], axis=0, keepdims=True)


def steps_kernel(
    f_ref,
    base_ref,
    disks_ref,
    masks_ref,
    cur_ref,
    west_ref,
    east_ref,
    p_ref,
    pa_ref,
    pb_ref,
    fp_ref,
    lap_ref,
    out_ref,
    first_ref,
    first_corner_ref,
    last_ref,
    mid_ref,
    new_ref,
    force_ref,
    rim_force_ref,
    ring_ref,
    edge_ref,
    corner_ref,
    sems,
):
    nz = f_ref.shape[1]
    tile_x = lax.axis_index("gx")
    tile_y = lax.axis_index("gy")
    last_x = lax.axis_size("gx") - 1
    even_y = tile_y % 2 == 0
    first_x = tile_x * 16
    first_y = tile_y * 128
    fp = fp_ref[...]
    fx, fy, fz = fp[0:1], fp[1:2], fp[2:3]
    lane = iota((16, 128), 1)
    sub = iota((16, 128), 0)

    def pick(half, c):
        a, b = pa_ref[half, c], pb_ref[half, c]
        return jnp.where(even_y, b, a), jnp.where(even_y, a, b)

    k24 = iota((24, 128), 1) % 4
    left_cols, right_cols = [], []
    for c in range(4):
        lefts, rights = [], []
        for half in range(2):
            left, right = pick(half, c)
            own = p_ref[half, c]
            lefts.append(jnp.where(k24 < 2, left, own))
            rights.append(jnp.where(k24 < 2, own, right))
            edge = jnp.where(k24 == 1, left, pltpu.roll(right, 126, 1))
            edge_ref[0, half, c] = edge[0:16]
            corner_ref[half, 2 * c + 1 : 2 * c + 2, :] = edge[16:17]
            corner_ref[half, 2 * c : 2 * c + 1, :] = edge[17:18]
        left_cols.append(jnp.concatenate(lefts, axis=1))
        right_cols.append(jnp.concatenate(rights, axis=1))
    def total(half):
        left, right = pick(half, 0)
        return p_ref[half, 0, 18:19, :] + left[18:19] + right[18:19]

    def thrust_of(sums):
        speed = sums * (1.0 / CELLS)
        return -GAIN * DT * speed * jnp.abs(speed)

    thrust1 = thrust_of(total(0))
    k256 = iota((24, 256), 1) % 4

    def facing(cols, mask):
        u, v = cols[0], cols[1]
        cs, cn = upwind(v)
        term = jnp.where(k256 == 1, cn * pltpu.roll(u, 255, 1), cs * pltpu.roll(u, 1, 1))
        term = jnp.concatenate([term, jnp.zeros((8, 256), F32)], axis=0)
        return dot_nn(term, mask)

    faces = facing(left_cols, masks_ref[0]) + facing(right_cols, masks_ref[1])
    sub32 = iota((32, 128), 0)
    column = jnp.where(sub32 == 16, -1, jnp.where(sub32 == 17, 16, sub32))
    mask_x32 = within(first_x + column, fx, DISK_X) * (sub32 < 18).astype(F32)
    faces = jnp.sum(faces * mask_x32, axis=0, keepdims=True)
    pushed = jnp.dot(
        jnp.broadcast_to(thrust1, (8, 128)),
        lap_ref[...],
        precision=lax.Precision.HIGHEST,
        preferred_element_type=F32,
    )
    thrust2 = thrust_of(total(1) + faces + pushed[0:1])

    span = within(first_y + iota((128, 128), 0), fy, DISK_Y)
    disks = disks_ref[...].reshape(nz * 16, 128)

    def dot_disks(mask, weights):
        high = weights.astype(jnp.bfloat16)
        low = (weights - high.astype(F32)).astype(jnp.bfloat16)
        dims = (((1,), (1,)), ((), ()))
        return lax.dot_general(
            mask, high, dims, preferred_element_type=F32
        ) + lax.dot_general(mask, low, dims, preferred_element_type=F32)

    force_ref[0] = dot_disks(disks, span * thrust1).reshape(nz, 16, 128)
    force_ref[1] = dot_disks(disks, span * thrust2).reshape(nz, 16, 128)
    levels = within(iota((nz, 128), 0), fz, DISK_Z).astype(jnp.bfloat16)
    for side, x in ((0, 16), (1, -1)):
        weights = span * (thrust1 * within(first_x + x, fx, DISK_X))
        rim_force_ref[side] = dot_disks(levels, weights)
    by_x1 = within(first_x + sub, fx, DISK_X) * thrust1
    force_cols = dot_nt(by_x1, masks_ref[2])

    lane256 = iota((16, 256), 1)
    sub256 = iota((16, 256), 0)

    def rim_cols(cols):
        cur = [x[0:16] for x in cols]
        c = coefs(cur[0], cur[1], cur[2])
        new = []
        for i in range(4):
            f = cur[i]
            west = jnp.where(sub256 == 0, cols[i][16:17], pltpu.roll(f, 1, 0))
            east = jnp.where(sub256 == 15, cols[i][17:18], pltpu.roll(f, 15, 0))
            south = pltpu.roll(f, 1, 1)
            north = pltpu.roll(f, 255, 1)
            down = jnp.where(lane256 < 4, f, pltpu.roll(f, 4, 1))
            up = jnp.where(lane256 >= 4 * nz - 4, f, pltpu.roll(f, 252, 1))
            new.append(mix(c, f, west, east, south, north, down, up))
        new[0] = new[0] + force_cols
        new[2] = new[2] + (DT * BUOY) * cur[3]
        return new

    left_new, right_new = rim_cols(left_cols), rim_cols(right_cols)
    for c in range(4):
        edge = jnp.where(lane256 % 4 == 1, left_new[c], pltpu.roll(right_new[c], 254, 1))
        edge_ref[1, 0, c] = edge[:, 0:128]
        edge_ref[1, 1, c] = edge[:, 128:256]

    lane8 = iota((8, 128), 1)
    sub8 = iota((8, 128), 0)
    odd = sub8 % 2 == 1

    def rim_rows(z, carry):
        below = jnp.maximum(z - 1, 0)
        above = jnp.minimum(z + 1, nz - 1)
        half = z // 32
        shift = (255 - 4 * (z - 32 * half)) % 128
        cur = cur_ref[z]
        corner = pltpu.roll(corner_ref[half], shift, 1)
        south = jnp.where(lane8 == 0, corner, pltpu.roll(cur, 1, 1))
        north = jnp.where(lane8 == 127, corner, pltpu.roll(cur, 127, 1))
        vel = [jnp.where(odd, cur[2 * i + 1 : 2 * i + 2], cur[2 * i : 2 * i + 1]) for i in range(4)]
        c = coefs(vel[0], vel[1], vel[2])
        new = mix(c, cur, west_ref[z], east_ref[z], south, north, cur_ref[below], cur_ref[above])
        new = new + jnp.where(sub8 // 2 == 2, (DT * BUOY) * vel[3], 0.0)
        new = new + jnp.where(sub8 == 0, rim_force_ref[0, pl.ds(z, 1), :], 0.0)
        new = new + jnp.where(sub8 == 1, rim_force_ref[1, pl.ds(z, 1), :], 0.0)
        ring_ref[z] = jnp.where(odd & (tile_x == 0), cur, new)
        return carry

    lax.fori_loop(0, nz, rim_rows, 0, unroll=WIDE)

    def first_step(group, carry):
        for j in range(WIDE):
            z = group * WIDE + j
            half = z // 32
            shift = (255 - 4 * (z - 32 * half)) % 128
            near = cur_ref[z]
            cw, ce = upwind(f_ref[0, z])
            cs, cn = upwind(f_ref[1, z])
            along_x = jnp.where(sub == 0, cw, jnp.where(sub == 15, ce, 0.0))
            along_y = jnp.where(lane == 0, cs, jnp.where(lane == 127, cn, 0.0))
            for i in range(4):
                beside = jnp.where(sub < 8, near[2 * i + 1 : 2 * i + 2], near[2 * i : 2 * i + 1])
                edge = pltpu.roll(edge_ref[0, half, i], shift, 1)
                new = base_ref[i, z] + along_x * beside + along_y * edge
                if i == 0:
                    new = new + force_ref[0, z]
                mid_ref[i, z] = new
        return carry

    def level(z):
        below = jnp.maximum(z - 1, 0)
        above = jnp.minimum(z + 1, nz - 1)
        half = z // 32
        shift = (255 - 4 * (z - 32 * half)) % 128
        cur = [mid_ref[c, z] for c in range(4)]
        ring = ring_ref[z]
        c = coefs(cur[0], cur[1], cur[2])
        for i in range(4):
            f = cur[i]
            west = jnp.where(sub == 0, ring[2 * i + 1 : 2 * i + 2], pltpu.roll(f, 1, 0))
            outside = jnp.where(tile_x == last_x, f[15:16], ring[2 * i : 2 * i + 1])
            east = jnp.where(sub == 15, outside, pltpu.roll(f, 15, 0))
            edge = pltpu.roll(edge_ref[1, half, i], shift, 1)
            south = jnp.where(lane == 0, edge, pltpu.roll(f, 1, 1))
            north = jnp.where(lane == 127, edge, pltpu.roll(f, 127, 1))
            new = mix(c, f, west, east, south, north, mid_ref[i, below], mid_ref[i, above])
            if i == 0:
                new = new + force_ref[1, z]
            if i == 2:
                new = new + (DT * BUOY) * cur[3]
            new_ref[i, z] = new

    def send(chunk):
        part = pl.ds(chunk * CHUNK, CHUNK)
        return pltpu.make_async_copy(new_ref.at[:, part], out_ref.at[:, part], sems.at[chunk])

    def second_step(group, carry):
        for i in range(WIDE):
            z = group * WIDE + i
            level(z)
            if i % CHUNK == CHUNK - 1:
                send(group * (WIDE // CHUNK) + i // CHUNK).start()
        return carry

    lax.fori_loop(0, nz // WIDE, first_step, 0)
    lax.fori_loop(0, nz // WIDE, second_step, 0)

    @pl.when(tile_x == 0)
    def _():
        for c in range(4):
            first_ref[:, 2 * c : 2 * c + 2, :] = mid_ref[c, :, 0:2, :]
            last_ref[:, 2 * c : 2 * c + 2, :] = new_ref[c, :, 0:2, :]
            for half in range(2):
                first_corner_ref[half, 2 * c : 2 * c + 1, :] = edge_ref[1, half, c, 0:1, :]
                first_corner_ref[half, 2 * c + 1 : 2 * c + 2, :] = edge_ref[0, half, c, 0:1, :]

    for chunk in range(nz // CHUNK):
        send(chunk).wait()


def fix_kernel(
    out_in, in_ref, sb_ref, first_ref, corner_ref, last_ref, out_ref, inlet, new, wide, done, sems
):
    nz = first_ref.shape[0]
    lane = iota((8, 128), 1)
    sub = iota((8, 128), 0)
    is_even = sub % 2 == 0


    def send(group):
        part = pl.ds(group * WIDE, WIDE)
        return [
            pltpu.make_async_copy(
                done.at[part, pl.ds(2 * c, 2), :], out_ref.at[c, part, pl.ds(0, 2), :], sems.at[group, c]
            )
            for c in range(4)
        ]

    @pl.when(lax.axis_index("gx") == 0)
    def _():
        inlet[...] = jnp.zeros_like(inlet)
        for c in range(4):
            for z in range(nz):
                inlet[z, 2 * c : 2 * c + 1, :] = in_ref[c, z : z + 1, :]
        for half in range(2):
            old = corner_ref[half]
            push = upwind(old[1:2])[0]
            for c in range(4):
                msg = in_ref[c, nz + half : nz + half + 1, :]
                side = jnp.where(
                    lane[0:1] % 4 == 1, pltpu.roll(msg, 1, 1), pltpu.roll(msg, 127, 1)
                )
                wide[half, 2 * c : 2 * c + 1, :] = old[2 * c : 2 * c + 1] + push * side
                wide[half, 2 * c + 1 : 2 * c + 2, :] = jnp.zeros((1, 128), F32)

        def first(group, carry):
            for i in range(WIDE):
                z = group * WIDE + i
                push = upwind(sb_ref[z, 0:1, :])[0]
                new[z] = first_ref[z] + jnp.where(is_even, push * inlet[z], 0.0)
            return carry

        lax.fori_loop(0, nz // WIDE, first, 0)

        def second(group, carry):
            for i in range(WIDE):
                z = group * WIDE + i
                below = jnp.maximum(z - 1, 0)
                above = jnp.minimum(z + 1, nz - 1)
                half = z // 32
                shift = (255 - 4 * (z - 32 * half)) % 128
                cur = new[z]
                east = pltpu.roll(cur, 7, 0)
                corner = pltpu.roll(wide[half], shift, 1)
                south = jnp.where(lane == 0, corner, pltpu.roll(cur, 1, 1))
                north = jnp.where(lane == 127, corner, pltpu.roll(cur, 127, 1))
                c = coefs(cur[0:1], cur[2:3], cur[4:5])
                zero = mix(c, cur, inlet[z], east, south, north, new[below], new[above])
                zero = zero + jnp.where(sub == 4, (DT * BUOY) * cur[6:7], 0.0)
                delta = pltpu.roll(cur - first_ref[z], 1, 0)
                one = last_ref[z] + upwind(cur[1:2])[0] * delta
                done[z] = jnp.where(is_even, zero, one)
            for copy in send(group):
                copy.start()
            return carry

        lax.fori_loop(0, nz // WIDE, second, 0)
        for group in range(nz // WIDE):
            for copy in send(group):
                copy.wait()


VMEM = pl.BlockSpec(memory_space=pltpu.VMEM)
ANY = pl.BlockSpec(memory_space=pl.ANY)
SMEM = pl.BlockSpec(memory_space=pltpu.SMEM)
HBM = pl.BlockSpec(memory_space=pltpu.HBM)


def call(kernel, out, scratch=(), aliases=None, ins=None, outs=None, flops=1 << 20):
    specs = {}
    if ins is not None:
        specs["in_specs"] = ins
    if outs is not None:
        specs["out_specs"] = outs
    return pl.pallas_call(
        kernel,
        out_shape=out,
        scratch_shapes=scratch,
        input_output_aliases=aliases or {},
        compiler_params=pltpu.CompilerParams(vmem_limit_bytes=24 << 20),
        cost_estimate=pl.CostEstimate(flops=flops, bytes_accessed=1 << 20, transcendentals=0),
        **specs,
    )


def row_of(place):
    for one, two in TRADES:
        if place in (one, two):
            return one + two - place
    return place


def send_inlet(msg, after, count_x, count_y):
    heard = {}
    for m in (2, 3, 1, 0):
        moves = [
            (row_of(GROUP * m + j % GROUP) * count_y + j, j)
            for j in range(count_y)
            if GROUP * m + j % GROUP
        ]
        if m == 0:
            sent, *_ = lax.optimization_barrier((msg, *after))
        else:
            sent = msg
        heard[m] = lax.ppermute(sent, ("gx", "gy"), moves)
    return [heard[m] for m in range(4)]


def share_inlet(msg, heard, code, count_y):
    heard[0] = jnp.where(lax.axis_index("gy") % GROUP == 0, msg, heard[0])

    def pick(k):
        out = heard[0]
        for m in range(1, len(heard)):
            out = jnp.where(code[k] & 7 == m, heard[m], out)
        return out

    core = lax.ppermute(
        jnp.concatenate([pick(1), pick(3)]), "gy", [(j, j ^ 1) for j in range(count_y)]
    )
    mine = jnp.where(code[0] & 8 != 0, pick(0), core[0:4])
    theirs = jnp.where(code[2] & 8 != 0, pick(2), core[4:8])
    other = lax.ppermute(theirs, "gy", [(j, j ^ 2) for j in range(count_y)])
    return jnp.where(code[0] & 16 != 0, mine, other)


def body(flow_state, inflow, footprint, block_map):
    levels = flow_state.shape[1]
    count_x = lax.axis_size("gx")
    count_y = lax.axis_size("gy")
    turbines = footprint.shape[0]
    shape = lambda *s: jax.ShapeDtypeStruct(s, F32)
    x_pack = shape(levels, 8, 128)
    y_pack = shape(2, 4, 24, 128)

    send_a, send_b = call(
        pack_x_kernel, (x_pack, x_pack), [pltpu.SemaphoreType.DMA((4, 2))], ins=[HBM], outs=[VMEM] * 2
    )(flow_state)
    recv_a = lax.ppermute(send_a, "gx", pairs(count_x, False))
    recv_b = lax.ppermute(send_b, ("gx", "gy"), pairs_inside(count_x, count_y))

    late, _ = lax.optimization_barrier((footprint, send_a))
    fp = jnp.pad(late.T, ((0, 5), (0, 128 - turbines)), constant_values=FAR)
    lap = jnp.ones((128, 128), F32)
    for i, extent in enumerate((DISK_X, DISK_Y, DISK_Z)):
        lap = lap * jnp.maximum(extent - jnp.abs(fp[i][:, None] - fp[i][None, :]), 0).astype(F32)
    live = jnp.arange(128) < turbines
    lap = jnp.where(live[:, None] & live[None, :], lap, 0.0)

    own = call(pack_y_kernel, y_pack, flops=PACK_COST)(flow_state, send_a)
    msg, code = call(
        pack_inlet_kernel,
        (shape(4, levels + 8, 128), jax.ShapeDtypeStruct((GROUP, levels + 8, 128), jnp.int32)),
        ins=[SMEM, VMEM, VMEM],
    )(block_map, inflow, own)
    base, disks, masks, sums = call(
        base_kernel,
        (
            shape(*flow_state.shape),
            jax.ShapeDtypeStruct((levels, 16, 128), jnp.bfloat16),
            jax.ShapeDtypeStruct((3, 256, 128), jnp.bfloat16),
            shape(8, 128),
        ),
        [pltpu.VMEM((2, levels, 16, 128), F32)],
        flops=TILE_COST,
    )(flow_state, fp)
    heard = send_inlet(msg, (recv_b, sums), count_x, count_y)

    own, near, west, east = call(
        rim_kernel, (y_pack, x_pack, x_pack, x_pack), [pltpu.VMEM((levels, 8, 128), F32)] * 3
    )(send_a, send_b, recv_a, recv_b, fp, sums, own)
    side_a = lax.ppermute(own, "gy", pairs(count_y, False))
    side_b = lax.ppermute(own, "gy", pairs(count_y, True))
    *heard, _ = lax.optimization_barrier((*heard, side_b))
    inlet = share_inlet(msg, list(heard), code, count_y)
    out, first, corner, last = call(
        steps_kernel,
        (shape(*flow_state.shape), x_pack, shape(2, 8, 128), x_pack),
        [
            pltpu.VMEM(flow_state.shape, F32),
            pltpu.VMEM(flow_state.shape, F32),
            pltpu.VMEM((2, levels, 16, 128), F32),
            pltpu.VMEM((2, levels, 128), F32),
            pltpu.VMEM((levels, 8, 128), F32),
            pltpu.VMEM((2, 2, 4, 16, 128), F32),
            pltpu.VMEM((2, 8, 128), F32),
            pltpu.SemaphoreType.DMA((levels // CHUNK,)),
        ],
        outs=[ANY, VMEM, VMEM, VMEM],
        flops=STEPS_COST,
    )(flow_state, base, disks, masks, near, west, east, own, side_a, side_b, fp, lap)
    return call(
        fix_kernel,
        shape(*flow_state.shape),
        [
            pltpu.VMEM((levels, 8, 128), F32),
            pltpu.VMEM((levels, 8, 128), F32),
            pltpu.VMEM((2, 8, 128), F32),
            pltpu.VMEM((levels, 8, 128), F32),
            pltpu.SemaphoreType.DMA((levels // WIDE, 4)),
        ],
        aliases={0: 0},
        ins=[ANY, VMEM, VMEM, VMEM, VMEM, VMEM],
        outs=ANY,
    )(out, inlet, send_b, first, corner, last)


def solution(mesh):
    placed = (P(None, None, "gx", "gy"), P(None, None, "gx"), P(), P())
    return jax.shard_map(
        body, mesh=mesh, in_specs=placed, out_specs=P(None, None, "gx", "gy"), check_vma=False
    )
```

```python
import jax
import jax.numpy as jnp
from jax import lax
from jax.experimental import pallas as pl
from jax.experimental.pallas import tpu as pltpu
from jax.sharding import PartitionSpec as P

DISK_X = 2
DISK_Y = 24
DISK_Z = 24
CELLS = float(DISK_X * DISK_Y * DISK_Z)

DT = 0.15
VISC = 0.3
BUOY = 0.3
GAIN = 2.0
BASE = DT * VISC
FAR = -100000
F32 = jnp.float32
UNROLL = 16
WIDE = 48
TRADES = ((2, 5), (3, 13))
CHUNK = 8
GROUP = 4
TILE_COST = 1 << 20
PACK_COST = 1 << 33
STEPS_COST = 1 << 32


def pairs(n, odd):
    if not odd:
        return [(i, i ^ 1) for i in range(n)]
    return [(i, (i + 1) % n if i % 2 else (i - 1) % n) for i in range(n)]


def pairs_inside(nx, ny):
    out = []
    for i in range(nx):
        for j in range(ny):
            if i in (0, nx - 1):
                to = (i, j ^ 1)
            else:
                to = (i + 1 if i % 2 else i - 1, j)
            out.append((i * ny + j, to[0] * ny + to[1]))
    return out


def upwind(vel):
    scaled = DT * vel
    return jnp.maximum(scaled, 0.0) + BASE, BASE - jnp.minimum(scaled, 0.0)


def coefs(u, v, w):
    cw, ce = upwind(u)
    cs, cn = upwind(v)
    cb, ca = upwind(w)
    c0 = 1.0 - ((cw + ce) + (cs + cn) + (cb + ca))
    return c0, cw, ce, cs, cn, cb, ca


def mix(c, f, w, e, s, n, b, a):
    return c[0] * f + c[1] * w + c[2] * e + c[3] * s + c[4] * n + c[5] * b + c[6] * a


def dot_nt(a, m):
    high = a.astype(jnp.bfloat16)
    low = (a - high.astype(F32)).astype(jnp.bfloat16)
    dims = (((1,), (1,)), ((), ()))
    return lax.dot_general(high, m, dims, preferred_element_type=F32) + lax.dot_general(
        low, m, dims, preferred_element_type=F32
    )


def dot_nn(a, m):
    high = a.astype(jnp.bfloat16)
    low = (a - high.astype(F32)).astype(jnp.bfloat16)
    return jnp.dot(high, m, preferred_element_type=F32) + jnp.dot(
        low, m, preferred_element_type=F32
    )


def iota(shape, dim):
    return lax.broadcasted_iota(jnp.int32, shape, dim)


def within(cells, start, extent):
    return ((cells >= start) & (cells < start + extent)).astype(F32)


def span_mask(fp, first, count):
    return within(first + iota((count, 128), 0), fp[1:2], DISK_Y).astype(jnp.bfloat16)


def pack_x_kernel(f_ref, a_ref, b_ref, sems):
    even = lax.axis_index("gx") % 2 == 0
    first_a = jnp.where(even, 14, 0)
    first_b = jnp.where(even, 0, 14)
    copies = []
    for c in range(4):
        for i, (first, ref) in enumerate(((first_a, a_ref), (first_b, b_ref))):
            copies.append(
                pltpu.make_async_copy(
                    f_ref.at[c, :, pl.ds(first, 2), :],
                    ref.at[:, pl.ds(2 * c, 2), :],
                    sems.at[c, i],
                )
            )
    for copy in copies:
        copy.start()
    for copy in copies:
        copy.wait()


def pack_inlet_kernel(map_ref, in_ref, after_ref, msg_ref, code_ref):
    nz = in_ref.shape[1]
    lane = iota((1, 128), 1)
    for c in range(4):
        msg_ref[c, 0:nz, :] = in_ref[c]
        msg_ref[c, nz : nz + 8, :] = jnp.zeros((8, 128), F32)
        for half in range(2):
            packed = jnp.zeros((1, 128), F32)
            for z in range(half * 32, min(nz, half * 32 + 32)):
                at = z - half * 32
                moved = pltpu.roll(in_ref[c, z : z + 1, :], (4 * at + 1) % 128, 1)
                packed = jnp.where(lane // 4 == at, moved, packed)
            msg_ref[c, nz + half : nz + half + 1, :] = packed

    tile_y = lax.axis_index("gy")
    count = lax.axis_size("gy")
    place = tile_y % GROUP
    level = iota((nz + 8, 128), 0)
    first = iota((nz + 8, 128), 1) % 4 == 0
    for k in range(GROUP):
        column = tile_y // GROUP * GROUP + (place ^ k)
        own = map_ref[column]
        left = map_ref[(column + count - 1) % count]
        right = map_ref[(column + 1) % count]
        source = jnp.where(level < nz, own, jnp.where(first, left, right))
        moved = source
        for one, two in TRADES:
            moved = jnp.where(source == one, two, jnp.where(source == two, one, moved))
        source = moved
        code = source // GROUP
        code = code + jnp.where(source % GROUP == place, 8, 0)
        code_ref[k] = code + jnp.where(source % GROUP // 2 == place // 2, 16, 0)


def pack_y_kernel(f_ref, after_ref, p_ref):
    nz = f_ref.shape[1]
    lane = iota((16, 128), 1)
    p_ref[...] = jnp.zeros_like(p_ref)
    for half in range(2):
        lo, hi = half * 32, min(nz, half * 32 + 32)

        def one(z, packed):
            here = lane // 4 == z - lo
            shift = (2 + 4 * (z - lo)) % 128
            return tuple(
                jnp.where(here, pltpu.roll(f_ref[i, z], shift, 1), packed[i]) for i in range(4)
            )

        zero = jnp.zeros((16, 128), F32)
        packed = lax.fori_loop(lo, hi, one, (zero,) * 4, unroll=UNROLL)
        for i in range(4):
            p_ref[half, i, 0:16, :] = packed[i]


def base_kernel(f_ref, fp_ref, base_ref, disks_ref, masks_ref, sums_ref, rows_ref):
    nz = f_ref.shape[1]
    first_x = lax.axis_index("gx") * 16
    first_y = lax.axis_index("gy") * 128
    fp = fp_ref[...]
    lane = iota((16, 128), 1)
    sub = iota((16, 128), 0)
    mask_x = within(first_x + sub, fp[0:1], DISK_X)

    def one(z, carry):
        below = jnp.maximum(z - 1, 0)
        above = jnp.minimum(z + 1, nz - 1)
        cur = [f_ref[c, z] for c in range(4)]
        c = coefs(cur[0], cur[1], cur[2])
        cw = jnp.where(sub == 0, 0.0, c[1])
        ce = jnp.where(sub == 15, 0.0, c[2])
        cs = jnp.where(lane == 0, 0.0, c[3])
        cn = jnp.where(lane == 127, 0.0, c[4])
        c = (c[0], cw, ce, cs, cn, c[5], c[6])
        for i in range(4):
            f = cur[i]
            new = mix(
                c,
                f,
                pltpu.roll(f, 1, 0),
                pltpu.roll(f, 15, 0),
                pltpu.roll(f, 1, 1),
                pltpu.roll(f, 127, 1),
                f_ref[i, below],
                f_ref[i, above],
            )
            if i == 2:
                new = new + (DT * BUOY) * cur[3]
            base_ref[i, z] = new
        disks_ref[z] = (mask_x * within(z, fp[2:3], DISK_Z)).astype(jnp.bfloat16)
        return carry

    lax.fori_loop(0, nz, one, 0, unroll=WIDE)
    span = span_mask(fp, first_y, 128)
    rows_ref[0] = dot_nn(f_ref[0].reshape(nz * 16, 128), span).reshape(nz, 16, 128)
    rows_ref[1] = dot_nn(base_ref[0].reshape(nz * 16, 128), span).reshape(nz, 16, 128)

    def add(z, acc):
        mask = within(z, fp[2:3], DISK_Z)
        return acc[0] + rows_ref[0, z] * mask, acc[1] + rows_ref[1, z] * mask

    zero = jnp.zeros((16, 128), F32)
    acc = lax.fori_loop(0, nz, add, (zero, zero), unroll=WIDE)
    sums_ref[0:1, :] = jnp.sum(acc[0] * mask_x, axis=0, keepdims=True)
    sums_ref[1:2, :] = jnp.sum(acc[1] * mask_x, axis=0, keepdims=True)
    sums_ref[2:8, :] = jnp.zeros((6, 128), F32)

    fy, fz = fp[1:2], fp[2:3]
    all_y = lax.axis_size("gy") * 128
    at = iota((256, 128), 0)
    level = at // 4
    k_at = at % 4
    mask_level = within(level, fz, DISK_Z) * (level < nz).astype(F32)
    y_left = jnp.where(k_at == 1, jnp.where(first_y == 0, all_y - 1, first_y - 1), first_y)
    y_right = jnp.where(
        k_at == 1, first_y + 127, jnp.where(first_y + 128 == all_y, 0, first_y + 128)
    )
    middle = ((k_at == 1) | (k_at == 2)).astype(F32)
    mask_left = mask_level * within(y_left, fy, DISK_Y) * middle
    mask_right = mask_level * within(y_right, fy, DISK_Y) * middle
    y_cols = jnp.where(k_at == 1, y_left, y_right)
    mask_cols = mask_level * within(y_cols, fy, DISK_Y) * middle
    for i, mask in enumerate((mask_left, mask_right, mask_cols)):
        masks_ref[i] = mask.astype(jnp.bfloat16)


def rim_kernel(
    sa_ref,
    sb_ref,
    ra_ref,
    rb_ref,
    fp_ref,
    sums_ref,
    p_in,
    p_ref,
    cur_ref,
    west_ref,
    east_ref,
    hl_ref,
    hh_ref,
    rows_ref,
):
    nz = hl_ref.shape[0]
    tile_x = lax.axis_index("gx")
    last_x = lax.axis_size("gx") - 1
    even = tile_x % 2 == 0
    first_x = tile_x * 16
    first_y = lax.axis_index("gy") * 128
    fp = fp_ref[...]
    lane = iota((8, 128), 1)
    sub = iota((8, 128), 0)

    @pl.when(even)
    def _():
        hl_ref[...] = rb_ref[...]
        hh_ref[...] = ra_ref[...]

    @pl.when(jnp.logical_not(even))
    def _():
        hl_ref[...] = ra_ref[...]
        hh_ref[...] = rb_ref[...]

    @pl.when(tile_x == 0)
    def _():
        hl_ref[...] = jnp.zeros_like(hl_ref)

    @pl.when(tile_x == last_x)
    def _():
        for z in range(nz):
            hh_ref[z] = pltpu.roll(sb_ref[z], 7, 0)

    def row(x, i):
        return x[i : i + 1]

    for half in range(2):
        lo, hi = half * 32, min(nz, half * 32 + 32)

        def one(z, packed):
            below = jnp.maximum(z - 1, 0)
            above = jnp.minimum(z + 1, nz - 1)
            own_a, own_b = sa_ref[z], sb_ref[z]
            own_low = jnp.where(even, own_b, own_a)
            own_high = jnp.where(even, own_a, own_b)
            low, high = hl_ref[z], hh_ref[z]
            u_low = jnp.where(sub == 0, row(low, 1), row(high, 0))
            v_low = jnp.where(sub == 0, row(low, 3), row(high, 2))
            w_low = jnp.where(sub == 0, row(low, 5), row(high, 4))
            west = jnp.where(sub == 0, row(low, 0), row(own_high, 1))
            east = jnp.where(sub == 0, row(own_low, 0), row(high, 1))
            down = jnp.where(sub == 0, row(hl_ref[below], 1), row(hh_ref[below], 0))
            up = jnp.where(sub == 0, row(hl_ref[above], 1), row(hh_ref[above], 0))
            south = jnp.where(lane == 0, 0.0, pltpu.roll(u_low, 1, 1))
            north = jnp.where(lane == 127, 0.0, pltpu.roll(u_low, 127, 1))
            ring = mix(coefs(u_low, v_low, w_low), u_low, west, east, south, north, down, up)
            into_low = upwind(row(own_low, 0))[0] * row(low, 1)
            into_high = upwind(row(own_high, 1))[1] * row(high, 0)
            both = jnp.where(sub == 2, into_low, jnp.where(sub == 3, into_high, ring))
            both = jnp.where(sub == 4, row(low, 0), both)
            both = jnp.where(sub == 5, row(low, 1), both)
            both = jnp.where(sub == 6, row(high, 0), both)
            both = jnp.where(sub == 7, row(high, 1), both)
            rows_ref[z] = both
            odd = sub % 2 == 1
            cur_ref[z] = jnp.where(odd, low, high)
            west_ref[z] = jnp.where(odd, pltpu.roll(low, 1, 0), pltpu.roll(own_high, 7, 0))
            east_ref[z] = jnp.where(odd, pltpu.roll(own_low, 1, 0), pltpu.roll(high, 7, 0))
            here = lane // 4 == z - lo
            shift = (2 + 4 * (z - lo)) % 128
            return (
                jnp.where(here, pltpu.roll(low, shift, 1), packed[0]),
                jnp.where(here, pltpu.roll(high, shift, 1), packed[1]),
            )

        zero = jnp.zeros((8, 128), F32)
        packed = lax.fori_loop(lo, hi, one, (zero, zero), unroll=UNROLL)
        for c in range(4):
            p_ref[half, c, 0:16, :] = p_in[half, c, 0:16, :]
            p_ref[half, c, 16:17, :] = row(packed[0], 2 * c + 1)
            p_ref[half, c, 17:18, :] = row(packed[1], 2 * c)
            p_ref[half, c, 18:24, :] = jnp.zeros((6, 128), F32)

    span = span_mask(fp, first_y, 128)
    rows_ref[...] = dot_nn(rows_ref[...].reshape(nz * 8, 128), span).reshape(nz, 8, 128)

    def add(z, acc):
        return acc + rows_ref[z] * within(z, fp[2:3], DISK_Z)

    acc = lax.fori_loop(0, nz, add, jnp.zeros((8, 128), F32), unroll=WIDE)
    column = jnp.where(sub == 0, -1, 16)
    column = jnp.where(sub == 2, 0, jnp.where(sub == 3, 15, column))
    column = jnp.where(sub >= 4, jnp.where(sub < 6, sub - 6, sub + 10), column)
    acc = acc * within(first_x + column, fp[0:1], DISK_X)
    p_ref[0, 0, 18:19, :] = sums_ref[0:1, :] + jnp.sum(acc[4:8], axis=0, keepdims=True)
    p_ref[1, 0, 18:19, :] = sums_ref[1:2, :] + jnp.sum(acc[0:4], axis=0, keepdims=True)


def steps_kernel(
    f_ref,
    base_ref,
    disks_ref,
    masks_ref,
    cur_ref,
    west_ref,
    east_ref,
    p_ref,
    pa_ref,
    pb_ref,
    fp_ref,
    lap_ref,
    out_ref,
    first_ref,
    first_corner_ref,
    last_ref,
    mid_ref,
    new_ref,
    force_ref,
    rim_force_ref,
    ring_ref,
    edge_ref,
    corner_ref,
    sems,
):
    nz = f_ref.shape[1]
    tile_x = lax.axis_index("gx")
    tile_y = lax.axis_index("gy")
    last_x = lax.axis_size("gx") - 1
    even_y = tile_y % 2 == 0
    first_x = tile_x * 16
    first_y = tile_y * 128
    fp = fp_ref[...]
    fx, fy, fz = fp[0:1], fp[1:2], fp[2:3]
    lane = iota((16, 128), 1)
    sub = iota((16, 128), 0)

    def pick(half, c):
        a, b = pa_ref[half, c], pb_ref[half, c]
        return jnp.where(even_y, b, a), jnp.where(even_y, a, b)

    k24 = iota((24, 128), 1) % 4
    left_cols, right_cols = [], []
    for c in range(4):
        lefts, rights = [], []
        for half in range(2):
            left, right = pick(half, c)
            own = p_ref[half, c]
            lefts.append(jnp.where(k24 < 2, left, own))
            rights.append(jnp.where(k24 < 2, own, right))
            edge = jnp.where(k24 == 1, left, pltpu.roll(right, 126, 1))
            edge_ref[0, half, c] = edge[0:16]
            corner_ref[half, 2 * c + 1 : 2 * c + 2, :] = edge[16:17]
            corner_ref[half, 2 * c : 2 * c + 1, :] = edge[17:18]
        left_cols.append(jnp.concatenate(lefts, axis=1))
        right_cols.append(jnp.concatenate(rights, axis=1))
    def total(half):
        left, right = pick(half, 0)
        return p_ref[half, 0, 18:19, :] + left[18:19] + right[18:19]

    def thrust_of(sums):
        speed = sums * (1.0 / CELLS)
        return -GAIN * DT * speed * jnp.abs(speed)

    thrust1 = thrust_of(total(0))
    k256 = iota((24, 256), 1) % 4

    def facing(cols, mask):
        u, v = cols[0], cols[1]
        cs, cn = upwind(v)
        term = jnp.where(k256 == 1, cn * pltpu.roll(u, 255, 1), cs * pltpu.roll(u, 1, 1))
        term = jnp.concatenate([term, jnp.zeros((8, 256), F32)], axis=0)
        return dot_nn(term, mask)

    faces = facing(left_cols, masks_ref[0]) + facing(right_cols, masks_ref[1])
    sub32 = iota((32, 128), 0)
    column = jnp.where(sub32 == 16, -1, jnp.where(sub32 == 17, 16, sub32))
    mask_x32 = within(first_x + column, fx, DISK_X) * (sub32 < 18).astype(F32)
    faces = jnp.sum(faces * mask_x32, axis=0, keepdims=True)
    pushed = jnp.dot(
        jnp.broadcast_to(thrust1, (8, 128)),
        lap_ref[...],
        precision=lax.Precision.HIGHEST,
        preferred_element_type=F32,
    )
    thrust2 = thrust_of(total(1) + faces + pushed[0:1])

    span = within(first_y + iota((128, 128), 0), fy, DISK_Y)
    disks = disks_ref[...].reshape(nz * 16, 128)

    def dot_disks(mask, weights):
        high = weights.astype(jnp.bfloat16)
        low = (weights - high.astype(F32)).astype(jnp.bfloat16)
        dims = (((1,), (1,)), ((), ()))
        return lax.dot_general(
            mask, high, dims, preferred_element_type=F32
        ) + lax.dot_general(mask, low, dims, preferred_element_type=F32)

    force_ref[0] = dot_disks(disks, span * thrust1).reshape(nz, 16, 128)
    force_ref[1] = dot_disks(disks, span * thrust2).reshape(nz, 16, 128)
    levels = within(iota((nz, 128), 0), fz, DISK_Z).astype(jnp.bfloat16)
    for side, x in ((0, 16), (1, -1)):
        weights = span * (thrust1 * within(first_x + x, fx, DISK_X))
        rim_force_ref[side] = dot_disks(levels, weights)
    by_x1 = within(first_x + sub, fx, DISK_X) * thrust1
    force_cols = dot_nt(by_x1, masks_ref[2])

    lane256 = iota((16, 256), 1)
    sub256 = iota((16, 256), 0)

    def rim_cols(cols):
        cur = [x[0:16] for x in cols]
        c = coefs(cur[0], cur[1], cur[2])
        new = []
        for i in range(4):
            f = cur[i]
            west = jnp.where(sub256 == 0, cols[i][16:17], pltpu.roll(f, 1, 0))
            east = jnp.where(sub256 == 15, cols[i][17:18], pltpu.roll(f, 15, 0))
            south = pltpu.roll(f, 1, 1)
            north = pltpu.roll(f, 255, 1)
            down = jnp.where(lane256 < 4, f, pltpu.roll(f, 4, 1))
            up = jnp.where(lane256 >= 4 * nz - 4, f, pltpu.roll(f, 252, 1))
            new.append(mix(c, f, west, east, south, north, down, up))
        new[0] = new[0] + force_cols
        new[2] = new[2] + (DT * BUOY) * cur[3]
        return new

    left_new, right_new = rim_cols(left_cols), rim_cols(right_cols)
    for c in range(4):
        edge = jnp.where(lane256 % 4 == 1, left_new[c], pltpu.roll(right_new[c], 254, 1))
        edge_ref[1, 0, c] = edge[:, 0:128]
        edge_ref[1, 1, c] = edge[:, 128:256]

    lane8 = iota((8, 128), 1)
    sub8 = iota((8, 128), 0)
    odd = sub8 % 2 == 1

    def rim_rows(z, carry):
        below = jnp.maximum(z - 1, 0)
        above = jnp.minimum(z + 1, nz - 1)
        half = z // 32
        shift = (255 - 4 * (z - 32 * half)) % 128
        cur = cur_ref[z]
        corner = pltpu.roll(corner_ref[half], shift, 1)
        south = jnp.where(lane8 == 0, corner, pltpu.roll(cur, 1, 1))
        north = jnp.where(lane8 == 127, corner, pltpu.roll(cur, 127, 1))
        vel = [jnp.where(odd, cur[2 * i + 1 : 2 * i + 2], cur[2 * i : 2 * i + 1]) for i in range(4)]
        c = coefs(vel[0], vel[1], vel[2])
        new = mix(c, cur, west_ref[z], east_ref[z], south, north, cur_ref[below], cur_ref[above])
        new = new + jnp.where(sub8 // 2 == 2, (DT * BUOY) * vel[3], 0.0)
        new = new + jnp.where(sub8 == 0, rim_force_ref[0, pl.ds(z, 1), :], 0.0)
        new = new + jnp.where(sub8 == 1, rim_force_ref[1, pl.ds(z, 1), :], 0.0)
        ring_ref[z] = jnp.where(odd & (tile_x == 0), cur, new)
        return carry

    lax.fori_loop(0, nz, rim_rows, 0, unroll=WIDE)

    def first_step(group, carry):
        for j in range(WIDE):
            z = group * WIDE + j
            half = z // 32
            shift = (255 - 4 * (z - 32 * half)) % 128
            near = cur_ref[z]
            cw, ce = upwind(f_ref[0, z])
            cs, cn = upwind(f_ref[1, z])
            along_x = jnp.where(sub == 0, cw, jnp.where(sub == 15, ce, 0.0))
            along_y = jnp.where(lane == 0, cs, jnp.where(lane == 127, cn, 0.0))
            for i in range(4):
                beside = jnp.where(sub < 8, near[2 * i + 1 : 2 * i + 2], near[2 * i : 2 * i + 1])
                edge = pltpu.roll(edge_ref[0, half, i], shift, 1)
                new = base_ref[i, z] + along_x * beside + along_y * edge
                if i == 0:
                    new = new + force_ref[0, z]
                mid_ref[i, z] = new
        return carry

    def level(z):
        below = jnp.maximum(z - 1, 0)
        above = jnp.minimum(z + 1, nz - 1)
        half = z // 32
        shift = (255 - 4 * (z - 32 * half)) % 128
        cur = [mid_ref[c, z] for c in range(4)]
        ring = ring_ref[z]
        c = coefs(cur[0], cur[1], cur[2])
        for i in range(4):
            f = cur[i]
            west = jnp.where(sub == 0, ring[2 * i + 1 : 2 * i + 2], pltpu.roll(f, 1, 0))
            outside = jnp.where(tile_x == last_x, f[15:16], ring[2 * i : 2 * i + 1])
            east = jnp.where(sub == 15, outside, pltpu.roll(f, 15, 0))
            edge = pltpu.roll(edge_ref[1, half, i], shift, 1)
            south = jnp.where(lane == 0, edge, pltpu.roll(f, 1, 1))
            north = jnp.where(lane == 127, edge, pltpu.roll(f, 127, 1))
            new = mix(c, f, west, east, south, north, mid_ref[i, below], mid_ref[i, above])
            if i == 0:
                new = new + force_ref[1, z]
            if i == 2:
                new = new + (DT * BUOY) * cur[3]
            new_ref[i, z] = new

    def send(chunk):
        part = pl.ds(chunk * CHUNK, CHUNK)
        return pltpu.make_async_copy(new_ref.at[:, part], out_ref.at[:, part], sems.at[chunk])

    def second_step(group, carry):
        for i in range(WIDE):
            z = group * WIDE + i
            level(z)
            if i % CHUNK == CHUNK - 1:
                send(group * (WIDE // CHUNK) + i // CHUNK).start()
        return carry

    lax.fori_loop(0, nz // WIDE, first_step, 0)
    lax.fori_loop(0, nz // WIDE, second_step, 0)

    @pl.when(tile_x == 0)
    def _():
        for c in range(4):
            first_ref[:, 2 * c : 2 * c + 2, :] = mid_ref[c, :, 0:2, :]
            last_ref[:, 2 * c : 2 * c + 2, :] = new_ref[c, :, 0:2, :]
            for half in range(2):
                first_corner_ref[half, 2 * c : 2 * c + 1, :] = edge_ref[1, half, c, 0:1, :]
                first_corner_ref[half, 2 * c + 1 : 2 * c + 2, :] = edge_ref[0, half, c, 0:1, :]

    for chunk in range(nz // CHUNK):
        send(chunk).wait()


def fix_kernel(
    out_in, in_ref, sb_ref, first_ref, corner_ref, last_ref, out_ref, inlet, new, wide, done, sems
):
    nz = first_ref.shape[0]
    lane = iota((8, 128), 1)
    sub = iota((8, 128), 0)
    is_even = sub % 2 == 0


    def send(group):
        part = pl.ds(group * WIDE, WIDE)
        return [
            pltpu.make_async_copy(
                done.at[part, pl.ds(2 * c, 2), :], out_ref.at[c, part, pl.ds(0, 2), :], sems.at[group, c]
            )
            for c in range(4)
        ]

    @pl.when(lax.axis_index("gx") == 0)
    def _():
        inlet[...] = jnp.zeros_like(inlet)
        for c in range(4):
            for z in range(nz):
                inlet[z, 2 * c : 2 * c + 1, :] = in_ref[c, z : z + 1, :]
        for half in range(2):
            old = corner_ref[half]
            push = upwind(old[1:2])[0]
            for c in range(4):
                msg = in_ref[c, nz + half : nz + half + 1, :]
                side = jnp.where(
                    lane[0:1] % 4 == 1, pltpu.roll(msg, 1, 1), pltpu.roll(msg, 127, 1)
                )
                wide[half, 2 * c : 2 * c + 1, :] = old[2 * c : 2 * c + 1] + push * side
                wide[half, 2 * c + 1 : 2 * c + 2, :] = jnp.zeros((1, 128), F32)

        def first(group, carry):
            for i in range(WIDE):
                z = group * WIDE + i
                push = upwind(sb_ref[z, 0:1, :])[0]
                new[z] = first_ref[z] + jnp.where(is_even, push * inlet[z], 0.0)
            return carry

        lax.fori_loop(0, nz // WIDE, first, 0)

        def second(group, carry):
            for i in range(WIDE):
                z = group * WIDE + i
                below = jnp.maximum(z - 1, 0)
                above = jnp.minimum(z + 1, nz - 1)
                half = z // 32
                shift = (255 - 4 * (z - 32 * half)) % 128
                cur = new[z]
                east = pltpu.roll(cur, 7, 0)
                corner = pltpu.roll(wide[half], shift, 1)
                south = jnp.where(lane == 0, corner, pltpu.roll(cur, 1, 1))
                north = jnp.where(lane == 127, corner, pltpu.roll(cur, 127, 1))
                c = coefs(cur[0:1], cur[2:3], cur[4:5])
                zero = mix(c, cur, inlet[z], east, south, north, new[below], new[above])
                zero = zero + jnp.where(sub == 4, (DT * BUOY) * cur[6:7], 0.0)
                delta = pltpu.roll(cur - first_ref[z], 1, 0)
                one = last_ref[z] + upwind(cur[1:2])[0] * delta
                done[z] = jnp.where(is_even, zero, one)
            for copy in send(group):
                copy.start()
            return carry

        lax.fori_loop(0, nz // WIDE, second, 0)
        for group in range(nz // WIDE):
            for copy in send(group):
                copy.wait()


VMEM = pl.BlockSpec(memory_space=pltpu.VMEM)
ANY = pl.BlockSpec(memory_space=pl.ANY)
SMEM = pl.BlockSpec(memory_space=pltpu.SMEM)
HBM = pl.BlockSpec(memory_space=pltpu.HBM)


def call(kernel, out, scratch=(), aliases=None, ins=None, outs=None, flops=1 << 20):
    specs = {}
    if ins is not None:
        specs["in_specs"] = ins
    if outs is not None:
        specs["out_specs"] = outs
    return pl.pallas_call(
        kernel,
        out_shape=out,
        scratch_shapes=scratch,
        input_output_aliases=aliases or {},
        compiler_params=pltpu.CompilerParams(vmem_limit_bytes=24 << 20),
        cost_estimate=pl.CostEstimate(flops=flops, bytes_accessed=1 << 20, transcendentals=0),
        **specs,
    )


def row_of(place):
    for one, two in TRADES:
        if place in (one, two):
            return one + two - place
    return place


def send_inlet(msg, after, count_x, count_y):
    heard = {}
    for m in (2, 3, 1, 0):
        moves = [
            (row_of(GROUP * m + j % GROUP) * count_y + j, j)
            for j in range(count_y)
            if GROUP * m + j % GROUP
        ]
        if m == 0:
            sent, *_ = lax.optimization_barrier((msg, *after))
        else:
            sent = msg
        heard[m] = lax.ppermute(sent, ("gx", "gy"), moves)
    return [heard[m] for m in range(4)]


def share_inlet(own, msg, heard, code, count_y):
    heard[0] = jnp.where(lax.axis_index("gy") % GROUP == 0, msg, heard[0])

    def pick(k):
        out = heard[0]
        for m in range(1, len(heard)):
            out = jnp.where(code[k] & 7 == m, heard[m], out)
        return out

    parts = [x.reshape(-1, 128) for x in (own, pick(1), pick(3))]
    got = lax.ppermute(jnp.concatenate(parts), "gy", pairs(count_y, False))
    side = got[: parts[0].shape[0]].reshape(own.shape)
    core = got[parts[0].shape[0] :].reshape(8, *msg.shape[1:])
    mine = jnp.where(code[0] & 8 != 0, pick(0), core[0:4])
    theirs = jnp.where(code[2] & 8 != 0, pick(2), core[4:8])
    other = lax.ppermute(theirs, "gy", [(j, j ^ 2) for j in range(count_y)])
    return side, jnp.where(code[0] & 16 != 0, mine, other)


def body(flow_state, inflow, footprint, block_map):
    levels = flow_state.shape[1]
    count_x = lax.axis_size("gx")
    count_y = lax.axis_size("gy")
    turbines = footprint.shape[0]
    shape = lambda *s: jax.ShapeDtypeStruct(s, F32)
    x_pack = shape(levels, 8, 128)
    y_pack = shape(2, 4, 24, 128)

    send_a, send_b = call(
        pack_x_kernel, (x_pack, x_pack), [pltpu.SemaphoreType.DMA((4, 2))], ins=[HBM], outs=[VMEM] * 2
    )(flow_state)
    recv_a = lax.ppermute(send_a, "gx", pairs(count_x, False))
    recv_b = lax.ppermute(send_b, ("gx", "gy"), pairs_inside(count_x, count_y))

    late, _ = lax.optimization_barrier((footprint, send_a))
    fp = jnp.pad(late.T, ((0, 5), (0, 128 - turbines)), constant_values=FAR)
    lap = jnp.ones((128, 128), F32)
    for i, extent in enumerate((DISK_X, DISK_Y, DISK_Z)):
        lap = lap * jnp.maximum(extent - jnp.abs(fp[i][:, None] - fp[i][None, :]), 0).astype(F32)
    live = jnp.arange(128) < turbines
    lap = jnp.where(live[:, None] & live[None, :], lap, 0.0)

    own = call(pack_y_kernel, y_pack, flops=PACK_COST)(flow_state, send_a)
    msg, code = call(
        pack_inlet_kernel,
        (shape(4, levels + 8, 128), jax.ShapeDtypeStruct((GROUP, levels + 8, 128), jnp.int32)),
        ins=[SMEM, VMEM, VMEM],
    )(block_map, inflow, own)
    base, disks, masks, sums = call(
        base_kernel,
        (
            shape(*flow_state.shape),
            jax.ShapeDtypeStruct((levels, 16, 128), jnp.bfloat16),
            jax.ShapeDtypeStruct((3, 256, 128), jnp.bfloat16),
            shape(8, 128),
        ),
        [pltpu.VMEM((2, levels, 16, 128), F32)],
        flops=TILE_COST,
    )(flow_state, fp)
    heard = send_inlet(msg, (recv_b, sums), count_x, count_y)

    own, near, west, east = call(
        rim_kernel, (y_pack, x_pack, x_pack, x_pack), [pltpu.VMEM((levels, 8, 128), F32)] * 3
    )(send_a, send_b, recv_a, recv_b, fp, sums, own)
    side_b = lax.ppermute(own, "gy", pairs(count_y, True))
    *heard, _ = lax.optimization_barrier((*heard, side_b))
    side_a, inlet = share_inlet(own, msg, list(heard), code, count_y)
    out, first, corner, last = call(
        steps_kernel,
        (shape(*flow_state.shape), x_pack, shape(2, 8, 128), x_pack),
        [
            pltpu.VMEM(flow_state.shape, F32),
            pltpu.VMEM(flow_state.shape, F32),
            pltpu.VMEM((2, levels, 16, 128), F32),
            pltpu.VMEM((2, levels, 128), F32),
            pltpu.VMEM((levels, 8, 128), F32),
            pltpu.VMEM((2, 2, 4, 16, 128), F32),
            pltpu.VMEM((2, 8, 128), F32),
            pltpu.SemaphoreType.DMA((levels // CHUNK,)),
        ],
        outs=[ANY, VMEM, VMEM, VMEM],
        flops=STEPS_COST,
    )(flow_state, base, disks, masks, near, west, east, own, side_a, side_b, fp, lap)
    return call(
        fix_kernel,
        shape(*flow_state.shape),
        [
            pltpu.VMEM((levels, 8, 128), F32),
            pltpu.VMEM((levels, 8, 128), F32),
            pltpu.VMEM((2, 8, 128), F32),
            pltpu.VMEM((levels, 8, 128), F32),
            pltpu.SemaphoreType.DMA((levels // WIDE, 4)),
        ],
        aliases={0: 0},
        ins=[ANY, VMEM, VMEM, VMEM, VMEM, VMEM],
        outs=ANY,
    )(out, inlet, send_b, first, corner, last)


def solution(mesh):
    placed = (P(None, None, "gx", "gy"), P(None, None, "gx"), P(), P())
    return jax.shard_map(
        body, mesh=mesh, in_specs=placed, out_specs=P(None, None, "gx", "gy"), check_vma=False
    )
```
